32 devices in a mesh: snap: 2 (over x), inner: 16 (over z, y, core).
Axes of the slice: x: 2, y: 2, z: 4, core: 2. Of those that a mesh axis runs over, the one named last changes fastest.
Arguments:
- vertices: float32 [16384, 256], P(('snap', 'inner')), parts along dimension 0, may hold values from -0.75 to 0.75
- vertex_moments: float32 [16384, 256], P(('snap', 'inner')), parts along dimension 0, may hold values from 0.1 to 2
- contexts: float32 [32768, 256], P(('snap', 'inner')), parts along dimension 0, may hold values from -0.75 to 0.75
- context_moments: float32 [32768, 256], P(('snap', 'inner')), parts along dimension 0, may hold values from 0.1 to 2
- edge_counts: int32 [3, 512, 32768], P(None, None, ('snap', 'inner')), parts along dimension 2, may hold values from 0 to 4
- negative_weights: int32 [3, 32768], P(None, ('snap', 'inner')), parts along dimension 1, may hold values from 1 to 6
Outputs:
- vertex_out: float32 [16384, 256], P(('snap', 'inner')), parts along dimension 0
- vertex_moments_out: float32 [16384, 256], P(('snap', 'inner')), parts along dimension 0
- context_out: float32 [32768, 256], P(('snap', 'inner')), parts along dimension 0
- context_moments_out: float32 [32768, 256], P(('snap', 'inner')), parts along dimension 0
The draws below stay inside these ranges and needn't reach their ends.
There are 2 independent parts, one for each index of `snap`. The reference program is written for one: setup_inputs(seed, part) draws one part's arguments, and reference() takes and returns one part's arrays. A program takes and returns all parts, laid end to end along the dimension named above; each array names one. Nothing has to cross between parts.
All inputs are finite; a program needn't handle non-finite values.
Results may differ from the reference program's by a relative error of at most 0.0001.
Values sent between devices are 32-bit elements; how exact they have to be, the bound alone decides.
No kernel may reach another device: no remote copies, remote signals or barrier semaphores. Data moves between devices by JAX's collectives and lax.ppermute only.
A program may use at most 64 MiB of HBM per device.

```python
import math
import jax
import jax.numpy as jnp
from jax import lax

D = 256
VB = 512
CB = 1024
STEPS = 3
VERTS = 8192
CONTEXTS = 16384
N_INNER = 16


def touch_ends(result, key, least, largest):
    dims = result.shape
    place = [jax.random.randint(jax.random.fold_in(key, axis), (), 0, dims[axis]) for axis in range(len(dims))]
    result = result.at[tuple(place)].set(least)
    longest = dims.index(max(dims))
    place[longest] = (place[longest] + 1) % dims[longest]
    return result.at[tuple(place)].set(largest)


def levels(rng, dims, cuts, smallest, top_value):
    factor_of = 1.0
    for axis_at, parts in cuts:
        steps = jax.random.uniform(jax.random.fold_in(jax.random.fold_in(rng, 6), axis_at), (parts,), jnp.float32, smallest / len(cuts), top_value / len(cuts))
        factor_of = factor_of * jnp.repeat(jnp.exp(steps), dims[axis_at] // parts).reshape((-1,) + (1,) * (len(dims) - 1 - axis_at))
    return factor_of


def gaussian(own_key, shape, deviation, limit, shards=(), dtype=jnp.bfloat16):
    factor_of = levels(own_key, shape, shards, -0.22, 0.18) if shards else 1.0
    result = jax.random.normal(own_key, shape, jnp.float32) * deviation * factor_of
    return jnp.minimum(jnp.maximum(result, -limit), limit).astype(dtype)


def setup_inputs(seed: int = 0, part: int = 0) -> dict:
    key_of = jax.random.split(jax.random.key(seed), 7)
    part_keys = jax.random.split(jax.random.fold_in(key_of[6], part), 7)
    vertices = gaussian(part_keys[0], (VERTS, D), 0.125, 0.75, ((0, 16),), jnp.float32)
    vertex_moments = jnp.clip(jnp.exp(math.log(2.0) - 2.9957323 * jax.random.uniform(part_keys[1], (VERTS, D), jnp.float32) ** levels(part_keys[1], (VERTS, D), ((0, 16),), -0.2, 0.2)), 0.1, 2.0)
    contexts = gaussian(part_keys[2], (CONTEXTS, D), 0.125, 0.75, ((0, 16),), jnp.float32)
    context_moments = jnp.clip(jnp.exp(math.log(2.0) - 2.9957323 * jax.random.uniform(part_keys[3], (CONTEXTS, D), jnp.float32) ** levels(part_keys[3], (CONTEXTS, D), ((0, 16),), -0.2, 0.2)), 0.1, 2.0)
    edge_counts = touch_ends(jax.random.randint(part_keys[4], (STEPS, VB, CONTEXTS), 0, 5), jax.random.fold_in(part_keys[4], 1), 0, 4).astype(jnp.int32)
    negative_weights = touch_ends(jax.random.randint(part_keys[5], (STEPS, CONTEXTS), 1, 7), jax.random.fold_in(part_keys[5], 1), 1, 6).astype(jnp.int32)
    return {"vertices": vertices, "vertex_moments": vertex_moments, "contexts": contexts, "context_moments": context_moments, "edge_counts": edge_counts, "negative_weights": negative_weights}


def one_step(ublk, gblk, cblk, hblk, counts, negs):
    scores = jnp.einsum('bvd,bcd->bvc', ublk, cblk, precision=lax.Precision.HIGHEST)
    ecount = counts.astype(jnp.float32)
    resid = (ecount + negs.astype(jnp.float32)[:, None, :]) * jax.nn.sigmoid(scores) - ecount
    grad_u = jnp.einsum('bvc,bcd->bvd', resid, cblk, precision=lax.Precision.HIGHEST)
    grad_c = jnp.einsum('bvc,bvd->bcd', resid, ublk, precision=lax.Precision.HIGHEST)
    gblk = gblk + grad_u * grad_u
    ublk = ublk - 0.05 * grad_u / jnp.sqrt(gblk)
    hblk = hblk + grad_c * grad_c
    cblk = cblk - 0.05 * grad_c / jnp.sqrt(hblk)
    return (ublk, gblk, cblk, hblk)

def reference(vertices, vertex_moments, contexts, context_moments, edge_counts, negative_weights):
    blocks = N_INNER
    ublk = vertices.reshape(blocks, VB, D)
    gblk = vertex_moments.reshape(blocks, VB, D)
    cblk = contexts.reshape(blocks, CB, D)
    hblk = context_moments.reshape(blocks, CB, D)
    for step in range(STEPS):
        counts = jnp.transpose(edge_counts[step].reshape(VB, blocks, CB), (1, 0, 2))
        negs = negative_weights[step].reshape(blocks, CB)
        moved_u = jnp.roll(ublk, step, axis=0)
        moved_g = jnp.roll(gblk, step, axis=0)
        moved_u, moved_g, cblk, hblk = one_step(moved_u, moved_g, cblk, hblk, counts, negs)
        ublk = jnp.roll(moved_u, -step, axis=0)
        gblk = jnp.roll(moved_g, -step, axis=0)
    return (ublk.reshape(VERTS, D), gblk.reshape(VERTS, D), cblk.reshape(CONTEXTS, D), hblk.reshape(CONTEXTS, D))
```

```python
import jax
import jax.numpy as jnp
from jax import lax
from jax.experimental import pallas as pl
from jax.experimental.pallas import tpu as pltpu
from jax.sharding import PartitionSpec as P

F32 = jnp.float32
BF16 = jnp.bfloat16
RATE = 0.05
VMEM = pl.BlockSpec(memory_space=pltpu.VMEM)
HBM = pl.BlockSpec(memory_space=pltpu.HBM)
ANY = pl.BlockSpec(memory_space=pl.ANY)


def split(x):
    high = x.astype(BF16)
    return high, (x - high.astype(F32)).astype(BF16)


def product(a, b, dim_a, dim_b):
    def one(x, y):
        return lax.dot_general(
            x, y, (((dim_a,), (dim_b,)), ((), ())), preferred_element_type=F32
        )

    return one(a[0], b[0]) + (one(a[1], b[0]) + one(a[0], b[1]))


def block_of(size, most):
    return most if size % most == 0 else size


def is_odd():
    return lax.rem(lax.axis_index("inner"), 2) == 1


def adagrad(value, moment, grad):
    moment = moment + grad * grad
    return value - RATE * grad * lax.rsqrt(moment), moment


def vertex_pass(u, c, e, w, r_high, r_low, emit):
    cs = split(c[...])
    wf = w.astype(F32)
    rows = block_of(u.shape[0], 256)
    for i in range(u.shape[0] // rows):
        at = pl.ds(i * rows, rows)
        half_scores = product(split(0.5 * u[at, :]), cs, 1, 1)
        ef = e(i, rows).astype(F32)
        resid = split((ef + wf) * jnp.tanh(half_scores) + (wf - ef))
        r_high[at, :] = resid[0]
        r_low[at, :] = resid[1]
        emit(at, 0.5 * product(resid, cs, 1, 0))


def context_pass(u, c, h, r_high, r_low, c_out, h_out):
    us = split(0.5 * u[...])
    rows = block_of(c.shape[0], 256)
    for j in range(c.shape[0] // rows):
        at = pl.ds(j * rows, rows)
        grad = product((r_high[:, at], r_low[:, at]), us, 0, 0)
        c_out[at, :], h_out[at, :] = adagrad(c[at, :], h[at, :], grad)


def call(body, in_specs, outs, scratch, args, name):
    return pl.pallas_call(
        body,
        out_shape=outs,
        in_specs=in_specs,
        out_specs=[VMEM] * len(outs),
        scratch_shapes=scratch,
        compiler_params=pltpu.CompilerParams(vmem_limit_bytes=24 << 20),
        name=name,
    )(*args)


def load(pairs, sems):
    copies = [pltpu.make_async_copy(a, b, sems.at[i]) for i, (a, b) in enumerate(pairs)]
    for copy in copies:
        copy.start()
    return copies


def first_odd(u, g, c, e, w, s1, r_high, r_low, ub, gb, cb, eb, sems):
    nrows = ub.shape[0]
    rows = block_of(nrows, 256)
    count = nrows // rows

    @pl.when(is_odd())
    def _():
        copies = load(
            [(u, ub), (c, cb)]
            + [(e.at[0, pl.ds(i * rows, rows)], eb.at[pl.ds(i * rows, rows)]) for i in range(count)]
            + [(g, gb)],
            sems,
        )
        copies[0].wait()
        copies[1].wait()

        def edges(i, rows):
            copies[2 + i].wait()
            if i == count - 1:
                copies[-1].wait()
            return eb[pl.ds(i * rows, rows), :]

        grads = []
        vertex_pass(ub, cb, edges, w[0:1, :], r_high, r_low, lambda at, grad: grads.append((at, grad)))
        for at, grad in grads:
            s1[0, at, :], s1[1, at, :] = adagrad(ub[at, :], gb[at, :], grad)


def first_rest(u, g, c, h, e, w, r_high_in, r_low_in, s1, c_out, h_out, ub, gb, cb, hb, eb, r_high, r_low, sems):
    odd = is_odd()
    load_context = [(u, ub), (c, cb), (h, hb)]

    @pl.when(odd)
    def _():
        for copy in load(load_context, sems):
            copy.wait()
        context_pass(ub, cb, hb, r_high_in, r_low_in, c_out, h_out)

    @pl.when(jnp.logical_not(odd))
    def _():
        for copy in load(load_context + [(g, gb), (e.at[0], eb)], sems):
            copy.wait()

        def emit(at, grad):
            s1[0, at, :], s1[1, at, :] = adagrad(ub[at, :], gb[at, :], grad)

        vertex_pass(ub, cb, lambda i, rows: eb[pl.ds(i * rows, rows), :], w[0:1, :], r_high, r_low, emit)
        context_pass(ub, cb, hb, r_high, r_low, c_out, h_out)


def second_odd(s1, c, h, e, w, u2, s2, c_out, h_out, r_high, r_low):
    @pl.when(is_odd())
    def _():
        def emit(at, grad):
            value, moment = adagrad(s1[0, at, :], s1[1, at, :], grad)
            u2[at, :] = value
            s2[0, at, :] = value
            s2[1, at, :] = moment

        vertex_pass(s1.at[0], c, lambda i, rows: e[pl.ds(i * rows, rows), :], w[1:2, :], r_high, r_low, emit)
        context_pass(s1.at[0], c, h, r_high, r_low, c_out, h_out)


def second_even(s1, c, h, e, w, after, g1, u2, c_out, h_out, r_high, r_low):
    @pl.when(jnp.logical_not(is_odd()))
    def _():
        def emit(at, grad):
            g1[at, :] = grad
            u2[at, :] = adagrad(s1[0, at, :], s1[1, at, :], grad)[0]

        vertex_pass(s1.at[0], c, lambda i, rows: e[pl.ds(i * rows, rows), :], w[1:2, :], r_high, r_low, emit)
        context_pass(s1.at[0], c, h, r_high, r_low, c_out, h_out)


def third(odd, u, c, e, w, after, g2, r_high, r_low):
    @pl.when(is_odd() == odd)
    def _():
        def emit(at, grad):
            g2[at, :] = grad

        vertex_pass(u, c, lambda i, rows: e[pl.ds(i * rows, rows), :], w[2:3, :], r_high, r_low, emit)


def third_odd(*refs):
    third(True, *refs)


def third_even(*refs):
    third(False, *refs)


def third_context(u_odd, c_odd, h_odd, rh_odd, rl_odd, u_even, c_even, h_even, rh_even, rl_even, c_out, h_out):
    odd = is_odd()

    @pl.when(odd)
    def _():
        context_pass(u_odd, c_odd, h_odd, rh_odd, rl_odd, c_out, h_out)

    @pl.when(jnp.logical_not(odd))
    def _():
        context_pass(u_even, c_even, h_even, rh_even, rl_even, c_out, h_out)


def last(s1, g1, g2_odd, s2, g2_even, u_out, g_out):
    odd = is_odd()

    @pl.when(odd)
    def _():
        value, moment = adagrad(s1[0], s1[1], g1[...])
        u_out[...], g_out[...] = adagrad(value, moment, g2_odd[...])

    @pl.when(jnp.logical_not(odd))
    def _():
        u_out[...], g_out[...] = adagrad(s2[0], s2[1], g2_even[...])


def per_device(vertices, vertex_moments, contexts, context_moments, edge_counts, negative_weights):
    nrows, width = vertices.shape
    ncols = contexts.shape[0]
    count = lax.axis_size("inner")
    assert count % 2 == 0 and edge_counts.shape[0] == 3

    ring = [(i, (i + 1) % count) for i in range(count)]
    unring = [(b, a) for a, b in ring]
    swap = [(i, i ^ 1) for i in range(count)]
    home_odd = [(i, (i - 2) % count if i % 2 else i) for i in range(count)]
    home_even = [(i, i if i % 2 else (i - 2) % count) for i in range(count)]

    def move(value, pairs):
        return lax.ppermute(value, "inner", pairs)

    def f32(*shape):
        return jax.ShapeDtypeStruct(shape, F32)

    block = f32(nrows, width)
    pair = f32(2, nrows, width)
    ctx = f32(ncols, width)
    half = jax.ShapeDtypeStruct((nrows, ncols), BF16)
    half_buf = pltpu.VMEM((nrows, ncols), BF16)
    vert_buf = pltpu.VMEM((nrows, width), F32)
    ctx_buf = pltpu.VMEM((ncols, width), F32)
    edge_buf = pltpu.VMEM((nrows, ncols), jnp.int32)
    sems = pltpu.SemaphoreType.DMA((3 + max(2, nrows // block_of(nrows, 256)),))

    s1o, rh0, rl0 = call(
        first_odd, [HBM] * 4 + [VMEM], [pair, half, half],
        [vert_buf, vert_buf, ctx_buf, edge_buf, sems],
        (vertices, vertex_moments, contexts, edge_counts, negative_weights), "first_odd",
    )
    s1x = move(s1o, ring)
    s1, c1, h1 = call(
        first_rest, [HBM] * 5 + [VMEM] * 3, [pair, ctx, ctx],
        [vert_buf, vert_buf, ctx_buf, ctx_buf, edge_buf, half_buf, half_buf, sems],
        (vertices, vertex_moments, contexts, context_moments, edge_counts, negative_weights, rh0, rl0), "first_rest",
    )
    s1i = move(s1, swap)
    u2e, s2e, c2o, h2o = call(
        second_odd, [VMEM] * 5, [block, pair, ctx, ctx], [half_buf, half_buf],
        (s1i, c1, h1, edge_counts[1], negative_weights), "second_odd",
    )
    u2x = move(u2e, ring)
    s2h = move(s2e, swap)
    g1, u2b, c2e, h2e = call(
        second_even, [VMEM] * 5 + [ANY], [block, block, ctx, ctx], [half_buf, half_buf],
        (s1x, c1, h1, edge_counts[1], negative_weights, u2e), "second_even",
    )
    g1x = move(g1, unring)
    u2i = move(u2b, swap)
    g2o, rho, rlo = call(
        third_odd, [VMEM] * 4 + [ANY], [block, half, half], [],
        (u2i, c2o, edge_counts[2], negative_weights, u2b), "third_odd",
    )
    g2xo = move(g2o, home_odd)
    g2e, rhe, rle = call(
        third_even, [VMEM] * 4 + [ANY], [block, half, half], [],
        (u2x, c2e, edge_counts[2], negative_weights, g2o), "third_even",
    )
    g2xe = move(g2e, home_even)
    c3, h3 = call(
        third_context, [VMEM] * 10, [ctx, ctx], [],
        (u2i, c2o, h2o, rho, rlo, u2x, c2e, h2e, rhe, rle), "third_context",
    )
    u3, g3 = call(last, [VMEM] * 5, [block, block], [], (s1o, g1x, g2xo, s2h, g2xe), "last")
    return u3, g3, c3, h3


def solution(mesh):
    split_rows = P(("snap", "inner"), None)
    return jax.shard_map(
        per_device,
        mesh=mesh,
        in_specs=(
            split_rows,
            split_rows,
            split_rows,
            split_rows,
            P(None, None, ("snap", "inner")),
            P(None, ("snap", "inner")),
        ),
        out_specs=(split_rows,) * 4,
        check_vma=False,
    )
```

```python
import jax
import jax.numpy as jnp
from jax import lax
from jax.experimental import pallas as pl
from jax.experimental.pallas import tpu as pltpu
from jax.sharding import PartitionSpec as P

F32 = jnp.float32
BF16 = jnp.bfloat16
RATE = 0.05
VMEM = pl.BlockSpec(memory_space=pltpu.VMEM)
HBM = pl.BlockSpec(memory_space=pltpu.HBM)
ANY = pl.BlockSpec(memory_space=pl.ANY)


def split(x):
    high = x.astype(BF16)
    return high, (x - high.astype(F32)).astype(BF16)


def product(a, b, dim_a, dim_b):
    def one(x, y):
        return lax.dot_general(
            x, y, (((dim_a,), (dim_b,)), ((), ())), preferred_element_type=F32
        )

    return one(a[0], b[0]) + (one(a[1], b[0]) + one(a[0], b[1]))


def block_of(size, most):
    return most if size % most == 0 else size


def is_odd():
    return lax.rem(lax.axis_index("inner"), 2) == 1


def adagrad(value, moment, grad):
    moment = moment + grad * grad
    return value - RATE * grad * lax.rsqrt(moment), moment


def vertex_pass(u, c, e, w, r_high, r_low, emit):
    cs = split(c[...])
    wf = w.astype(F32)
    rows = block_of(u.shape[0], 256)
    for i in range(u.shape[0] // rows):
        at = pl.ds(i * rows, rows)
        half_scores = product(split(0.5 * u[at, :]), cs, 1, 1)
        ef = e(i, rows).astype(F32)
        resid = split((ef + wf) * jnp.tanh(half_scores) + (wf - ef))
        r_high[at, :] = resid[0]
        r_low[at, :] = resid[1]
        emit(at, 0.5 * product(resid, cs, 1, 0))


def context_pass(u, c, h, r_high, r_low, c_out, h_out):
    us = split(0.5 * u[...])
    rows = block_of(c.shape[0], 256)
    for j in range(c.shape[0] // rows):
        at = pl.ds(j * rows, rows)
        grad = product((r_high[:, at], r_low[:, at]), us, 0, 0)
        c_out[at, :], h_out[at, :] = adagrad(c[at, :], h[at, :], grad)


def call(body, in_specs, outs, scratch, args, name, room=24):
    return pl.pallas_call(
        body,
        out_shape=outs,
        in_specs=in_specs,
        out_specs=[VMEM] * len(outs),
        scratch_shapes=scratch,
        compiler_params=pltpu.CompilerParams(vmem_limit_bytes=room << 20),
        cost_estimate=pl.CostEstimate(flops=1024, bytes_accessed=1024, transcendentals=0),
        name=name,
    )(*args)


def load(pairs, sems):
    copies = [pltpu.make_async_copy(a, b, sems.at[i]) for i, (a, b) in enumerate(pairs)]
    for copy in copies:
        copy.start()
    return copies


def first_odd(u, g, c, e, w, s1, r_high, r_low, ub, gb, cb, eb, sems):
    nrows = ub.shape[0]
    rows = block_of(nrows, 256)
    count = nrows // rows

    @pl.when(is_odd())
    def _():
        copies = load(
            [(u, ub), (c, cb)]
            + [(e.at[0, pl.ds(i * rows, rows)], eb.at[pl.ds(i * rows, rows)]) for i in range(count)]
            + [(g, gb)],
            sems,
        )
        copies[0].wait()
        copies[1].wait()

        def edges(i, rows):
            copies[2 + i].wait()
            if i == count - 1:
                copies[-1].wait()
            return eb[pl.ds(i * rows, rows), :]

        grads = []
        vertex_pass(ub, cb, edges, w[0:1, :], r_high, r_low, lambda at, grad: grads.append((at, grad)))
        for at, grad in grads:
            s1[0, at, :], s1[1, at, :] = adagrad(ub[at, :], gb[at, :], grad)


def first_rest(u, g, c, h, e, w, r_high_in, r_low_in, su, sg, c_out, h_out, ub, gb, cb, hb, eb, r_high, r_low, sems):
    odd = is_odd()
    load_context = [(u, ub), (c, cb), (h, hb)]

    @pl.when(odd)
    def _():
        for copy in load(load_context, sems):
            copy.wait()
        context_pass(ub, cb, hb, r_high_in, r_low_in, c_out, h_out)

    @pl.when(jnp.logical_not(odd))
    def _():
        for copy in load(load_context + [(g, gb), (e.at[0], eb)], sems):
            copy.wait()

        def emit(at, grad):
            su[at, :], sg[at, :] = adagrad(ub[at, :], gb[at, :], grad)

        vertex_pass(ub, cb, lambda i, rows: eb[pl.ds(i * rows, rows), :], w[0:1, :], r_high, r_low, emit)
        context_pass(ub, cb, hb, r_high, r_low, c_out, h_out)


def second_odd(su, sg, c, h, e, w, u2, s2, c_out, h_out, r_high, r_low):
    @pl.when(is_odd())
    def _():
        def emit(at, grad):
            value, moment = adagrad(su[at, :], sg[at, :], grad)
            u2[at, :] = value
            s2[0, at, :] = value
            s2[1, at, :] = moment

        vertex_pass(su, c, lambda i, rows: e[pl.ds(i * rows, rows), :], w[1:2, :], r_high, r_low, emit)
        context_pass(su, c, h, r_high, r_low, c_out, h_out)


def second_even(s1, c, h, e, w, after, g1, u2_top, u2_end, c_out, h_out, r_high, r_low):
    @pl.when(jnp.logical_not(is_odd()))
    def _():
        def emit(at, grad):
            g1[at, :] = grad

        vertex_pass(s1.at[0], c, lambda i, rows: e[pl.ds(i * rows, rows), :], w[1:2, :], r_high, r_low, emit)
        middle = u2_top.shape[0]
        for u2, at in ((u2_top, pl.ds(0, middle)), (u2_end, pl.ds(middle, middle))):
            u2[...] = adagrad(s1[0, at, :], s1[1, at, :], g1[at, :])[0]
        context_pass(s1.at[0], c, h, r_high, r_low, c_out, h_out)


def third(odd, u, c, e, w, after, g2, r_high, r_low):
    @pl.when(is_odd() == odd)
    def _():
        def emit(at, grad):
            g2[at, :] = grad

        vertex_pass(u, c, lambda i, rows: e[pl.ds(i * rows, rows), :], w[2:3, :], r_high, r_low, emit)


def third_odd(u_top, u_end, c, e, w, after, u, *refs):
    middle = u_top.shape[0]
    u[:middle, :] = u_top[...]
    u[middle:, :] = u_end[...]
    third(True, u, c, e, w, after, *refs)


def third_even(*refs):
    third(False, *refs)


def third_context(u_odd, c_odd, h_odd, rh_odd, rl_odd, u_even, c_even, h_even, rh_even, rl_even, c_out, h_out):
    odd = is_odd()

    @pl.when(odd)
    def _():
        context_pass(u_odd, c_odd, h_odd, rh_odd, rl_odd, c_out, h_out)

    @pl.when(jnp.logical_not(odd))
    def _():
        context_pass(u_even, c_even, h_even, rh_even, rl_even, c_out, h_out)


def last(s1, g1, g2_odd, s2, g2_even, u_out, g_out):
    odd = is_odd()

    @pl.when(odd)
    def _():
        value, moment = adagrad(s1[0], s1[1], g1[...])
        u_out[...], g_out[...] = adagrad(value, moment, g2_odd[...])

    @pl.when(jnp.logical_not(odd))
    def _():
        u_out[...], g_out[...] = adagrad(s2[0], s2[1], g2_even[...])


def per_device(vertices, vertex_moments, contexts, context_moments, edge_counts, negative_weights):
    nrows, width = vertices.shape
    ncols = contexts.shape[0]
    count = lax.axis_size("inner")
    assert count % 2 == 0 and edge_counts.shape[0] == 3

    ring = [(i, (i + 1) % count) for i in range(count)]
    unring = [(b, a) for a, b in ring]
    swap = [(i, i ^ 1) for i in range(count)]
    home_odd = [(i, (i - 2) % count if i % 2 else i) for i in range(count)]
    home_even = [(i, i if i % 2 else (i - 2) % count) for i in range(count)]

    def move(value, pairs):
        return lax.ppermute(value, "inner", pairs)

    def f32(*shape):
        return jax.ShapeDtypeStruct(shape, F32)

    block = f32(nrows, width)
    pair = f32(2, nrows, width)
    ctx = f32(ncols, width)
    half = jax.ShapeDtypeStruct((nrows, ncols), BF16)
    half_buf = pltpu.VMEM((nrows, ncols), BF16)
    vert_buf = pltpu.VMEM((nrows, width), F32)
    ctx_buf = pltpu.VMEM((ncols, width), F32)
    edge_buf = pltpu.VMEM((nrows, ncols), jnp.int32)
    sems = pltpu.SemaphoreType.DMA((3 + max(2, nrows // block_of(nrows, 256)),))

    hbm = [
        pltpu.with_memory_space_constraint(x, pltpu.HBM)
        for x in (vertices, vertex_moments, contexts, context_moments, edge_counts)
    ]
    s1o, rh0, rl0 = call(
        first_odd, [HBM] * 4 + [VMEM], [pair, half, half],
        [vert_buf, vert_buf, ctx_buf, edge_buf, sems],
        (*hbm[:3], hbm[4], negative_weights), "first_odd",
    )
    s1x = move(s1o, ring)
    su, sg, c1, h1 = call(
        first_rest, [HBM] * 5 + [VMEM] * 3, [block, block, ctx, ctx],
        [vert_buf, vert_buf, ctx_buf, ctx_buf, edge_buf, half_buf, half_buf, sems],
        (*hbm, negative_weights, rh0, rl0), "first_rest",
    )
    sui = move(su, swap)
    sgi = move(sg, swap)
    u2e, s2e, c2o, h2o = call(
        second_odd, [VMEM] * 6, [block, pair, ctx, ctx], [half_buf, half_buf],
        (sui, sgi, c1, h1, edge_counts[1], negative_weights), "second_odd",
    )
    u2x = move(u2e, ring)
    s2h = move(s2e, swap)
    g1, u2t, u2d, c2e, h2e = call(
        second_even, [VMEM] * 5 + [ANY], [block, f32(nrows // 2, width), f32(nrows // 2, width), ctx, ctx], [half_buf, half_buf],
        (s1x, c1, h1, edge_counts[1], negative_weights, u2e), "second_even",
    )
    g1x = move(g1, unring)
    u2ti = move(u2t, swap)
    u2di = move(u2d, swap)
    u2i, g2o, rho, rlo = call(
        third_odd, [VMEM] * 5 + [ANY], [block, block, half, half], [],
        (u2ti, u2di, c2o, edge_counts[2], negative_weights, u2t), "third_odd",
    )
    g2xo = move(g2o, home_odd)
    g2e, rhe, rle = call(
        third_even, [VMEM] * 4 + [ANY], [block, half, half], [],
        (u2x, c2e, edge_counts[2], negative_weights, g2o), "third_even",
    )
    g2xe = move(g2e, home_even)
    c3, h3 = call(
        third_context, [VMEM] * 10, [ctx, ctx], [],
        (u2i, c2o, h2o, rho, rlo, u2x, c2e, h2e, rhe, rle), "third_context",
    )
    u3, g3 = call(last, [VMEM] * 5, [block, block], [], (s1o, g1x, g2xo, s2h, g2xe), "last")
    return u3, g3, c3, h3


def solution(mesh):
    split_rows = P(("snap", "inner"), None)
    return jax.shard_map(
        per_device,
        mesh=mesh,
        in_specs=(
            split_rows,
            split_rows,
            split_rows,
            split_rows,
            P(None, None, ("snap", "inner")),
            P(None, ("snap", "inner")),
        ),
        out_specs=(split_rows,) * 4,
        check_vma=False,
    )
```

```python
import jax
import jax.numpy as jnp
from jax import lax
from jax.experimental import pallas as pl
from jax.experimental.pallas import tpu as pltpu
from jax.sharding import PartitionSpec as P

F32 = jnp.float32
BF16 = jnp.bfloat16
RATE = 0.05
VMEM = pl.BlockSpec(memory_space=pltpu.VMEM)
HBM = pl.BlockSpec(memory_space=pltpu.HBM)
ANY = pl.BlockSpec(memory_space=pl.ANY)


def split(x):
    high = x.astype(BF16)
    return high, (x - high.astype(F32)).astype(BF16)


def product(a, b, dim_a, dim_b):
    def one(x, y):
        return lax.dot_general(
            x, y, (((dim_a,), (dim_b,)), ((), ())), preferred_element_type=F32
        )

    return one(a[0], b[0]) + (one(a[1], b[0]) + one(a[0], b[1]))


def block_of(size, most):
    return most if size % most == 0 else size


def is_odd():
    return lax.rem(lax.axis_index("inner"), 2) == 1


def adagrad(value, moment, grad):
    moment = moment + grad * grad
    return value - RATE * grad * lax.rsqrt(moment), moment


def vertex_pass(u, c, e, w, r_high, r_low, ready=None):
    us = split(0.5 * u[...])
    wf = w.astype(F32)
    cols = block_of(c.shape[0], 256)
    count = c.shape[0] // cols
    parts = []

    def scores(j):
        if ready is not None:
            ready(j)
        parts.append(split(c[pl.ds(j * cols, cols), :]))
        return product(us, parts[j], 1, 1)

    grad = None
    half_scores = scores(0)
    for j in range(count):
        at = pl.ds(j * cols, cols)
        later = scores(j + 1) if j + 1 < count else None
        ef = e[:, at].astype(F32)
        wj = wf[:, j * cols : (j + 1) * cols]
        resid = split((ef + wj) * jnp.tanh(half_scores) + (wj - ef))
        r_high[:, at] = resid[0]
        r_low[:, at] = resid[1]
        term = product(resid, parts[j], 1, 0)
        grad = term if grad is None else grad + term
        half_scores = later
    return 0.5 * grad


def context_pass(u, c, h, r_high, r_low, c_out, h_out):
    us = split(0.5 * u[...])
    rows = block_of(c.shape[0], 256)
    for j in range(c.shape[0] // rows):
        at = pl.ds(j * rows, rows)
        grad = product((r_high[:, at], r_low[:, at]), us, 0, 0)
        c_out[at, :], h_out[at, :] = adagrad(c[at, :], h[at, :], grad)


def call(body, in_specs, outs, scratch, args, name, room=24):
    return pl.pallas_call(
        body,
        out_shape=outs,
        in_specs=in_specs,
        out_specs=[VMEM] * len(outs),
        scratch_shapes=scratch,
        compiler_params=pltpu.CompilerParams(vmem_limit_bytes=room << 20),
        cost_estimate=pl.CostEstimate(flops=1024, bytes_accessed=1024, transcendentals=0),
        name=name,
    )(*args)


def load(pairs, sems, first=0):
    copies = [pltpu.make_async_copy(a, b, sems.at[first + i]) for i, (a, b) in enumerate(pairs)]
    for copy in copies:
        copy.start()
    return copies


def load_chunks(u, c, e, w, ub, cb, eb, wb, more, sems):
    cols = block_of(cb.shape[0], 256)
    count = cb.shape[0] // cols
    chunks = []
    for j in range(count):
        at = pl.ds(j * cols, cols)
        chunks += [(c.at[at], cb.at[at]), (e.at[0, :, at], eb.at[:, at])]
    copies = load([(w, wb), (u, ub)] + chunks[:4], sems)
    copies[0].wait()
    copies += load(chunks[4:] + more, sems, len(copies))
    copies[1].wait()

    def ready(j):
        copies[2 + 2 * j].wait()
        copies[3 + 2 * j].wait()

    return ready, copies[2 + 2 * count :]


def first_odd(u, g, c, e, w, s1, r_high, r_low, ub, gb, cb, eb, wb, sems):
    @pl.when(is_odd())
    def _():
        ready, more = load_chunks(u, c, e, w, ub, cb, eb, wb, [(g, gb)], sems)
        grad = vertex_pass(ub, cb, eb, wb[0:1, :], r_high, r_low, ready)
        more[0].wait()
        s1[0], s1[1] = adagrad(ub[...], gb[...], grad)


def first_rest(
    u, g, c, h, e, w, r_high_in, r_low_in, u1, g1, c_out, h_out,
    ub, gb, cb, hb, eb, wb, r_high, r_low, sems,
):
    odd = is_odd()

    @pl.when(odd)
    def _():
        for copy in load([(u, ub), (c, cb), (h, hb)], sems):
            copy.wait()
        context_pass(ub, cb, hb, r_high_in, r_low_in, c_out, h_out)

    @pl.when(jnp.logical_not(odd))
    def _():
        ready, more = load_chunks(u, c, e, w, ub, cb, eb, wb, [(g, gb), (h, hb)], sems)
        grad = vertex_pass(ub, cb, eb, wb[0:1, :], r_high, r_low, ready)
        more[0].wait()
        u1[...], g1[...] = adagrad(ub[...], gb[...], grad)
        more[1].wait()
        context_pass(ub, cb, hb, r_high, r_low, c_out, h_out)


def second_odd(u1, g1, c, h, e, w, u2, s2, c_out, h_out, r_high, r_low):
    @pl.when(is_odd())
    def _():
        grad = vertex_pass(u1, c, e.at[1], w[1:2, :], r_high, r_low)
        value, moment = adagrad(u1[...], g1[...], grad)
        u2[...] = value
        s2[0], s2[1] = value, moment
        context_pass(u1, c, h, r_high, r_low, c_out, h_out)


def second_even(s1, c, h, e, w, after, grad_out, u2_top, u2_end, c_out, h_out, r_high, r_low):
    @pl.when(jnp.logical_not(is_odd()))
    def _():
        grad = vertex_pass(s1.at[0], c, e.at[1], w[1:2, :], r_high, r_low)
        grad_out[...] = grad
        value = adagrad(s1[0], s1[1], grad)[0]
        middle = u2_top.shape[0]
        u2_top[...], u2_end[...] = value[:middle], value[middle:]
        context_pass(s1.at[0], c, h, r_high, r_low, c_out, h_out)


def third(odd, u, c, e, w, after, g2, r_high, r_low):
    @pl.when(is_odd() == odd)
    def _():
        g2[...] = vertex_pass(u, c, e.at[2], w[2:3, :], r_high, r_low)


def third_odd(u_top, u_end, c, e, w, after, u, *refs):
    middle = u_top.shape[0]
    u[:middle, :] = u_top[...]
    u[middle:, :] = u_end[...]
    third(True, u, c, e, w, after, *refs)


def third_even(*refs):
    third(False, *refs)


def third_context(u_odd, c_odd, h_odd, rh_odd, rl_odd, u_even, c_even, h_even, rh_even, rl_even, c_out, h_out):
    odd = is_odd()

    @pl.when(odd)
    def _():
        context_pass(u_odd, c_odd, h_odd, rh_odd, rl_odd, c_out, h_out)

    @pl.when(jnp.logical_not(odd))
    def _():
        context_pass(u_even, c_even, h_even, rh_even, rl_even, c_out, h_out)


def last(s1, g1, g2_odd, s2, g2_even, u_out, g_out):
    odd = is_odd()

    @pl.when(odd)
    def _():
        value, moment = adagrad(s1[0], s1[1], g1[...])
        u_out[...], g_out[...] = adagrad(value, moment, g2_odd[...])

    @pl.when(jnp.logical_not(odd))
    def _():
        u_out[...], g_out[...] = adagrad(s2[0], s2[1], g2_even[...])


def per_device(vertices, vertex_moments, contexts, context_moments, edge_counts, negative_weights):
    nrows, width = vertices.shape
    ncols = contexts.shape[0]
    count = lax.axis_size("inner")
    assert count % 2 == 0 and edge_counts.shape[0] == 3

    ring = [(i, (i + 1) % count) for i in range(count)]
    unring = [(b, a) for a, b in ring]
    swap = [(i, i ^ 1) for i in range(count)]
    home_odd = [(i, (i - 2) % count if i % 2 else i) for i in range(count)]
    home_even = [(i, i if i % 2 else (i - 2) % count) for i in range(count)]

    def move(value, pairs):
        return lax.ppermute(value, "inner", pairs)

    def f32(*shape):
        return jax.ShapeDtypeStruct(shape, F32)

    block = f32(nrows, width)
    part = f32(nrows // 2, width)
    pair = f32(2, nrows, width)
    ctx = f32(ncols, width)
    half = jax.ShapeDtypeStruct((nrows, ncols), BF16)
    half_buf = pltpu.VMEM((nrows, ncols), BF16)
    vert_buf = pltpu.VMEM((nrows, width), F32)
    ctx_buf = pltpu.VMEM((ncols, width), F32)
    edge_buf = pltpu.VMEM((nrows, ncols), jnp.int32)
    weight_buf = pltpu.VMEM(negative_weights.shape, jnp.int32)
    sems = pltpu.SemaphoreType.DMA((4 + 2 * (ncols // block_of(ncols, 256)),))
    hbm = [
        pltpu.with_memory_space_constraint(x, pltpu.HBM)
        for x in (vertices, vertex_moments, contexts, context_moments, edge_counts, negative_weights)
    ]

    s1o, rh0, rl0 = call(
        first_odd, [HBM] * 5, [pair, half, half],
        [vert_buf, vert_buf, ctx_buf, edge_buf, weight_buf, sems],
        (*hbm[:3], *hbm[4:]), "first_odd",
    )
    s1x = move(s1o, ring)
    *s1, c1, h1 = call(
        first_rest, [HBM] * 6 + [VMEM] * 2, [block, block, ctx, ctx],
        [vert_buf, vert_buf, ctx_buf, ctx_buf, edge_buf, weight_buf, half_buf, half_buf, sems],
        (*hbm, rh0, rl0), "first_rest",
    )
    s1i = [move(x, swap) for x in s1]
    u2e, s2e, c2o, h2o = call(
        second_odd, [VMEM] * 6, [block, pair, ctx, ctx], [half_buf, half_buf],
        (*s1i, c1, h1, edge_counts, negative_weights), "second_odd",
    )
    u2x = move(u2e, ring)
    s2h = move(s2e, swap)
    g1, u2t, u2d, c2e, h2e = call(
        second_even, [VMEM] * 5 + [ANY], [block, part, part, ctx, ctx], [half_buf, half_buf],
        (s1x, c1, h1, edge_counts, negative_weights, u2e), "second_even",
    )
    g1x = move(g1, unring)
    u2ti = move(u2t, swap)
    u2di = move(u2d, swap)
    u2i, g2o, rho, rlo = call(
        third_odd, [VMEM] * 5 + [ANY], [block, block, half, half], [],
        (u2ti, u2di, c2o, edge_counts, negative_weights, u2t), "third_odd",
    )
    g2xo = move(g2o, home_odd)
    g2e, rhe, rle = call(
        third_even, [VMEM] * 4 + [ANY], [block, half, half], [],
        (u2x, c2e, edge_counts, negative_weights, g2o), "third_even",
    )
    g2xe = move(g2e, home_even)
    c3, h3 = call(
        third_context, [VMEM] * 10, [ctx, ctx], [],
        (u2i, c2o, h2o, rho, rlo, u2x, c2e, h2e, rhe, rle), "third_context",
    )
    u3, g3 = call(last, [VMEM] * 5, [block, block], [], (s1o, g1x, g2xo, s2h, g2xe), "last")
    return u3, g3, c3, h3


def solution(mesh):
    split_rows = P(("snap", "inner"), None)
    return jax.shard_map(
        per_device,
        mesh=mesh,
        in_specs=(
            split_rows,
            split_rows,
            split_rows,
            split_rows,
            P(None, None, ("snap", "inner")),
            P(None, ("snap", "inner")),
        ),
        out_specs=(split_rows,) * 4,
        check_vma=False,
    )
```

```python
import jax
import jax.numpy as jnp
from jax import lax
from jax.experimental import pallas as pl
from jax.experimental.pallas import tpu as pltpu
from jax.sharding import PartitionSpec as P

F32 = jnp.float32
BF16 = jnp.bfloat16
RATE = 0.05
EARLY = 3
VMEM = pl.BlockSpec(memory_space=pltpu.VMEM)
HBM = pl.BlockSpec(memory_space=pltpu.HBM)
ANY = pl.BlockSpec(memory_space=pl.ANY)


def split(x):
    high = x.astype(BF16)
    return high, (x - high.astype(F32)).astype(BF16)


def product(a, b, dim_a, dim_b):
    def one(x, y):
        return lax.dot_general(
            x, y, (((dim_a,), (dim_b,)), ((), ())), preferred_element_type=F32
        )

    return one(a[0], b[0]) + (one(a[1], b[0]) + one(a[0], b[1]))


def block_of(size, most):
    return most if size % most == 0 else size


def is_odd():
    return lax.rem(lax.axis_index("inner"), 2) == 1


def adagrad(value, moment, grad):
    moment = moment + grad * grad
    return value - RATE * grad * lax.rsqrt(moment), moment


def vertex_pass(u, c, e, w, r_high, r_low, ready=None):
    us = split(0.5 * u[...])
    wf = w.astype(F32)
    cols = block_of(c.shape[0], 256)
    count = c.shape[0] // cols
    parts = []

    def scores(j):
        if ready is not None:
            ready(j)
        parts.append(split(c[pl.ds(j * cols, cols), :]))
        return product(us, parts[j], 1, 1)

    grad = None
    half_scores = scores(0)
    for j in range(count):
        at = pl.ds(j * cols, cols)
        later = scores(j + 1) if j + 1 < count else None
        ef = e[:, at].astype(F32)
        wj = wf[:, j * cols : (j + 1) * cols]
        resid = split((ef + wj) * jnp.tanh(half_scores) + (wj - ef))
        r_high[:, at] = resid[0]
        r_low[:, at] = resid[1]
        term = product(resid, parts[j], 1, 0)
        grad = term if grad is None else grad + term
        half_scores = later
    return 0.5 * grad


def context_pass(parts, c, h, c_out, h_out):
    us = [split(0.5 * u[...]) for u, _, _ in parts]
    rows = block_of(c.shape[0], 256)
    for j in range(c.shape[0] // rows):
        at = pl.ds(j * rows, rows)
        grad = sum(product((high[:, at], low[:, at]), u, 0, 0) for u, (_, high, low) in zip(us, parts))
        c_out[at, :], h_out[at, :] = adagrad(c[at, :], h[at, :], grad)


def call(body, in_specs, outs, scratch, args, name, room=24):
    return pl.pallas_call(
        body,
        out_shape=outs,
        in_specs=in_specs,
        out_specs=[VMEM] * len(outs),
        scratch_shapes=scratch,
        compiler_params=pltpu.CompilerParams(vmem_limit_bytes=room << 20),
        cost_estimate=pl.CostEstimate(flops=1024, bytes_accessed=1024, transcendentals=0),
        name=name,
    )(*args)


def load(pairs, sems, first=0):
    copies = [pltpu.make_async_copy(a, b, sems.at[first + i]) for i, (a, b) in enumerate(pairs)]
    for copy in copies:
        copy.start()
    return copies


def first_top(u, g, c, h, e, w, s1, r_high, r_low, ub, gb, cb, hb, eb, wb, sems):
    @pl.when(is_odd())
    def _():
        middle = s1.shape[1]
        top, end = pl.ds(0, middle), pl.ds(middle, ub.shape[0] - middle)
        cols = block_of(cb.shape[0], 512)
        count = cb.shape[0] // cols
        chunks = []
        for j in range(count):
            at = pl.ds(j * cols, cols)
            chunks += [(c.at[at], cb.at[at]), (e.at[0, top, at], eb.at[top, at])]
        copies = load(
            [(w, wb), (u, ub)] + chunks + [(g, gb), (e.at[0, end], eb.at[end]), (h, hb)], sems
        )
        copies[0].wait()
        copies[1].wait()
        small = block_of(cb.shape[0], 256)

        def ready(j):
            if j * small % cols == 0:
                at = 2 + 2 * (j * small // cols)
                copies[at].wait()
                copies[at + 1].wait()

        grad = vertex_pass(ub.at[top], cb, eb.at[top], wb[0:1, :], r_high, r_low, ready)
        copies[2 + 2 * count].wait()
        s1[0], s1[1] = adagrad(ub[top, :], gb[top, :], grad)
        for copy in copies[3 + 2 * count :]:
            copy.wait()


def first_end(u, g, c, e, w, s1, r_high, r_low):
    @pl.when(is_odd())
    def _():
        rows = s1.shape[1]
        end = pl.ds(u.shape[0] - rows, rows)
        grad = vertex_pass(u.at[end], c, e.at[end], w[0:1, :], r_high, r_low)
        s1[0], s1[1] = adagrad(u[end, :], g[end, :], grad)


def first_even(
    u, g, c, e, w, u_odd, c_odd, h_odd, rh_top, rl_top, rh_end, rl_end,
    u1, g1, r_high, r_low, c_out, h_out, ub, gb, cb, eb, wb, sems,
):
    odd = is_odd()

    @pl.when(odd)
    def _():
        middle, rest = rh_top.shape[0], rh_end.shape[0]
        parts = [
            (u_odd.at[pl.ds(0, middle)], rh_top, rl_top),
            (u_odd.at[pl.ds(middle, rest)], rh_end, rl_end),
        ]
        context_pass(parts, c_odd, h_odd, c_out, h_out)

    @pl.when(jnp.logical_not(odd))
    def _():
        cols = block_of(cb.shape[0], 256)
        count = cb.shape[0] // cols
        chunks = []
        for j in range(count):
            at = pl.ds(j * cols, cols)
            chunks += [(c.at[at], cb.at[at]), (e.at[0, :, at], eb.at[:, at])]
        copies = load([(w, wb), (u, ub)] + chunks + [(g, gb)], sems)
        copies[0].wait()
        copies[1].wait()

        def ready(j):
            copies[2 + 2 * j].wait()
            copies[3 + 2 * j].wait()

        grad = vertex_pass(ub, cb, eb, wb[0:1, :], r_high, r_low, ready)
        copies[-1].wait()
        u1[...], g1[...] = adagrad(ub[...], gb[...], grad)


def first_context(u, c, h, r_high, r_low, c_out, h_out, ub, cb, hb, sems):
    @pl.when(jnp.logical_not(is_odd()))
    def _():
        for copy in load([(u, ub), (c, cb), (h, hb)], sems):
            copy.wait()
        context_pass([(ub, r_high, r_low)], cb, hb, c_out, h_out)


def second_odd(u1, g1, c, e, w, u2, s2, r_high, r_low):
    @pl.when(is_odd())
    def _():
        grad = vertex_pass(u1, c, e.at[1], w[1:2, :], r_high, r_low)
        value, moment = adagrad(u1[...], g1[...], grad)
        u2[...] = value
        s2[0], s2[1] = value, moment


def second_even(
    s1_top, s1_end, c, e, w, after, u_odd, c_odd, h_odd, rh_odd, rl_odd,
    grad_out, u2_top, u2_end, u1, r_high, r_low, c_out, h_out,
):
    odd = is_odd()

    @pl.when(odd)
    def _():
        context_pass([(u_odd, rh_odd, rl_odd)], c_odd, h_odd, c_out, h_out)

    @pl.when(jnp.logical_not(odd))
    def _():
        middle = s1_top.shape[1]
        u1[:middle, :] = s1_top[0]
        u1[middle:, :] = s1_end[0]
        grad = vertex_pass(u1, c, e.at[1], w[1:2, :], r_high, r_low)
        grad_out[...] = grad
        moment = jnp.concatenate([s1_top[1], s1_end[1]], axis=0)
        value = adagrad(u1[...], moment, grad)[0]
        half = u2_top.shape[0]
        u2_top[...], u2_end[...] = value[:half], value[half:]


def second_context(u, c, h, r_high, r_low, c_out, h_out):
    @pl.when(jnp.logical_not(is_odd()))
    def _():
        context_pass([(u, r_high, r_low)], c, h, c_out, h_out)


def third(odd, u, c, e, w, after, g2, r_high, r_low):
    @pl.when(is_odd() == odd)
    def _():
        g2[...] = vertex_pass(u, c, e.at[2], w[2:3, :], r_high, r_low)


def third_odd(u_top, u_end, c, e, w, after, u, *refs):
    middle = u_top.shape[0]
    u[:middle, :] = u_top[...]
    u[middle:, :] = u_end[...]
    third(True, u, c, e, w, after, *refs)


def third_even(*refs):
    third(False, *refs)


def third_context(u_odd, c_odd, h_odd, rh_odd, rl_odd, u_even, c_even, h_even, rh_even, rl_even, c_out, h_out):
    odd = is_odd()

    @pl.when(odd)
    def _():
        context_pass([(u_odd, rh_odd, rl_odd)], c_odd, h_odd, c_out, h_out)

    @pl.when(jnp.logical_not(odd))
    def _():
        context_pass([(u_even, rh_even, rl_even)], c_even, h_even, c_out, h_out)


def last(s1_top, s1_end, g1, g2_odd, s2, g2_even, u_out, g_out):
    odd = is_odd()

    @pl.when(odd)
    def _():
        middle, rest = s1_top.shape[1], s1_end.shape[1]
        for s1, at in ((s1_top, pl.ds(0, middle)), (s1_end, pl.ds(middle, rest))):
            value, moment = adagrad(s1[0], s1[1], g1[at, :])
            u_out[at, :], g_out[at, :] = adagrad(value, moment, g2_odd[at, :])

    @pl.when(jnp.logical_not(odd))
    def _():
        u_out[...], g_out[...] = adagrad(s2[0], s2[1], g2_even[...])


def per_device(vertices, vertex_moments, contexts, context_moments, edge_counts, negative_weights):
    nrows, width = vertices.shape
    ncols = contexts.shape[0]
    count = lax.axis_size("inner")
    assert count % 2 == 0 and edge_counts.shape[0] == 3

    ring = [(i, (i + 1) % count) for i in range(count)]
    unring = [(b, a) for a, b in ring]
    swap = [(i, i ^ 1) for i in range(count)]
    home_odd = [(i, (i - 2) % count if i % 2 else i) for i in range(count)]
    home_even = [(i, i if i % 2 else (i - 2) % count) for i in range(count)]

    def move(value, pairs):
        return lax.ppermute(value, "inner", pairs)

    def f32(*shape):
        return jax.ShapeDtypeStruct(shape, F32)

    block = f32(nrows, width)
    part = f32(nrows // 2, width)
    pair = f32(2, nrows, width)
    ctx = f32(ncols, width)
    half = jax.ShapeDtypeStruct((nrows, ncols), BF16)
    half_buf = pltpu.VMEM((nrows, ncols), BF16)
    vert_buf = pltpu.VMEM((nrows, width), F32)
    ctx_buf = pltpu.VMEM((ncols, width), F32)
    edge_buf = pltpu.VMEM((nrows, ncols), jnp.int32)
    weight_buf = pltpu.VMEM(negative_weights.shape, jnp.int32)
    sems = pltpu.SemaphoreType.DMA((4 + 2 * (ncols // block_of(ncols, 256)),))
    hbm = [
        pltpu.with_memory_space_constraint(x, pltpu.HBM)
        for x in (vertices, vertex_moments, contexts, context_moments, edge_counts, negative_weights)
    ]

    def stage(rows):
        return [f32(2, rows, width)] + [jax.ShapeDtypeStruct((rows, ncols), BF16)] * 2

    early = EARLY * nrows // 64 * 16
    edges = jax.ShapeDtypeStruct((nrows, ncols), jnp.int32)
    weights = jax.ShapeDtypeStruct(negative_weights.shape, jnp.int32)
    s1t, rht, rlt, ub, gb, cb, hb, eb, wb = call(
        first_top, [HBM] * 6, stage(early) + [block, block, ctx, ctx, edges, weights], [sems], hbm, "first_top",
    )
    s1tx = move(s1t, ring)
    s1d, rhd, rld = call(
        first_end, [VMEM] * 5, stage(nrows - early), [], (ub, gb, cb, eb, wb), "first_end",
    )
    s1dx = move(s1d, ring)
    *s1, rhe0, rle0, c1o, h1o = call(
        first_even, [HBM] * 5 + [VMEM] * 7, [block, block, half, half, ctx, ctx],
        [vert_buf, vert_buf, ctx_buf, edge_buf, weight_buf, sems],
        (*hbm[:3], *hbm[4:], ub, cb, hb, rht, rlt, rhd, rld), "first_even",
    )
    s1i = [move(x, swap) for x in s1]
    c1e, h1e = call(
        first_context, [HBM] * 3 + [VMEM] * 2, [ctx, ctx], [vert_buf, ctx_buf, ctx_buf, sems],
        (hbm[0], hbm[2], hbm[3], rhe0, rle0), "first_context",
    )
    u2e, s2e, rho1, rlo1 = call(
        second_odd, [VMEM] * 5, [block, pair, half, half], [],
        (*s1i, c1o, edge_counts, negative_weights), "second_odd",
    )
    u2x = move(u2e, ring)
    s2h = move(s2e, swap)
    g1, u2t, u2d, u1v, rhe1, rle1, c2o, h2o = call(
        second_even, [VMEM] * 5 + [ANY] + [VMEM] * 5, [block, part, part, block, half, half, ctx, ctx], [],
        (s1tx, s1dx, c1e, edge_counts, negative_weights, u2e, s1i[0], c1o, h1o, rho1, rlo1), "second_even",
    )
    c2e, h2e = call(
        second_context, [VMEM] * 5, [ctx, ctx], [], (u1v, c1e, h1e, rhe1, rle1), "second_context",
    )
    g1x = move(g1, unring)
    u2ti = move(u2t, swap)
    u2di = move(u2d, swap)
    u2i, g2o, rho, rlo = call(
        third_odd, [VMEM] * 5 + [ANY], [block, block, half, half], [],
        (u2ti, u2di, c2o, edge_counts, negative_weights, u2t), "third_odd",
    )
    g2xo = move(g2o, home_odd)
    g2e, rhe, rle = call(
        third_even, [VMEM] * 4 + [ANY], [block, half, half], [],
        (u2x, c2e, edge_counts, negative_weights, g2o), "third_even",
    )
    g2xe = move(g2e, home_even)
    c3, h3 = call(
        third_context, [VMEM] * 10, [ctx, ctx], [],
        (u2i, c2o, h2o, rho, rlo, u2x, c2e, h2e, rhe, rle), "third_context",
    )
    u3, g3 = call(last, [VMEM] * 6, [block, block], [], (s1t, s1d, g1x, g2xo, s2h, g2xe), "last")
    return u3, g3, c3, h3


def solution(mesh):
    split_rows = P(("snap", "inner"), None)
    return jax.shard_map(
        per_device,
        mesh=mesh,
        in_specs=(
            split_rows,
            split_rows,
            split_rows,
            split_rows,
            P(None, None, ("snap", "inner")),
            P(None, ("snap", "inner")),
        ),
        out_specs=(split_rows,) * 4,
        check_vma=False,
    )
```

```python
import jax
import jax.numpy as jnp
from jax import lax
from jax.experimental import pallas as pl
from jax.experimental.pallas import tpu as pltpu
from jax.sharding import PartitionSpec as P

F32 = jnp.float32
BF16 = jnp.bfloat16
RATE = 0.05
EARLY = 3
VMEM = pl.BlockSpec(memory_space=pltpu.VMEM)
HBM = pl.BlockSpec(memory_space=pltpu.HBM)
ANY = pl.BlockSpec(memory_space=pl.ANY)


def split(x):
    high = x.astype(BF16)
    return high, (x - high.astype(F32)).astype(BF16)


def product(a, b, dim_a, dim_b):
    def one(x, y):
        return lax.dot_general(
            x, y, (((dim_a,), (dim_b,)), ((), ())), preferred_element_type=F32
        )

    return one(a[0], b[0]) + (one(a[1], b[0]) + one(a[0], b[1]))


def block_of(size, most):
    return most if size % most == 0 else size


def is_odd():
    return lax.rem(lax.axis_index("inner"), 2) == 1


def adagrad(value, moment, grad):
    moment = moment + grad * grad
    return value - RATE * grad * lax.rsqrt(moment), moment


def vertex_pass(u, c, e, w, r_high, r_low, ready=None):
    us = split(0.5 * u[...])
    wf = w.astype(F32)
    cols = block_of(c.shape[0], 256)
    count = c.shape[0] // cols
    parts = []

    def scores(j):
        if ready is not None:
            ready(j)
        parts.append(split(c[pl.ds(j * cols, cols), :]))
        return product(us, parts[j], 1, 1)

    grad = None
    half_scores = scores(0)
    for j in range(count):
        at = pl.ds(j * cols, cols)
        later = scores(j + 1) if j + 1 < count else None
        ef = e[:, at].astype(F32)
        wj = wf[:, j * cols : (j + 1) * cols]
        resid = split((ef + wj) * jnp.tanh(half_scores) + (wj - ef))
        r_high[:, at] = resid[0]
        r_low[:, at] = resid[1]
        term = product(resid, parts[j], 1, 0)
        grad = term if grad is None else grad + term
        half_scores = later
    return 0.5 * grad


def context_pass(parts, c, h, c_out, h_out):
    us = [split(0.5 * u[...]) for u, _, _ in parts]
    rows = block_of(c.shape[0], 256)
    for j in range(c.shape[0] // rows):
        at = pl.ds(j * rows, rows)
        grad = sum(product((high[:, at], low[:, at]), u, 0, 0) for u, (_, high, low) in zip(us, parts))
        c_out[at, :], h_out[at, :] = adagrad(c[at, :], h[at, :], grad)


def call(body, in_specs, outs, scratch, args, name, room=24):
    return pl.pallas_call(
        body,
        out_shape=outs,
        in_specs=in_specs,
        out_specs=[VMEM] * len(outs),
        scratch_shapes=scratch,
        compiler_params=pltpu.CompilerParams(vmem_limit_bytes=room << 20),
        cost_estimate=pl.CostEstimate(flops=1024, bytes_accessed=1024, transcendentals=0),
        name=name,
    )(*args)


def load(pairs, sems, first=0):
    copies = [pltpu.make_async_copy(a, b, sems.at[first + i]) for i, (a, b) in enumerate(pairs)]
    for copy in copies:
        copy.start()
    return copies


def first_top(u, g, c, h, e, w, s1, r_high, r_low, ub, gb, cb, hb, eb, wb, sems):
    @pl.when(is_odd())
    def _():
        middle = s1.shape[1]
        top, end = pl.ds(0, middle), pl.ds(middle, ub.shape[0] - middle)
        cols = block_of(cb.shape[0], 512)
        count = cb.shape[0] // cols
        chunks = []
        for j in range(count):
            at = pl.ds(j * cols, cols)
            chunks += [(c.at[at], cb.at[at]), (e.at[0, top, at], eb.at[top, at])]
        copies = load(
            [(w, wb), (u, ub)] + chunks + [(g, gb), (e.at[0, end], eb.at[end]), (h, hb)], sems
        )
        copies[0].wait()
        copies[1].wait()
        small = block_of(cb.shape[0], 256)

        def ready(j):
            if j * small % cols == 0:
                at = 2 + 2 * (j * small // cols)
                copies[at].wait()
                copies[at + 1].wait()

        grad = vertex_pass(ub.at[top], cb, eb.at[top], wb[0:1, :], r_high, r_low, ready)
        copies[2 + 2 * count].wait()
        s1[0], s1[1] = adagrad(ub[top, :], gb[top, :], grad)
        for copy in copies[3 + 2 * count :]:
            copy.wait()


def first_end(u, g, c, e, w, s1, r_high, r_low):
    @pl.when(is_odd())
    def _():
        rows = s1.shape[1]
        end = pl.ds(u.shape[0] - rows, rows)
        grad = vertex_pass(u.at[end], c, e.at[end], w[0:1, :], r_high, r_low)
        s1[0], s1[1] = adagrad(u[end, :], g[end, :], grad)


def first_even(
    u, g, c, e, w, u_odd, c_odd, h_odd, rh_top, rl_top, rh_end, rl_end,
    u1, g1, r_high, r_low, c_out, h_out, ub, gb, cb, eb, wb, sems,
):
    odd = is_odd()

    @pl.when(odd)
    def _():
        middle, rest = rh_top.shape[0], rh_end.shape[0]
        parts = [
            (u_odd.at[pl.ds(0, middle)], rh_top, rl_top),
            (u_odd.at[pl.ds(middle, rest)], rh_end, rl_end),
        ]
        context_pass(parts, c_odd, h_odd, c_out, h_out)

    @pl.when(jnp.logical_not(odd))
    def _():
        cols = block_of(cb.shape[0], 256)
        count = cb.shape[0] // cols
        chunks = []
        for j in range(count):
            at = pl.ds(j * cols, cols)
            chunks += [(c.at[at], cb.at[at]), (e.at[0, :, at], eb.at[:, at])]
        copies = load([(w, wb), (u, ub)] + chunks + [(g, gb)], sems)
        copies[0].wait()
        copies[1].wait()

        def ready(j):
            copies[2 + 2 * j].wait()
            copies[3 + 2 * j].wait()

        grad = vertex_pass(ub, cb, eb, wb[0:1, :], r_high, r_low, ready)
        copies[-1].wait()
        u1[...], g1[...] = adagrad(ub[...], gb[...], grad)


def first_context(u, c, h, r_high, r_low, c_out, h_out, ub, cb, hb, sems):
    @pl.when(jnp.logical_not(is_odd()))
    def _():
        for copy in load([(u, ub), (c, cb), (h, hb)], sems):
            copy.wait()
        context_pass([(ub, r_high, r_low)], cb, hb, c_out, h_out)


def second_odd(u1, g1, c, e, w, u2, s2, r_high, r_low):
    @pl.when(is_odd())
    def _():
        grad = vertex_pass(u1, c, e.at[1], w[1:2, :], r_high, r_low)
        value, moment = adagrad(u1[...], g1[...], grad)
        u2[...] = value
        s2[0], s2[1] = value, moment


def second_even(
    s1_top, s1_end, c, e, w, after, u_odd, c_odd, h_odd, rh_odd, rl_odd,
    grad_out, u2_top, u2_end, u1, r_high, r_low, c_out, h_out,
):
    odd = is_odd()

    @pl.when(odd)
    def _():
        context_pass([(u_odd, rh_odd, rl_odd)], c_odd, h_odd, c_out, h_out)

    @pl.when(jnp.logical_not(odd))
    def _():
        middle = s1_top.shape[1]
        u1[:middle, :] = s1_top[0]
        u1[middle:, :] = s1_end[0]
        grad = vertex_pass(u1, c, e.at[1], w[1:2, :], r_high, r_low)
        grad_out[...] = grad
        moment = jnp.concatenate([s1_top[1], s1_end[1]], axis=0)
        value = adagrad(u1[...], moment, grad)[0]
        half = u2_top.shape[0]
        u2_top[...], u2_end[...] = value[:half], value[half:]


def second_context(u, c, h, r_high, r_low, c_out, h_out):
    @pl.when(jnp.logical_not(is_odd()))
    def _():
        context_pass([(u, r_high, r_low)], c, h, c_out, h_out)


def third(odd, u, c, e, w, after, g2, r_high, r_low):
    @pl.when(is_odd() == odd)
    def _():
        g2[...] = vertex_pass(u, c, e.at[2], w[2:3, :], r_high, r_low)


def third_odd(u_top, u_end, c, e, w, after, u, *refs):
    middle = u_top.shape[0]
    u[:middle, :] = u_top[...]
    u[middle:, :] = u_end[...]
    third(True, u, c, e, w, after, *refs)


def third_even(u, c, e, w, g2_odd, g2, r_high, r_low):
    @pl.when(is_odd())
    def _():
        g2[...] = g2_odd[...]

    third(False, u, c, e, w, g2_odd, g2, r_high, r_low)


def third_context(u_odd, c_odd, h_odd, rh_odd, rl_odd, u_even, c_even, h_even, rh_even, rl_even, c_out, h_out):
    odd = is_odd()

    @pl.when(odd)
    def _():
        context_pass([(u_odd, rh_odd, rl_odd)], c_odd, h_odd, c_out, h_out)

    @pl.when(jnp.logical_not(odd))
    def _():
        context_pass([(u_even, rh_even, rl_even)], c_even, h_even, c_out, h_out)


def last(s1_top, s1_end, g1, s2, g2, u_out, g_out):
    odd = is_odd()

    @pl.when(odd)
    def _():
        middle, rest = s1_top.shape[1], s1_end.shape[1]
        for s1, at in ((s1_top, pl.ds(0, middle)), (s1_end, pl.ds(middle, rest))):
            value, moment = adagrad(s1[0], s1[1], g1[at, :])
            u_out[at, :], g_out[at, :] = adagrad(value, moment, g2[at, :])

    @pl.when(jnp.logical_not(odd))
    def _():
        u_out[...], g_out[...] = adagrad(s2[0], s2[1], g2[...])


def per_device(vertices, vertex_moments, contexts, context_moments, edge_counts, negative_weights):
    nrows, width = vertices.shape
    ncols = contexts.shape[0]
    count = lax.axis_size("inner")
    assert count % 2 == 0 and edge_counts.shape[0] == 3

    ring = [(i, (i + 1) % count) for i in range(count)]
    unring = [(b, a) for a, b in ring]
    swap = [(i, i ^ 1) for i in range(count)]
    home = [(i, (i - 2) % count) for i in range(count)]

    def move(value, pairs):
        return lax.ppermute(value, "inner", pairs)

    def f32(*shape):
        return jax.ShapeDtypeStruct(shape, F32)

    block = f32(nrows, width)
    part = f32(nrows // 2, width)
    pair = f32(2, nrows, width)
    ctx = f32(ncols, width)
    half = jax.ShapeDtypeStruct((nrows, ncols), BF16)
    half_buf = pltpu.VMEM((nrows, ncols), BF16)
    vert_buf = pltpu.VMEM((nrows, width), F32)
    ctx_buf = pltpu.VMEM((ncols, width), F32)
    edge_buf = pltpu.VMEM((nrows, ncols), jnp.int32)
    weight_buf = pltpu.VMEM(negative_weights.shape, jnp.int32)
    sems = pltpu.SemaphoreType.DMA((4 + 2 * (ncols // block_of(ncols, 256)),))
    hbm = [
        pltpu.with_memory_space_constraint(x, pltpu.HBM)
        for x in (vertices, vertex_moments, contexts, context_moments, edge_counts, negative_weights)
    ]

    def stage(rows):
        return [f32(2, rows, width)] + [jax.ShapeDtypeStruct((rows, ncols), BF16)] * 2

    early = EARLY * nrows // 64 * 16
    edges = jax.ShapeDtypeStruct((nrows, ncols), jnp.int32)
    weights = jax.ShapeDtypeStruct(negative_weights.shape, jnp.int32)
    s1t, rht, rlt, ub, gb, cb, hb, eb, wb = call(
        first_top, [HBM] * 6, stage(early) + [block, block, ctx, ctx, edges, weights], [sems], hbm, "first_top",
    )
    s1tx = move(s1t, ring)
    s1d, rhd, rld = call(
        first_end, [VMEM] * 5, stage(nrows - early), [], (ub, gb, cb, eb, wb), "first_end",
    )
    s1dx = move(s1d, ring)
    *s1, rhe0, rle0, c1o, h1o = call(
        first_even, [HBM] * 5 + [VMEM] * 7, [block, block, half, half, ctx, ctx],
        [vert_buf, vert_buf, ctx_buf, edge_buf, weight_buf, sems],
        (*hbm[:3], *hbm[4:], ub, cb, hb, rht, rlt, rhd, rld), "first_even",
    )
    s1i = [move(x, swap) for x in s1]
    c1e, h1e = call(
        first_context, [HBM] * 3 + [VMEM] * 2, [ctx, ctx], [vert_buf, ctx_buf, ctx_buf, sems],
        (hbm[0], hbm[2], hbm[3], rhe0, rle0), "first_context",
    )
    u2e, s2e, rho1, rlo1 = call(
        second_odd, [VMEM] * 5, [block, pair, half, half], [],
        (*s1i, c1o, edge_counts, negative_weights), "second_odd",
    )
    u2x = move(u2e, ring)
    s2h = move(s2e, swap)
    g1, u2t, u2d, u1v, rhe1, rle1, c2o, h2o = call(
        second_even, [VMEM] * 5 + [ANY] + [VMEM] * 5, [block, part, part, block, half, half, ctx, ctx], [],
        (s1tx, s1dx, c1e, edge_counts, negative_weights, u2e, s1i[0], c1o, h1o, rho1, rlo1), "second_even",
    )
    c2e, h2e = call(
        second_context, [VMEM] * 5, [ctx, ctx], [], (u1v, c1e, h1e, rhe1, rle1), "second_context",
    )
    g1x = move(g1, unring)
    u2ti = move(u2t, swap)
    u2di = move(u2d, swap)
    u2i, g2o, rho, rlo = call(
        third_odd, [VMEM] * 5 + [ANY], [block, block, half, half], [],
        (u2ti, u2di, c2o, edge_counts, negative_weights, u2t), "third_odd",
    )
    g2, rhe, rle = call(
        third_even, [VMEM] * 5, [block, half, half], [],
        (u2x, c2e, edge_counts, negative_weights, g2o), "third_even",
    )
    g2x = move(g2, home)
    c3, h3 = call(
        third_context, [VMEM] * 10, [ctx, ctx], [],
        (u2i, c2o, h2o, rho, rlo, u2x, c2e, h2e, rhe, rle), "third_context",
    )
    u3, g3 = call(last, [VMEM] * 5, [block, block], [], (s1t, s1d, g1x, s2h, g2x), "last")
    return u3, g3, c3, h3


def solution(mesh):
    split_rows = P(("snap", "inner"), None)
    return jax.shard_map(
        per_device,
        mesh=mesh,
        in_specs=(
            split_rows,
            split_rows,
            split_rows,
            split_rows,
            P(None, None, ("snap", "inner")),
            P(None, ("snap", "inner")),
        ),
        out_specs=(split_rows,) * 4,
        check_vma=False,
    )
```

```python
import jax
import jax.numpy as jnp
from jax import lax
from jax.experimental import pallas as pl
from jax.experimental.pallas import tpu as pltpu
from jax.sharding import PartitionSpec as P

F32 = jnp.float32
BF16 = jnp.bfloat16
RATE = 0.05
EARLY = 5
VMEM = pl.BlockSpec(memory_space=pltpu.VMEM)
HBM = pl.BlockSpec(memory_space=pltpu.HBM)
ANY = pl.BlockSpec(memory_space=pl.ANY)


def split(x):
    high = x.astype(BF16)
    return high, (x - high.astype(F32)).astype(BF16)


def product(a, b, dim_a, dim_b):
    def one(x, y):
        return lax.dot_general(
            x, y, (((dim_a,), (dim_b,)), ((), ())), preferred_element_type=F32
        )

    return one(a[0], b[0]) + (one(a[1], b[0]) + one(a[0], b[1]))


def block_of(size, most):
    return most if size % most == 0 else size


def is_odd():
    return lax.rem(lax.axis_index("inner"), 2) == 1


def adagrad(value, moment, grad):
    moment = moment + grad * grad
    return value - RATE * grad * lax.rsqrt(moment), moment


def vertex_pass(u, c, e, w, r_high, r_low, ready=None):
    us = split(0.5 * u[...])
    wf = w.astype(F32)
    cols = block_of(c.shape[0], 256)
    count = c.shape[0] // cols
    parts = []

    def scores(j):
        if ready is not None:
            ready(j)
        parts.append(split(c[pl.ds(j * cols, cols), :]))
        return product(us, parts[j], 1, 1)

    grad = None
    half_scores = scores(0)
    for j in range(count):
        at = pl.ds(j * cols, cols)
        later = scores(j + 1) if j + 1 < count else None
        ef = e[:, at].astype(F32)
        wj = wf[:, j * cols : (j + 1) * cols]
        resid = split((ef + wj) * jnp.tanh(half_scores) + (wj - ef))
        r_high[:, at] = resid[0]
        r_low[:, at] = resid[1]
        term = product(resid, parts[j], 1, 0)
        grad = term if grad is None else grad + term
        half_scores = later
    return 0.5 * grad


def context_pass(parts, c, h, c_out, h_out):
    us = [split(0.5 * u[...]) for u, _, _ in parts]
    rows = block_of(c.shape[0], 256)
    for j in range(c.shape[0] // rows):
        at = pl.ds(j * rows, rows)
        grad = sum(product((high[:, at], low[:, at]), u, 0, 0) for u, (_, high, low) in zip(us, parts))
        c_out[at, :], h_out[at, :] = adagrad(c[at, :], h[at, :], grad)


def call(body, in_specs, outs, scratch, args, name, flops=1024):
    return pl.pallas_call(
        body,
        out_shape=outs,
        in_specs=in_specs,
        out_specs=[VMEM] * len(outs),
        scratch_shapes=scratch,
        compiler_params=pltpu.CompilerParams(vmem_limit_bytes=24 << 20),
        cost_estimate=pl.CostEstimate(flops=flops, bytes_accessed=1024, transcendentals=0),
        name=name,
    )(*args)


def load(pairs, sems, first=0):
    copies = [pltpu.make_async_copy(a, b, sems.at[first + i]) for i, (a, b) in enumerate(pairs)]
    for copy in copies:
        copy.start()
    return copies


def first_top(u, g, c, h, e, w, s1, r_high, r_low, ub, gb, cb, hb, eb, wb, sems):
    @pl.when(is_odd())
    def _():
        middle = s1.shape[1]
        top, end = pl.ds(0, middle), pl.ds(middle, ub.shape[0] - middle)
        cols = block_of(cb.shape[0], 512)
        count = cb.shape[0] // cols
        chunks = []
        for j in range(count):
            at = pl.ds(j * cols, cols)
            chunks += [(c.at[at], cb.at[at]), (e.at[0, top, at], eb.at[top, at])]
        copies = load(
            [(w, wb), (u, ub)] + chunks + [(g, gb), (e.at[0, end], eb.at[end]), (h, hb)], sems
        )
        copies[0].wait()
        copies[1].wait()
        small = block_of(cb.shape[0], 256)

        def ready(j):
            if j * small % cols == 0:
                at = 2 + 2 * (j * small // cols)
                copies[at].wait()
                copies[at + 1].wait()

        grad = vertex_pass(ub.at[top], cb, eb.at[top], wb[0:1, :], r_high, r_low, ready)
        copies[2 + 2 * count].wait()
        s1[0], s1[1] = adagrad(ub[top, :], gb[top, :], grad)
        for copy in copies[3 + 2 * count :]:
            copy.wait()


def first_end(u, g, c, e, w, s1, r_high, r_low):
    @pl.when(is_odd())
    def _():
        rows = s1.shape[1]
        end = pl.ds(u.shape[0] - rows, rows)
        grad = vertex_pass(u.at[end], c, e.at[end], w[0:1, :], r_high, r_low)
        s1[0], s1[1] = adagrad(u[end, :], g[end, :], grad)


def first_even(
    u, g, c, e, w, u_odd, c_odd, h_odd, rh_top, rl_top, rh_end, rl_end,
    u1, g1, r_high, r_low, c_out, h_out, ub, gb, cb, eb, wb, sems,
):
    odd = is_odd()

    @pl.when(odd)
    def _():
        middle, rest = rh_top.shape[0], rh_end.shape[0]
        parts = [
            (u_odd.at[pl.ds(0, middle)], rh_top, rl_top),
            (u_odd.at[pl.ds(middle, rest)], rh_end, rl_end),
        ]
        context_pass(parts, c_odd, h_odd, c_out, h_out)

    @pl.when(jnp.logical_not(odd))
    def _():
        cols = block_of(cb.shape[0], 256)
        count = cb.shape[0] // cols
        chunks = []
        for j in range(count):
            at = pl.ds(j * cols, cols)
            chunks += [(c.at[at], cb.at[at]), (e.at[0, :, at], eb.at[:, at])]
        copies = load([(w, wb), (u, ub)] + chunks + [(g, gb)], sems)
        copies[0].wait()
        copies[1].wait()

        def ready(j):
            copies[2 + 2 * j].wait()
            copies[3 + 2 * j].wait()

        grad = vertex_pass(ub, cb, eb, wb[0:1, :], r_high, r_low, ready)
        copies[-1].wait()
        u1[...], g1[...] = adagrad(ub[...], gb[...], grad)


def first_context(u, c, h, r_high, r_low, after, c_out, h_out, ub, cb, hb, sems):
    @pl.when(jnp.logical_not(is_odd()))
    def _():
        for copy in load([(u, ub), (c, cb), (h, hb)], sems):
            copy.wait()
        context_pass([(ub, r_high, r_low)], cb, hb, c_out, h_out)


def second_odd(u1, g1, c, e, w, u2, g2, r_high, r_low):
    @pl.when(is_odd())
    def _():
        grad = vertex_pass(u1, c, e.at[1], w[1:2, :], r_high, r_low)
        u2[...], g2[...] = adagrad(u1[...], g1[...], grad)


def second_top(
    s1, c, e, w, u_odd, c_odd, h_odd, rh_odd, rl_odd, u2_odd,
    u2, grad_out, r_high, r_low, c_out, h_out,
):
    odd = is_odd()
    rows = u2.shape[0]

    @pl.when(odd)
    def _():
        u2[...] = u2_odd[:rows, :]
        context_pass([(u_odd, rh_odd, rl_odd)], c_odd, h_odd, c_out, h_out)

    @pl.when(jnp.logical_not(odd))
    def _():
        grad = vertex_pass(s1.at[0], c, e.at[1, pl.ds(0, rows)], w[1:2, :], r_high, r_low)
        grad_out[...] = grad
        u2[...] = adagrad(s1[0], s1[1], grad)[0]


def second_end(s1, c, e, w, grad_top, u2_odd, g2_odd, u2, grad_out, r_high, r_low):
    odd = is_odd()
    middle, rows = grad_top.shape[0], u2.shape[0]

    @pl.when(odd)
    def _():
        u2[...] = u2_odd[middle:, :]
        grad_out[...] = g2_odd[...]

    @pl.when(jnp.logical_not(odd))
    def _():
        grad = vertex_pass(s1.at[0], c, e.at[1, pl.ds(middle, rows)], w[1:2, :], r_high, r_low)
        grad_out[:middle, :] = grad_top[...]
        grad_out[middle:, :] = grad
        u2[...] = adagrad(s1[0], s1[1], grad)[0]


def second_context(s1_top, s1_end, c, h, rh_top, rl_top, rh_end, rl_end, c_out, h_out):
    @pl.when(jnp.logical_not(is_odd()))
    def _():
        parts = [(s1_top.at[0], rh_top, rl_top), (s1_end.at[0], rh_end, rl_end)]
        context_pass(parts, c, h, c_out, h_out)


def third(odd, u, c, e, w, after, g2, r_high, r_low):
    @pl.when(is_odd() == odd)
    def _():
        g2[...] = vertex_pass(u, c, e.at[2], w[2:3, :], r_high, r_low)


def third_odd(u_top, u_end, c, e, w, after, u, *refs):
    row = 0
    for part in (u_top, u_end):
        u[pl.ds(row, part.shape[0]), :] = part[...]
        row += part.shape[0]
    third(True, u, c, e, w, after, *refs)


def third_even(u, c, e, w, g2_odd, g2, r_high, r_low):
    @pl.when(is_odd())
    def _():
        g2[...] = g2_odd[...]

    third(False, u, c, e, w, g2_odd, g2, r_high, r_low)


def third_context(u_odd, c_odd, h_odd, rh_odd, rl_odd, u_even, c_even, h_even, rh_even, rl_even, after, c_out, h_out):
    odd = is_odd()

    @pl.when(odd)
    def _():
        context_pass([(u_odd, rh_odd, rl_odd)], c_odd, h_odd, c_out, h_out)

    @pl.when(jnp.logical_not(odd))
    def _():
        context_pass([(u_even, rh_even, rl_even)], c_even, h_even, c_out, h_out)


def last(s1_top, s1_end, g1, u2, g2, u_out, g_out):
    odd = is_odd()

    @pl.when(odd)
    def _():
        middle, rest = s1_top.shape[1], s1_end.shape[1]
        for s1, at in ((s1_top, pl.ds(0, middle)), (s1_end, pl.ds(middle, rest))):
            value, moment = adagrad(s1[0], s1[1], g1[at, :])
            u_out[at, :], g_out[at, :] = adagrad(value, moment, g2[at, :])

    @pl.when(jnp.logical_not(odd))
    def _():
        u_out[...], g_out[...] = adagrad(u2[...], g1[...], g2[...])


def per_device(vertices, vertex_moments, contexts, context_moments, edge_counts, negative_weights):
    nrows, width = vertices.shape
    ncols = contexts.shape[0]
    count = lax.axis_size("inner")
    assert count % 2 == 0 and edge_counts.shape[0] == 3

    ring = [(i, (i + 1) % count) for i in range(count)]
    unring = [(b, a) for a, b in ring]
    swap = [(i, i ^ 1) for i in range(count)]
    home = [(i, (i - 2) % count) for i in range(count)]

    def move(value, pairs):
        return lax.ppermute(value, "inner", pairs)

    def f32(*shape):
        return jax.ShapeDtypeStruct(shape, F32)

    block = f32(nrows, width)
    ctx = f32(ncols, width)
    half = jax.ShapeDtypeStruct((nrows, ncols), BF16)
    half_buf = pltpu.VMEM((nrows, ncols), BF16)
    vert_buf = pltpu.VMEM((nrows, width), F32)
    ctx_buf = pltpu.VMEM((ncols, width), F32)
    edge_buf = pltpu.VMEM((nrows, ncols), jnp.int32)
    weight_buf = pltpu.VMEM(negative_weights.shape, jnp.int32)
    sems = pltpu.SemaphoreType.DMA((4 + 2 * (ncols // block_of(ncols, 256)),))
    hbm = [
        pltpu.with_memory_space_constraint(x, pltpu.HBM)
        for x in (vertices, vertex_moments, contexts, context_moments, edge_counts, negative_weights)
    ]

    def stage(rows):
        return [f32(2, rows, width)] + [jax.ShapeDtypeStruct((rows, ncols), BF16)] * 2

    early = EARLY * nrows // 128 * 16
    edges = jax.ShapeDtypeStruct((nrows, ncols), jnp.int32)
    weights = jax.ShapeDtypeStruct(negative_weights.shape, jnp.int32)
    s1t, rht, rlt, ub, gb, cb, hb, eb, wb = call(
        first_top, [HBM] * 6, stage(early) + [block, block, ctx, ctx, edges, weights], [sems], hbm, "first_top",
    )
    s1tx = move(s1t, ring)
    s1d, rhd, rld = call(
        first_end, [VMEM] * 5, stage(nrows - early), [], (ub, gb, cb, eb, wb), "first_end",
    )
    s1dx = move(s1d, ring)
    *s1, rhe0, rle0, c1o, h1o = call(
        first_even, [HBM] * 5 + [VMEM] * 7, [block, block, half, half, ctx, ctx],
        [vert_buf, vert_buf, ctx_buf, edge_buf, weight_buf, sems],
        (*hbm[:3], *hbm[4:], ub, cb, hb, rht, rlt, rhd, rld), "first_even",
    )
    s1i = [move(x, swap) for x in s1]
    u2e, m2e, rho1, rlo1 = call(
        second_odd, [VMEM] * 5, [block, block, half, half], [],
        (*s1i, c1o, edge_counts, negative_weights), "second_odd",
    )
    c1e, h1e = call(
        first_context, [HBM] * 3 + [VMEM] * 2 + [ANY], [ctx, ctx], [vert_buf, ctx_buf, ctx_buf, sems],
        (hbm[0], hbm[2], hbm[3], rhe0, rle0, u2e), "first_context",
    )
    u2x = move(u2e, ring)
    u2t, g1t, rht1, rlt1, c2o, h2o = call(
        second_top, [VMEM] * 10, [f32(early, width)] * 2 + stage(early)[1:] + [ctx, ctx], [],
        (s1tx, c1e, edge_counts, negative_weights, s1i[0], c1o, h1o, rho1, rlo1, u2e), "second_top",
    )
    u2ti = move(u2t, swap)
    u2d, g1, rhd1, rld1 = call(
        second_end, [VMEM] * 7, [f32(nrows - early, width), block] + stage(nrows - early)[1:], [],
        (s1dx, c1e, edge_counts, negative_weights, g1t, u2e, m2e), "second_end",
    )
    u2di = move(u2d, swap)
    g1x = move(g1, unring)
    c2e, h2e = call(
        second_context, [VMEM] * 8, [ctx, ctx], [],
        (s1tx, s1dx, c1e, h1e, rht1, rlt1, rhd1, rld1), "second_context",
    )
    u2i, g2o, rho, rlo = call(
        third_odd, [VMEM] * 5 + [ANY], [block, block, half, half], [],
        (u2ti, u2di, c2o, edge_counts, negative_weights, u2d), "third_odd",
    )
    g2, rhe, rle = call(
        third_even, [VMEM] * 5, [block, half, half], [],
        (u2x, c2e, edge_counts, negative_weights, g2o), "third_even",
    )
    g2x = move(g2, home)
    c3, h3 = call(
        third_context, [VMEM] * 10 + [ANY], [ctx, ctx], [],
        (u2i, c2o, h2o, rho, rlo, u2x, c2e, h2e, rhe, rle, g1x), "third_context", 10000000000,
    )
    u3, g3 = call(last, [VMEM] * 5, [block, block], [], (s1t, s1d, g1x, u2i, g2x), "last")
    return u3, g3, c3, h3


def solution(mesh):
    split_rows = P(("snap", "inner"), None)
    return jax.shard_map(
        per_device,
        mesh=mesh,
        in_specs=(
            split_rows,
            split_rows,
            split_rows,
            split_rows,
            P(None, None, ("snap", "inner")),
            P(None, ("snap", "inner")),
        ),
        out_specs=(split_rows,) * 4,
        check_vma=False,
    )
```

```python
import functools

import jax
import jax.numpy as jnp
from jax import lax
from jax.experimental import pallas as pl
from jax.experimental.pallas import tpu as pltpu
from jax.sharding import PartitionSpec as P

F32 = jnp.float32
BF16 = jnp.bfloat16
RATE = 0.05
EARLY = 9
VMEM = pl.BlockSpec(memory_space=pltpu.VMEM)
HBM = pl.BlockSpec(memory_space=pltpu.HBM)
ANY = pl.BlockSpec(memory_space=pl.ANY)


def split(x):
    high = x.astype(BF16)
    return high, (x - high.astype(F32)).astype(BF16)


def product(a, b, dim_a, dim_b):
    def one(x, y):
        return lax.dot_general(
            x, y, (((dim_a,), (dim_b,)), ((), ())), preferred_element_type=F32
        )

    return one(a[0], b[0]) + (one(a[1], b[0]) + one(a[0], b[1]))


def block_of(size, most):
    return most if size % most == 0 else size


def is_odd():
    return lax.rem(lax.axis_index("inner"), 2) == 1


def adagrad(value, moment, grad):
    moment = moment + grad * grad
    return value - RATE * grad * lax.rsqrt(moment), moment


def vertex_pass(u, c, e, w, r_high, r_low, ready=None):
    us = split(0.5 * u[...])
    wf = w.astype(F32)
    cols = block_of(c.shape[0], 256)
    count = c.shape[0] // cols
    parts = []

    def scores(j):
        if ready is not None:
            ready(j)
        parts.append(split(c[pl.ds(j * cols, cols), :]))
        return product(us, parts[j], 1, 1)

    grad = None
    half_scores = scores(0)
    for j in range(count):
        at = pl.ds(j * cols, cols)
        later = scores(j + 1) if j + 1 < count else None
        ef = e[:, at].astype(F32)
        wj = wf[:, j * cols : (j + 1) * cols]
        resid = split((ef + wj) * jnp.tanh(half_scores) + (wj - ef))
        r_high[:, at] = resid[0]
        r_low[:, at] = resid[1]
        term = product(resid, parts[j], 1, 0)
        grad = term if grad is None else grad + term
        half_scores = later
    return 0.5 * grad


def context_pass(parts, c, h, c_out, h_out):
    us = [split(0.5 * u[...]) for u, _, _ in parts]
    rows = block_of(c.shape[0], 256)
    for j in range(c.shape[0] // rows):
        at = pl.ds(j * rows, rows)
        grad = sum(product((high[:, at], low[:, at]), u, 0, 0) for u, (_, high, low) in zip(us, parts))
        c_out[at, :], h_out[at, :] = adagrad(c[at, :], h[at, :], grad)


def call(body, in_specs, outs, scratch, args, name, flops=1024, out_spec=VMEM, aliases=None):
    return pl.pallas_call(
        body,
        out_shape=outs,
        in_specs=in_specs,
        out_specs=[out_spec] * len(outs),
        scratch_shapes=scratch,
        input_output_aliases=aliases or {},
        compiler_params=pltpu.CompilerParams(vmem_limit_bytes=24 << 20),
        cost_estimate=pl.CostEstimate(flops=flops, bytes_accessed=1024, transcendentals=0),
        name=name,
    )(*args)


def load(pairs, sems, first=0):
    copies = [pltpu.make_async_copy(a, b, sems.at[first + i]) for i, (a, b) in enumerate(pairs)]
    for copy in copies:
        copy.start()
    return copies


def first_top(u, g, c, e, w, s1, r_high, r_low, ub, cb, gb, eb, wb, sems):
    @pl.when(is_odd())
    def _():
        top = pl.ds(0, ub.shape[0])
        cols = block_of(cb.shape[0], 512)
        count = cb.shape[0] // cols
        chunks = []
        for j in range(count):
            at = pl.ds(j * cols, cols)
            chunks += [(c.at[at], cb.at[at]), (e.at[0, top, at], eb.at[:, at])]
        copies = load([(w, wb), (u.at[top], ub)] + chunks + [(g.at[top], gb)], sems)
        copies[0].wait()
        copies[1].wait()
        small = block_of(cb.shape[0], 256)

        def ready(j):
            if j * small % cols == 0:
                at = 2 + 2 * (j * small // cols)
                copies[at].wait()
                copies[at + 1].wait()

        grad = vertex_pass(ub, cb, eb, wb[0:1, :], r_high, r_low, ready)
        copies[-1].wait()
        s1[0], s1[1] = adagrad(ub[...], gb[...], grad)


def first_end(u, g, h, e, w, cb, s1, r_high, r_low, ub, hb, gb, eb, wb, sems):
    @pl.when(is_odd())
    def _():
        rows = ub.shape[0]
        end = pl.ds(u.shape[0] - rows, rows)
        for copy in load(
            [(u.at[end], ub), (g.at[end], gb), (e.at[0, end], eb), (w, wb), (h, hb)], sems
        ):
            copy.wait()
        grad = vertex_pass(ub, cb, eb, wb[0:1, :], r_high, r_low)
        s1[0], s1[1] = adagrad(ub[...], gb[...], grad)


def first_even(
    u, g, c, e, w, u_top, u_end, c_odd, h_odd, rh_top, rl_top, rh_end, rl_end,
    u1, g1, r_high, r_low, c_out, h_out, ub, gb, cb, eb, wb, sems,
):
    odd = is_odd()

    @pl.when(odd)
    def _():
        parts = [(u_top, rh_top, rl_top), (u_end, rh_end, rl_end)]
        context_pass(parts, c_odd, h_odd, c_out, h_out)

    @pl.when(jnp.logical_not(odd))
    def _():
        cols = block_of(cb.shape[0], 256)
        count = cb.shape[0] // cols
        chunks = []
        for j in range(count):
            at = pl.ds(j * cols, cols)
            chunks += [(c.at[at], cb.at[at]), (e.at[0, :, at], eb.at[:, at])]
        copies = load([(w, wb), (u, ub)] + chunks + [(g, gb)], sems)
        copies[0].wait()
        copies[1].wait()

        def ready(j):
            copies[2 + 2 * j].wait()
            copies[3 + 2 * j].wait()

        grad = vertex_pass(ub, cb, eb, wb[0:1, :], r_high, r_low, ready)
        copies[-1].wait()
        u1[...], g1[...] = adagrad(ub[...], gb[...], grad)


def first_context(u, c, h, r_high, r_low, after, c_out, h_out, ub, cb, hb, sems):
    @pl.when(jnp.logical_not(is_odd()))
    def _():
        for copy in load([(u, ub), (c, cb), (h, hb)], sems):
            copy.wait()
        context_pass([(ub, r_high, r_low)], cb, hb, c_out, h_out)


def second_odd(u1, g1, c, e, w, u2, g2, r_high, r_low):
    @pl.when(is_odd())
    def _():
        grad = vertex_pass(u1, c, e.at[1], w[1:2, :], r_high, r_low)
        u2[...], g2[...] = adagrad(u1[...], g1[...], grad)


def second_top(
    s1, c, e, w, u_odd, c_odd, h_odd, rh_odd, rl_odd, u2_odd,
    u2, grad_out, r_high, r_low, c_out, h_out,
):
    odd = is_odd()
    rows = u2.shape[0]

    @pl.when(odd)
    def _():
        u2[...] = u2_odd[:rows, :]
        context_pass([(u_odd, rh_odd, rl_odd)], c_odd, h_odd, c_out, h_out)

    @pl.when(jnp.logical_not(odd))
    def _():
        grad = vertex_pass(s1.at[0], c, e.at[1, pl.ds(0, rows)], w[1:2, :], r_high, r_low)
        grad_out[...] = grad
        u2[...] = adagrad(s1[0], s1[1], grad)[0]


def second_end(s1, c, e, w, grad_top, u2_odd, g2_odd, u2, grad_out, r_high, r_low):
    odd = is_odd()
    middle, rows = grad_top.shape[0], u2.shape[0]

    @pl.when(odd)
    def _():
        u2[...] = u2_odd[middle:, :]
        grad_out[...] = g2_odd[...]

    @pl.when(jnp.logical_not(odd))
    def _():
        grad = vertex_pass(s1.at[0], c, e.at[1, pl.ds(middle, rows)], w[1:2, :], r_high, r_low)
        grad_out[:middle, :] = grad_top[...]
        grad_out[middle:, :] = grad
        u2[...] = adagrad(s1[0], s1[1], grad)[0]


def second_context(s1_top, s1_end, c, h, rh_top, rl_top, rh_end, rl_end, c_out, h_out):
    @pl.when(jnp.logical_not(is_odd()))
    def _():
        parts = [(s1_top.at[0], rh_top, rl_top), (s1_end.at[0], rh_end, rl_end)]
        context_pass(parts, c, h, c_out, h_out)


def third(odd, row, u, c, e, w, g2, r_high, r_low):
    rows = pl.ds(row, g2.shape[0])

    @pl.when(is_odd() == odd)
    def _():
        g2[...] = vertex_pass(u.at[rows], c, e.at[2, rows], w[2:3, :], r_high, r_low)


def third_odd_top(u_top, u_end, c, e, w, after, u, g2, r_high, r_low):
    u[: u_top.shape[0], :] = u_top[...]
    u[u_top.shape[0] :, :] = u_end[...]
    third(True, 0, u, c, e, w, g2, r_high, r_low)


def third_odd_end(u, c, e, w, after, g2, r_high, r_low):
    third(True, u.shape[0] - g2.shape[0], u, c, e, w, g2, r_high, r_low)


def third_even(row, u, c, e, w, g2_odd, g2, r_high, r_low):
    @pl.when(is_odd())
    def _():
        g2[...] = g2_odd[...]

    third(False, row, u, c, e, w, g2, r_high, r_low)


def third_context(
    u_odd, c_odd, h_odd, rh_odd, rl_odd, rh_odd_end, rl_odd_end,
    u_even, c_even, h_even, rh_even, rl_even, rh_even_end, rl_even_end, after, c_out, h_out,
):
    odd = is_odd()
    middle = rh_odd.shape[0]
    top, end = pl.ds(0, middle), pl.ds(middle, rh_odd_end.shape[0])

    @pl.when(odd)
    def _():
        parts = [(u_odd.at[top], rh_odd, rl_odd), (u_odd.at[end], rh_odd_end, rl_odd_end)]
        context_pass(parts, c_odd, h_odd, c_out, h_out)

    @pl.when(jnp.logical_not(odd))
    def _():
        parts = [(u_even.at[top], rh_even, rl_even), (u_even.at[end], rh_even_end, rl_even_end)]
        context_pass(parts, c_even, h_even, c_out, h_out)


def last(row, s1_top, s1_end, g1, u2, g2, u_out, g_out, ub, gb, sems):
    odd = is_odd()
    rows = g2.shape[0]

    @pl.when(odd)
    def _():
        begin = 0
        for s1 in (s1_top, s1_end):
            low, high = max(row, begin), min(row + rows, begin + s1.shape[1])
            if low < high:
                at, here = pl.ds(low - begin, high - low), pl.ds(low - row, high - low)
                value, moment = adagrad(s1[0, at, :], s1[1, at, :], g1[pl.ds(low, high - low), :])
                ub[here, :], gb[here, :] = adagrad(value, moment, g2[here, :])
            begin += s1.shape[1]

    @pl.when(jnp.logical_not(odd))
    def _():
        at = pl.ds(row, rows)
        ub[...], gb[...] = adagrad(u2[at, :], g1[at, :], g2[...])

    at = pl.ds(row, rows)
    for copy in load([(ub, u_out.at[at]), (gb, g_out.at[at])], sems):
        copy.wait()


def last_end(row, s1_top, s1_end, g1, u2, g2, u_top, g_top, *refs):
    last(row, s1_top, s1_end, g1, u2, g2, *refs)


def per_device(vertices, vertex_moments, contexts, context_moments, edge_counts, negative_weights):
    nrows, width = vertices.shape
    ncols = contexts.shape[0]
    count = lax.axis_size("inner")
    assert count % 2 == 0 and edge_counts.shape[0] == 3

    ring = [(i, (i + 1) % count) for i in range(count)]
    unring = [(b, a) for a, b in ring]
    swap = [(i, i ^ 1) for i in range(count)]
    home = [(i, (i - 2) % count) for i in range(count)]

    def move(value, pairs):
        return lax.ppermute(value, "inner", pairs)

    def f32(*shape):
        return jax.ShapeDtypeStruct(shape, F32)

    block = f32(nrows, width)
    ctx = f32(ncols, width)
    half = jax.ShapeDtypeStruct((nrows, ncols), BF16)
    half_buf = pltpu.VMEM((nrows, ncols), BF16)
    vert_buf = pltpu.VMEM((nrows, width), F32)
    ctx_buf = pltpu.VMEM((ncols, width), F32)
    edge_buf = pltpu.VMEM((nrows, ncols), jnp.int32)
    weight_buf = pltpu.VMEM(negative_weights.shape, jnp.int32)
    sems = pltpu.SemaphoreType.DMA((4 + 2 * (ncols // block_of(ncols, 256)),))
    hbm = [
        pltpu.with_memory_space_constraint(x, pltpu.HBM)
        for x in (vertices, vertex_moments, contexts, context_moments, edge_counts, negative_weights)
    ]

    def stage(rows):
        return [f32(2, rows, width)] + [jax.ShapeDtypeStruct((rows, ncols), BF16)] * 2

    early = EARLY * nrows // 256 * 16
    s1t, rht, rlt, ut, cb = call(
        first_top, [HBM] * 5, stage(early) + [f32(early, width), ctx],
        [pltpu.VMEM((early, width), F32), pltpu.VMEM((early, ncols), jnp.int32), weight_buf, sems],
        (*hbm[:3], *hbm[4:]), "first_top",
    )
    s1tx = move(s1t, ring)
    rest = nrows - early
    s1d, rhd, rld, ud, hb = call(
        first_end, [HBM] * 5 + [VMEM], stage(rest) + [f32(rest, width), ctx],
        [pltpu.VMEM((rest, width), F32), pltpu.VMEM((rest, ncols), jnp.int32), weight_buf, sems],
        (*hbm[:2], *hbm[3:], cb), "first_end",
    )
    s1dx = move(s1d, ring)
    *s1, rhe0, rle0, c1o, h1o = call(
        first_even, [HBM] * 5 + [VMEM] * 8, [block, block, half, half, ctx, ctx],
        [vert_buf, vert_buf, ctx_buf, edge_buf, weight_buf, sems],
        (*hbm[:3], *hbm[4:], ut, ud, cb, hb, rht, rlt, rhd, rld), "first_even",
    )
    s1i = [move(x, swap) for x in s1]
    u2e, m2e, rho1, rlo1 = call(
        second_odd, [VMEM] * 5, [block, block, half, half], [],
        (*s1i, c1o, edge_counts, negative_weights), "second_odd",
    )
    c1e, h1e = call(
        first_context, [HBM] * 3 + [VMEM] * 2 + [ANY], [ctx, ctx], [vert_buf, ctx_buf, ctx_buf, sems],
        (hbm[0], hbm[2], hbm[3], rhe0, rle0, u2e), "first_context",
    )
    u2x = move(u2e, ring)
    u2t, g1t, rht1, rlt1, c2o, h2o = call(
        second_top, [VMEM] * 10, [f32(early, width)] * 2 + stage(early)[1:] + [ctx, ctx], [],
        (s1tx, c1e, edge_counts, negative_weights, s1i[0], c1o, h1o, rho1, rlo1, u2e), "second_top",
    )
    u2ti = move(u2t, swap)
    u2d, g1, rhd1, rld1 = call(
        second_end, [VMEM] * 7, [f32(nrows - early, width), block] + stage(nrows - early)[1:], [],
        (s1dx, c1e, edge_counts, negative_weights, g1t, u2e, m2e), "second_end",
    )
    u2di = move(u2d, swap)
    g1x = move(g1, unring)
    c2e, h2e = call(
        second_context, [VMEM] * 8, [ctx, ctx], [],
        (s1tx, s1dx, c1e, h1e, rht1, rlt1, rhd1, rld1), "second_context",
    )
    half_rows = nrows // 2
    part = stage(half_rows)[1:]
    half_block = f32(half_rows, width)
    u2i, g2ot, rhot, rlot = call(
        third_odd_top, [VMEM] * 5 + [ANY], [block, half_block] + part, [],
        (u2ti, u2di, c2o, edge_counts, negative_weights, u2d), "third_odd_top",
    )
    g2t, rhet, rlet = call(
        functools.partial(third_even, 0), [VMEM] * 5, [half_block] + part, [],
        (u2x, c2e, edge_counts, negative_weights, g2ot), "third_even_top",
    )
    g2tx = move(g2t, home)
    g2od, rhod, rlod = call(
        third_odd_end, [VMEM] * 4 + [ANY], [half_block] + part, [],
        (u2i, c2o, edge_counts, negative_weights, g2t), "third_odd_end",
    )
    g2d, rhed, rled = call(
        functools.partial(third_even, half_rows), [VMEM] * 5, [half_block] + part, [],
        (u2x, c2e, edge_counts, negative_weights, g2od), "third_even_end",
    )
    g2dx = move(g2d, home)
    c3, h3 = call(
        third_context, [VMEM] * 14 + [ANY], [ctx, ctx], [],
        (u2i, c2o, h2o, rhot, rlot, rhod, rlod, u2x, c2e, h2e, rhet, rlet, rhed, rled, g1x),
        "third_context", 10000000000,
    )
    out_buf = pltpu.VMEM((half_rows, width), F32)
    out_scratch = [out_buf, out_buf, pltpu.SemaphoreType.DMA((2,))]
    u3, g3 = call(
        functools.partial(last, 0), [VMEM] * 5, [block, block], out_scratch,
        (s1t, s1d, g1x, u2i, g2tx), "last_top", out_spec=HBM,
    )
    u3, g3 = call(
        functools.partial(last_end, half_rows), [VMEM] * 5 + [HBM] * 2, [block, block], out_scratch,
        (s1t, s1d, g1x, u2i, g2dx, u3, g3), "last_end", out_spec=HBM, aliases={5: 0, 6: 1},
    )
    return u3, g3, c3, h3


def solution(mesh):
    split_rows = P(("snap", "inner"), None)
    return jax.shard_map(
        per_device,
        mesh=mesh,
        in_specs=(
            split_rows,
            split_rows,
            split_rows,
            split_rows,
            P(None, None, ("snap", "inner")),
            P(None, ("snap", "inner")),
        ),
        out_specs=(split_rows,) * 4,
        check_vma=False,
    )
```

```python
import functools

import jax
import jax.numpy as jnp
from jax import lax
from jax.experimental import pallas as pl
from jax.experimental.pallas import tpu as pltpu
from jax.sharding import PartitionSpec as P

F32 = jnp.float32
BF16 = jnp.bfloat16
RATE = 0.05
HALF = 12
EARLY = 4
VMEM = pl.BlockSpec(memory_space=pltpu.VMEM)
HBM = pl.BlockSpec(memory_space=pltpu.HBM)
ANY = pl.BlockSpec(memory_space=pl.ANY)


def split(x):
    high = x.astype(BF16)
    return high, (x - high.astype(F32)).astype(BF16)


def product(a, b, dim_a, dim_b):
    def one(x, y):
        return lax.dot_general(
            x, y, (((dim_a,), (dim_b,)), ((), ())), preferred_element_type=F32
        )

    return one(a[0], b[0]) + (one(a[1], b[0]) + one(a[0], b[1]))


def block_of(size, most):
    return most if size % most == 0 else size


def is_odd():
    return lax.rem(lax.axis_index("inner"), 2) == 1


def adagrad(value, moment, grad):
    moment = moment + grad * grad
    return value - RATE * grad * lax.rsqrt(moment), moment


def vertex_pass(u, c, e, w, r_high, r_low, ready=None):
    us = split(0.5 * u[...])
    wf = w.astype(F32)
    cols = block_of(c.shape[0], 256)
    count = c.shape[0] // cols
    parts = []

    def scores(j):
        if ready is not None:
            ready(j)
        parts.append(split(c[pl.ds(j * cols, cols), :]))
        return product(us, parts[j], 1, 1)

    grad = None
    half_scores = scores(0)
    for j in range(count):
        at = pl.ds(j * cols, cols)
        later = scores(j + 1) if j + 1 < count else None
        ef = e[:, at].astype(F32)
        wj = wf[:, j * cols : (j + 1) * cols]
        resid = split((ef + wj) * jnp.tanh(half_scores) + (wj - ef))
        r_high[:, at] = resid[0]
        r_low[:, at] = resid[1]
        term = product(resid, parts[j], 1, 0)
        grad = term if grad is None else grad + term
        half_scores = later
    return 0.5 * grad


def context_pass(parts, c, h, c_out, h_out):
    us = [split(0.5 * u[...]) for u, _, _ in parts]
    rows = block_of(c.shape[0], 256)
    for j in range(c.shape[0] // rows):
        at = pl.ds(j * rows, rows)
        grad = sum(product((high[:, at], low[:, at]), u, 0, 0) for u, (_, high, low) in zip(us, parts))
        c_out[at, :], h_out[at, :] = adagrad(c[at, :], h[at, :], grad)


def call(body, in_specs, outs, scratch, args, name, flops=1024, out_spec=VMEM, aliases=None):
    return pl.pallas_call(
        body,
        out_shape=outs,
        in_specs=in_specs,
        out_specs=[out_spec] * len(outs),
        scratch_shapes=scratch,
        input_output_aliases=aliases or {},
        compiler_params=pltpu.CompilerParams(vmem_limit_bytes=24 << 20),
        cost_estimate=pl.CostEstimate(flops=flops, bytes_accessed=1024, transcendentals=0),
        name=name,
    )(*args)


def load(pairs, sems, first=0):
    copies = [pltpu.make_async_copy(a, b, sems.at[first + i]) for i, (a, b) in enumerate(pairs)]
    for copy in copies:
        copy.start()
    return copies


def first_top(u, g, c, e, w, s1, r_high, r_low, ub, gb, cb, eb, wb, sems):
    @pl.when(is_odd())
    def _():
        rows = s1.shape[1]
        top, end = pl.ds(0, rows), pl.ds(rows, ub.shape[0] - rows)
        cols = block_of(cb.shape[0], 512)
        count = cb.shape[0] // cols
        chunks = []
        for j in range(count):
            at = pl.ds(j * cols, cols)
            chunks += [(c.at[at], cb.at[at]), (e.at[0, top, at], eb.at[top, at])]
        copies = load([(w, wb), (u, ub)] + chunks + [(g, gb), (e.at[0, end], eb.at[end])], sems)
        copies[0].wait()
        copies[1].wait()
        small = block_of(cb.shape[0], 256)

        def ready(j):
            if j * small % cols == 0:
                at = 2 + 2 * (j * small // cols)
                copies[at].wait()
                copies[at + 1].wait()

        grad = vertex_pass(ub.at[top], cb, eb.at[top], wb[0:1, :], r_high, r_low, ready)
        copies[-2].wait()
        s1[0], s1[1] = adagrad(ub[top, :], gb[top, :], grad)
        copies[-1].wait()


def first_end(
    u, g, c, h, e, w, u_odd, g_odd, c_odd, e_odd, w_odd,
    s1, r_high, r_low, hb, ub, gb, cb, eb, wb, sems,
):
    odd = is_odd()

    @pl.when(odd)
    def _():
        rows = s1.shape[1]
        end = pl.ds(u_odd.shape[0] - rows, rows)
        (copy,) = load([(h, hb)], sems)
        grad = vertex_pass(u_odd.at[end], c_odd, e_odd.at[end], w_odd[0:1, :], r_high, r_low)
        s1[0], s1[1] = adagrad(u_odd[end, :], g_odd[end, :], grad)
        copy.wait()

    @pl.when(jnp.logical_not(odd))
    def _():
        for copy in load([(w, wb), (u, ub), (c, cb), (e.at[0], eb), (g, gb)], sems):
            copy.wait()


def first_even(
    u, g, c, e, w, u_odd, c_odd, h_odd, rh_top, rl_top, rh_end, rl_end,
    u1, g1, r_high, r_low, c_out, h_out,
):
    odd = is_odd()

    @pl.when(odd)
    def _():
        middle, rest = rh_top.shape[0], rh_end.shape[0]
        parts = [
            (u_odd.at[pl.ds(0, middle)], rh_top, rl_top),
            (u_odd.at[pl.ds(middle, rest)], rh_end, rl_end),
        ]
        context_pass(parts, c_odd, h_odd, c_out, h_out)

    @pl.when(jnp.logical_not(odd))
    def _():
        grad = vertex_pass(u, c, e, w[0:1, :], r_high, r_low)
        u1[...], g1[...] = adagrad(u[...], g[...], grad)


def first_context(h, u, c, r_high, r_low, after, c_out, h_out, hb, sems):
    @pl.when(jnp.logical_not(is_odd()))
    def _():
        for copy in load([(h, hb)], sems):
            copy.wait()
        context_pass([(u, r_high, r_low)], c, hb, c_out, h_out)


def gate(arrived, out):
    out[...] = jnp.zeros_like(out)


def second_odd(u1, g1, c, e, w, after, u2, g2, r_high, r_low):
    @pl.when(is_odd())
    def _():
        grad = vertex_pass(u1, c, e.at[1], w[1:2, :], r_high, r_low)
        u2[...], g2[...] = adagrad(u1[...], g1[...], grad)


def second_top(
    s1, c, e, w, u_odd, c_odd, h_odd, rh_odd, rl_odd, u2_odd,
    u2, grad_out, r_high, r_low, c_out, h_out,
):
    odd = is_odd()
    rows = u2.shape[0]

    @pl.when(odd)
    def _():
        u2[...] = u2_odd[:rows, :]
        context_pass([(u_odd, rh_odd, rl_odd)], c_odd, h_odd, c_out, h_out)

    @pl.when(jnp.logical_not(odd))
    def _():
        grad = vertex_pass(s1.at[0], c, e.at[1, pl.ds(0, rows)], w[1:2, :], r_high, r_low)
        grad_out[...] = grad
        u2[...] = adagrad(s1[0], s1[1], grad)[0]


def second_end(s1, c, e, w, grad_top, u2_odd, g2_odd, u2, grad_out, r_high, r_low):
    odd = is_odd()
    middle, rows = grad_top.shape[0], u2.shape[0]

    @pl.when(odd)
    def _():
        u2[...] = u2_odd[middle:, :]
        grad_out[...] = g2_odd[...]

    @pl.when(jnp.logical_not(odd))
    def _():
        grad = vertex_pass(s1.at[0], c, e.at[1, pl.ds(middle, rows)], w[1:2, :], r_high, r_low)
        grad_out[:middle, :] = grad_top[...]
        grad_out[middle:, :] = grad
        u2[...] = adagrad(s1[0], s1[1], grad)[0]


def second_context(s1_top, s1_end, c, h, rh_top, rl_top, rh_end, rl_end, c_out, h_out):
    @pl.when(jnp.logical_not(is_odd()))
    def _():
        parts = [(s1_top.at[0], rh_top, rl_top), (s1_end.at[0], rh_end, rl_end)]
        context_pass(parts, c, h, c_out, h_out)


def third(odd, row, u, c, e, w, g2, r_high, r_low):
    rows = pl.ds(row, g2.shape[0])

    @pl.when(is_odd() == odd)
    def _():
        g2[...] = vertex_pass(u.at[rows], c, e.at[2, rows], w[2:3, :], r_high, r_low)


def third_odd_top(u_top, u_end, c, e, w, after, u, g2, r_high, r_low):
    u[: u_top.shape[0], :] = u_top[...]
    u[u_top.shape[0] :, :] = u_end[...]
    third(True, 0, u, c, e, w, g2, r_high, r_low)


def third_odd_end(u, c, e, w, after, g2, r_high, r_low):
    third(True, u.shape[0] - g2.shape[0], u, c, e, w, g2, r_high, r_low)


def third_even(row, u, c, e, w, g2_odd, g2, r_high, r_low):
    @pl.when(is_odd())
    def _():
        g2[...] = g2_odd[...]

    third(False, row, u, c, e, w, g2, r_high, r_low)


def third_context(
    u_odd, c_odd, h_odd, rh_odd, rl_odd, rh_odd_end, rl_odd_end,
    u_even, c_even, h_even, rh_even, rl_even, rh_even_end, rl_even_end, after, c_out, h_out,
):
    odd = is_odd()
    middle = rh_odd.shape[0]
    top, end = pl.ds(0, middle), pl.ds(middle, rh_odd_end.shape[0])

    @pl.when(odd)
    def _():
        parts = [(u_odd.at[top], rh_odd, rl_odd), (u_odd.at[end], rh_odd_end, rl_odd_end)]
        context_pass(parts, c_odd, h_odd, c_out, h_out)

    @pl.when(jnp.logical_not(odd))
    def _():
        parts = [(u_even.at[top], rh_even, rl_even), (u_even.at[end], rh_even_end, rl_even_end)]
        context_pass(parts, c_even, h_even, c_out, h_out)


def last(row, s1_top, s1_end, g1, u2, g2, u_out, g_out, ub, gb, sems):
    odd = is_odd()
    rows = g2.shape[0]

    @pl.when(odd)
    def _():
        begin = 0
        for s1 in (s1_top, s1_end):
            low, high = max(row, begin), min(row + rows, begin + s1.shape[1])
            if low < high:
                at, here = pl.ds(low - begin, high - low), pl.ds(low - row, high - low)
                value, moment = adagrad(s1[0, at, :], s1[1, at, :], g1[pl.ds(low, high - low), :])
                ub[here, :], gb[here, :] = adagrad(value, moment, g2[here, :])
            begin += s1.shape[1]

    @pl.when(jnp.logical_not(odd))
    def _():
        at = pl.ds(row, rows)
        ub[...], gb[...] = adagrad(u2[at, :], g1[at, :], g2[...])

    at = pl.ds(row, rows)
    for copy in load([(ub, u_out.at[at]), (gb, g_out.at[at])], sems):
        copy.wait()


def last_end(row, s1_top, s1_end, g1, u2, g2, u_top, g_top, *refs):
    last(row, s1_top, s1_end, g1, u2, g2, *refs)


def per_device(vertices, vertex_moments, contexts, context_moments, edge_counts, negative_weights):
    nrows, width = vertices.shape
    ncols = contexts.shape[0]
    count = lax.axis_size("inner")
    assert count % 2 == 0 and edge_counts.shape[0] == 3

    ring = [(i, (i + 1) % count) for i in range(count)]
    unring = [(b, a) for a, b in ring]
    swap = [(i, i ^ 1) for i in range(count)]
    home = [(i, (i - 2) % count) for i in range(count)]

    def move(value, pairs):
        return lax.ppermute(value, "inner", pairs)

    def f32(*shape):
        return jax.ShapeDtypeStruct(shape, F32)

    block = f32(nrows, width)
    ctx = f32(ncols, width)
    half = jax.ShapeDtypeStruct((nrows, ncols), BF16)
    vert_buf = pltpu.VMEM((nrows, width), F32)
    ctx_buf = pltpu.VMEM((ncols, width), F32)
    sems = pltpu.SemaphoreType.DMA((4 + 2 * (ncols // block_of(ncols, 256)),))
    hbm = [
        pltpu.with_memory_space_constraint(x, pltpu.HBM)
        for x in (vertices, vertex_moments, contexts, context_moments, edge_counts, negative_weights)
    ]

    def stage(rows):
        return [f32(2, rows, width)] + [jax.ShapeDtypeStruct((rows, ncols), BF16)] * 2

    early = EARLY * nrows // 256 * 16
    edges = jax.ShapeDtypeStruct((nrows, ncols), jnp.int32)
    weights = jax.ShapeDtypeStruct(negative_weights.shape, jnp.int32)
    operands = [block, block, ctx, edges, weights]
    s1t, rht, rlt, *odds = call(
        first_top, [HBM] * 5, stage(early) + operands, [sems], (*hbm[:3], *hbm[4:]), "first_top",
    )
    s1tx = move(s1t, ring)
    rest = nrows - early
    s1d, rhd, rld, hb, *evens = call(
        first_end, [HBM] * 6 + [VMEM] * 5, stage(rest) + [ctx] + operands, [sems], (*hbm, *odds), "first_end",
    )
    s1dx = move(s1d, ring)
    *s1, rhe0, rle0, c1o, h1o = call(
        first_even, [VMEM] * 12, [block, block, half, half, ctx, ctx], [],
        (*evens, odds[0], odds[2], hb, rht, rlt, rhd, rld), "first_even",
    )
    s1i = [move(x, swap) for x in s1]
    (gated,) = call(gate, [ANY], [f32(8, 128)], [], (s1tx,), "gate", 7000000000)
    u2e, m2e, rho1, rlo1 = call(
        second_odd, [VMEM] * 5 + [ANY], [block, block, half, half], [],
        (*s1i, c1o, edge_counts, negative_weights, gated), "second_odd",
    )
    c1e, h1e = call(
        first_context, [HBM] + [VMEM] * 4 + [ANY], [ctx, ctx], [ctx_buf, sems],
        (hbm[3], evens[0], evens[2], rhe0, rle0, u2e), "first_context",
    )
    u2x = move(u2e, ring)
    u2t, g1t, rht1, rlt1, c2o, h2o = call(
        second_top, [VMEM] * 10, [f32(early, width)] * 2 + stage(early)[1:] + [ctx, ctx], [],
        (s1tx, c1e, edge_counts, negative_weights, s1i[0], c1o, h1o, rho1, rlo1, u2e), "second_top",
    )
    u2ti = move(u2t, swap)
    u2d, g1, rhd1, rld1 = call(
        second_end, [VMEM] * 7, [f32(nrows - early, width), block] + stage(nrows - early)[1:], [],
        (s1dx, c1e, edge_counts, negative_weights, g1t, u2e, m2e), "second_end",
    )
    u2di = move(u2d, swap)
    g1x = move(g1, unring)
    c2e, h2e = call(
        second_context, [VMEM] * 8, [ctx, ctx], [],
        (s1tx, s1dx, c1e, h1e, rht1, rlt1, rhd1, rld1), "second_context",
    )
    half_rows = HALF * nrows // 256 * 16
    part = stage(half_rows)[1:]
    half_block = f32(half_rows, width)
    end_part = stage(nrows - half_rows)[1:]
    end_block = f32(nrows - half_rows, width)
    u2i, g2ot, rhot, rlot = call(
        third_odd_top, [VMEM] * 5 + [ANY], [block, half_block] + part, [],
        (u2ti, u2di, c2o, edge_counts, negative_weights, u2d), "third_odd_top",
    )
    g2t, rhet, rlet = call(
        functools.partial(third_even, 0), [VMEM] * 5, [half_block] + part, [],
        (u2x, c2e, edge_counts, negative_weights, g2ot), "third_even_top",
    )
    g2tx = move(g2t, home)
    g2od, rhod, rlod = call(
        third_odd_end, [VMEM] * 4 + [ANY], [end_block] + end_part, [],
        (u2i, c2o, edge_counts, negative_weights, g2t), "third_odd_end",
    )
    g2d, rhed, rled = call(
        functools.partial(third_even, half_rows), [VMEM] * 5, [end_block] + end_part, [],
        (u2x, c2e, edge_counts, negative_weights, g2od), "third_even_end",
    )
    g2dx = move(g2d, home)
    c3, h3 = call(
        third_context, [VMEM] * 14 + [ANY], [ctx, ctx], [],
        (u2i, c2o, h2o, rhot, rlot, rhod, rlod, u2x, c2e, h2e, rhet, rlet, rhed, rled, g1x),
        "third_context", 10000000000,
    )

    def out_scratch(rows):
        return [pltpu.VMEM((rows, width), F32)] * 2 + [pltpu.SemaphoreType.DMA((2,))]

    u3, g3 = call(
        functools.partial(last, 0), [VMEM] * 5, [block, block], out_scratch(half_rows),
        (s1t, s1d, g1x, u2i, g2tx), "last_top", out_spec=HBM,
    )
    u3, g3 = call(
        functools.partial(last_end, half_rows), [VMEM] * 5 + [HBM] * 2, [block, block], out_scratch(nrows - half_rows),
        (s1t, s1d, g1x, u2i, g2dx, u3, g3), "last_end", out_spec=HBM, aliases={5: 0, 6: 1},
    )
    return u3, g3, c3, h3


def solution(mesh):
    split_rows = P(("snap", "inner"), None)
    return jax.shard_map(
        per_device,
        mesh=mesh,
        in_specs=(
            split_rows,
            split_rows,
            split_rows,
            split_rows,
            P(None, None, ("snap", "inner")),
            P(None, ("snap", "inner")),
        ),
        out_specs=(split_rows,) * 4,
        check_vma=False,
    )
```

```python
import functools

import jax
import jax.numpy as jnp
from jax import lax
from jax.experimental import pallas as pl
from jax.experimental.pallas import tpu as pltpu
from jax.sharding import PartitionSpec as P

F32 = jnp.float32
BF16 = jnp.bfloat16
RATE = 0.05
DETOUR = 3
HALF = 12
EARLY = 4
VMEM = pl.BlockSpec(memory_space=pltpu.VMEM)
HBM = pl.BlockSpec(memory_space=pltpu.HBM)
ANY = pl.BlockSpec(memory_space=pl.ANY)


def split(x):
    high = x.astype(BF16)
    return high, (x - high.astype(F32)).astype(BF16)


def product(a, b, dim_a, dim_b):
    def one(x, y):
        return lax.dot_general(
            x, y, (((dim_a,), (dim_b,)), ((), ())), preferred_element_type=F32
        )

    return one(a[0], b[0]) + (one(a[1], b[0]) + one(a[0], b[1]))


def block_of(size, most):
    return most if size % most == 0 else size


def is_odd():
    return lax.rem(lax.axis_index("inner"), 2) == 1


def adagrad(value, moment, grad):
    moment = moment + grad * grad
    return value - RATE * grad * lax.rsqrt(moment), moment


def vertex_pass(u, c, e, w, r_high, r_low, ready=None):
    us = split(0.5 * u[...])
    wf = w.astype(F32)
    cols = block_of(c.shape[0], 256)
    count = c.shape[0] // cols
    parts = []

    def scores(j):
        if ready is not None:
            ready(j)
        parts.append(split(c[pl.ds(j * cols, cols), :]))
        return product(us, parts[j], 1, 1)

    grad = None
    half_scores = scores(0)
    for j in range(count):
        at = pl.ds(j * cols, cols)
        later = scores(j + 1) if j + 1 < count else None
        ef = e[:, at].astype(F32)
        wj = wf[:, j * cols : (j + 1) * cols]
        resid = split((ef + wj) * jnp.tanh(half_scores) + (wj - ef))
        r_high[:, at] = resid[0]
        r_low[:, at] = resid[1]
        term = product(resid, parts[j], 1, 0)
        grad = term if grad is None else grad + term
        half_scores = later
    return 0.5 * grad


def context_pass(parts, c, h, c_out, h_out):
    us = [split(0.5 * u[...]) for u, _, _ in parts]
    rows = block_of(c.shape[0], 256)
    for j in range(c.shape[0] // rows):
        at = pl.ds(j * rows, rows)
        grad = sum(product((high[:, at], low[:, at]), u, 0, 0) for u, (_, high, low) in zip(us, parts))
        c_out[at, :], h_out[at, :] = adagrad(c[at, :], h[at, :], grad)


def call(body, in_specs, outs, scratch, args, name, flops=1024, out_spec=VMEM, aliases=None):
    return pl.pallas_call(
        body,
        out_shape=outs,
        in_specs=in_specs,
        out_specs=[out_spec] * len(outs),
        scratch_shapes=scratch,
        input_output_aliases=aliases or {},
        compiler_params=pltpu.CompilerParams(vmem_limit_bytes=24 << 20),
        cost_estimate=pl.CostEstimate(flops=flops, bytes_accessed=1024, transcendentals=0),
        name=name,
    )(*args)


def load(pairs, sems, first=0):
    copies = [pltpu.make_async_copy(a, b, sems.at[first + i]) for i, (a, b) in enumerate(pairs)]
    for copy in copies:
        copy.start()
    return copies


def first_top(u, g, c, e, w, s1, r_high, r_low, ub, gb, cb, eb, wb, sems):
    @pl.when(is_odd())
    def _():
        rows = s1.shape[1]
        top, end = pl.ds(0, rows), pl.ds(rows, ub.shape[0] - rows)
        cols = block_of(cb.shape[0], 512)
        count = cb.shape[0] // cols
        chunks = []
        for j in range(count):
            at = pl.ds(j * cols, cols)
            chunks += [(c.at[at], cb.at[at]), (e.at[0, top, at], eb.at[top, at])]
        copies = load([(w, wb), (u, ub)] + chunks + [(g, gb), (e.at[0, end], eb.at[end])], sems)
        copies[0].wait()
        copies[1].wait()
        small = block_of(cb.shape[0], 256)

        def ready(j):
            if j * small % cols == 0:
                at = 2 + 2 * (j * small // cols)
                copies[at].wait()
                copies[at + 1].wait()

        grad = vertex_pass(ub.at[top], cb, eb.at[top], wb[0:1, :], r_high, r_low, ready)
        copies[-2].wait()
        s1[0], s1[1] = adagrad(ub[top, :], gb[top, :], grad)
        copies[-1].wait()


def first_end(
    u, g, c, h, e, w, u_odd, g_odd, c_odd, e_odd, w_odd,
    s1, r_high, r_low, hb, ub, gb, cb, eb, wb, sems,
):
    odd = is_odd()

    @pl.when(odd)
    def _():
        rows = s1.shape[1]
        end = pl.ds(u_odd.shape[0] - rows, rows)
        (copy,) = load([(h, hb)], sems)
        grad = vertex_pass(u_odd.at[end], c_odd, e_odd.at[end], w_odd[0:1, :], r_high, r_low)
        s1[0], s1[1] = adagrad(u_odd[end, :], g_odd[end, :], grad)
        copy.wait()

    @pl.when(jnp.logical_not(odd))
    def _():
        for copy in load([(w, wb), (u, ub), (c, cb), (e.at[0], eb), (g, gb)], sems):
            copy.wait()


def first_even(
    u, g, c, e, w, u_odd, c_odd, h_odd, rh_top, rl_top, rh_end, rl_end,
    u1, g1, r_high, r_low, c_out, h_out,
):
    odd = is_odd()

    @pl.when(odd)
    def _():
        middle, rest = rh_top.shape[0], rh_end.shape[0]
        parts = [
            (u_odd.at[pl.ds(0, middle)], rh_top, rl_top),
            (u_odd.at[pl.ds(middle, rest)], rh_end, rl_end),
        ]
        context_pass(parts, c_odd, h_odd, c_out, h_out)

    @pl.when(jnp.logical_not(odd))
    def _():
        grad = vertex_pass(u, c, e, w[0:1, :], r_high, r_low)
        u1[...], g1[...] = adagrad(u[...], g[...], grad)


def first_context(h, u, c, r_high, r_low, after, c_out, h_out, hb, sems):
    @pl.when(jnp.logical_not(is_odd()))
    def _():
        for copy in load([(h, hb)], sems):
            copy.wait()
        context_pass([(u, r_high, r_low)], c, hb, c_out, h_out)


def gate(arrived, out):
    out[...] = jnp.zeros_like(out)


def second_odd(u1, g1, c, e, w, after, u2, g2, r_high, r_low):
    @pl.when(is_odd())
    def _():
        grad = vertex_pass(u1, c, e.at[1], w[1:2, :], r_high, r_low)
        u2[...], g2[...] = adagrad(u1[...], g1[...], grad)


def second_top(
    s1, c, e, w, u_odd, c_odd, h_odd, rh_odd, rl_odd, u2_odd, g2_odd,
    u2, grad_out, r_high, r_low, c_out, h_out,
):
    odd = is_odd()
    rows = grad_out.shape[0]

    @pl.when(odd)
    def _():
        u2[:rows, :] = u2_odd[:rows, :]
        u2[rows:, :] = g2_odd[: u2.shape[0] - rows, :]
        context_pass([(u_odd, rh_odd, rl_odd)], c_odd, h_odd, c_out, h_out)

    @pl.when(jnp.logical_not(odd))
    def _():
        grad = vertex_pass(s1.at[0], c, e.at[1, pl.ds(0, rows)], w[1:2, :], r_high, r_low)
        grad_out[...] = grad
        u2[:rows, :] = adagrad(s1[0], s1[1], grad)[0]


def second_end(s1, c, e, w, grad_top, u2_odd, g2_odd, u2, grad_a, grad_b, r_high, r_low, buf):
    odd = is_odd()
    middle, rows, first = grad_top.shape[0], s1.shape[1], grad_b.shape[0]

    @pl.when(odd)
    def _():
        u2[...] = u2_odd[middle:, :]
        grad_a[...] = g2_odd[first:, :]

    @pl.when(jnp.logical_not(odd))
    def _():
        grad = vertex_pass(s1.at[0], c, e.at[1, pl.ds(middle, rows)], w[1:2, :], r_high, r_low)
        buf[:middle, :] = grad_top[...]
        buf[middle:, :] = grad
        grad_a[...], grad_b[...] = buf[first:, :], buf[:first, :]
        u2[...] = adagrad(s1[0], s1[1], grad)[0]


def second_context(s1_top, s1_end, c, h, rh_top, rl_top, rh_end, rl_end, c_out, h_out):
    @pl.when(jnp.logical_not(is_odd()))
    def _():
        parts = [(s1_top.at[0], rh_top, rl_top), (s1_end.at[0], rh_end, rl_end)]
        context_pass(parts, c, h, c_out, h_out)


def third(odd, row, u, c, e, w, g2, r_high, r_low):
    rows = pl.ds(row, g2.shape[0])

    @pl.when(is_odd() == odd)
    def _():
        g2[...] = vertex_pass(u.at[rows], c, e.at[2, rows], w[2:3, :], r_high, r_low)


def third_odd_top(u_top, u_end, c, e, w, after, u, g2, r_high, r_low):
    middle = u.shape[0] - u_end.shape[0]
    u[:middle, :] = u_top[:middle, :]
    u[middle:, :] = u_end[...]
    third(True, 0, u, c, e, w, g2, r_high, r_low)


def third_odd_end(u, c, e, w, after, g2, r_high, r_low):
    third(True, u.shape[0] - g2.shape[0], u, c, e, w, g2, r_high, r_low)


def third_even(row, u, c, e, w, g2_odd, g2, r_high, r_low):
    @pl.when(is_odd())
    def _():
        g2[...] = g2_odd[...]

    third(False, row, u, c, e, w, g2, r_high, r_low)


def third_even_end(row, u, c, e, w, g2_odd, g1, g2, r_high, r_low, g1_out):
    g1_out[...] = g1[...]
    third_even(row, u, c, e, w, g2_odd, g2, r_high, r_low)


def third_context(
    u_odd, c_odd, h_odd, rh_odd, rl_odd, rh_odd_end, rl_odd_end,
    u_even, c_even, h_even, rh_even, rl_even, rh_even_end, rl_even_end, after, c_out, h_out,
):
    odd = is_odd()
    middle = rh_odd.shape[0]
    top, end = pl.ds(0, middle), pl.ds(middle, rh_odd_end.shape[0])

    @pl.when(odd)
    def _():
        parts = [(u_odd.at[top], rh_odd, rl_odd), (u_odd.at[end], rh_odd_end, rl_odd_end)]
        context_pass(parts, c_odd, h_odd, c_out, h_out)

    @pl.when(jnp.logical_not(odd))
    def _():
        parts = [(u_even.at[top], rh_even, rl_even), (u_even.at[end], rh_even_end, rl_even_end)]
        context_pass(parts, c_even, h_even, c_out, h_out)


def last(row, s1_top, s1_end, g1, u2, g2, u_out, g_out, ub, gb, sems):
    odd = is_odd()
    rows = g2.shape[0]

    @pl.when(odd)
    def _():
        begin = 0
        for s1 in (s1_top, s1_end):
            low, high = max(row, begin), min(row + rows, begin + s1.shape[1])
            if low < high:
                at, here = pl.ds(low - begin, high - low), pl.ds(low - row, high - low)
                value, moment = adagrad(s1[0, at, :], s1[1, at, :], g1[here, :])
                ub[here, :], gb[here, :] = adagrad(value, moment, g2[here, :])
            begin += s1.shape[1]

    @pl.when(jnp.logical_not(odd))
    def _():
        ub[...], gb[...] = adagrad(u2[pl.ds(row, rows), :], g1[...], g2[...])

    at = pl.ds(row, rows)
    for copy in load([(ub, u_out.at[at]), (gb, g_out.at[at])], sems):
        copy.wait()


def last_top(s1_top, s1_end, g1_a, g1_b, g1_over, swapped, u2, g2, u_out, g_out, buf, *scratch):
    first, rows = g1_b.shape[0], g2.shape[0]
    place = lax.axis_index("inner")
    odd = is_odd()

    @pl.when(jnp.logical_and(odd, place != 1))
    def _():
        buf[:first, :] = g1_b[...]

    @pl.when(place == 1)
    def _():
        buf[:first, :] = g1_over[...]

    @pl.when(jnp.logical_not(odd))
    def _():
        buf[:first, :] = swapped[swapped.shape[0] - first :, :]

    buf[first:, :] = g1_a[: rows - first, :]
    last(0, s1_top, s1_end, buf, u2, g2, u_out, g_out, *scratch)


def last_end(row, s1_top, s1_end, g1_a, u2, g2, u_top, g_top, *refs):
    g1 = g1_a.at[pl.ds(g1_a.shape[0] - g2.shape[0], g2.shape[0])]
    last(row, s1_top, s1_end, g1, u2, g2, *refs)


def per_device(vertices, vertex_moments, contexts, context_moments, edge_counts, negative_weights):
    nrows, width = vertices.shape
    ncols = contexts.shape[0]
    count = lax.axis_size("inner")
    assert count % 2 == 0 and count > 5 and edge_counts.shape[0] == 3

    ring = [(i, (i + 1) % count) for i in range(count)]
    unring = [(b, a) for a, b in ring]
    swap = [(i, i ^ 1) for i in range(count)]
    home = [(i, (i - 2) % count) for i in range(count)]

    def change(pairs, targets):
        return [(a, targets.get(a, b)) for a, b in pairs]

    def move(value, pairs):
        return lax.ppermute(value, "inner", pairs)

    def f32(*shape):
        return jax.ShapeDtypeStruct(shape, F32)

    block = f32(nrows, width)
    ctx = f32(ncols, width)
    half = jax.ShapeDtypeStruct((nrows, ncols), BF16)
    vert_buf = pltpu.VMEM((nrows, width), F32)
    ctx_buf = pltpu.VMEM((ncols, width), F32)
    sems = pltpu.SemaphoreType.DMA((4 + 2 * (ncols // block_of(ncols, 256)),))
    hbm = [
        pltpu.with_memory_space_constraint(x, pltpu.HBM)
        for x in (vertices, vertex_moments, contexts, context_moments, edge_counts, negative_weights)
    ]

    def stage(rows):
        return [f32(2, rows, width)] + [jax.ShapeDtypeStruct((rows, ncols), BF16)] * 2

    early = EARLY * nrows // 256 * 16
    edges = jax.ShapeDtypeStruct((nrows, ncols), jnp.int32)
    weights = jax.ShapeDtypeStruct(negative_weights.shape, jnp.int32)
    operands = [block, block, ctx, edges, weights]
    s1t, rht, rlt, *odds = call(
        first_top, [HBM] * 5, stage(early) + operands, [sems], (*hbm[:3], *hbm[4:]), "first_top",
    )
    s1tx = move(s1t, ring)
    rest = nrows - early
    s1d, rhd, rld, hb, *evens = call(
        first_end, [HBM] * 6 + [VMEM] * 5, stage(rest) + [ctx] + operands, [sems], (*hbm, *odds), "first_end",
    )
    s1dx = move(s1d, ring)
    *s1, rhe0, rle0, c1o, h1o = call(
        first_even, [VMEM] * 12, [block, block, half, half, ctx, ctx], [],
        (*evens, odds[0], odds[2], hb, rht, rlt, rhd, rld), "first_even",
    )
    s1i = [move(x, swap) for x in s1]
    (gated,) = call(gate, [ANY], [f32(8, 128)], [], (s1tx,), "gate", 7000000000)
    u2e, m2e, rho1, rlo1 = call(
        second_odd, [VMEM] * 5 + [ANY], [block, block, half, half], [],
        (*s1i, c1o, edge_counts, negative_weights, gated), "second_odd",
    )
    c1e, h1e = call(
        first_context, [HBM] + [VMEM] * 4 + [ANY], [ctx, ctx], [ctx_buf, sems],
        (hbm[3], evens[0], evens[2], rhe0, rle0, u2e), "first_context",
    )
    u2x = move(u2e, ring)
    detour = DETOUR * nrows // 256 * 16
    u2t, g1t, rht1, rlt1, c2o, h2o = call(
        second_top, [VMEM] * 11, [f32(early + detour, width), f32(early, width)] + stage(early)[1:] + [ctx, ctx], [],
        (s1tx, c1e, edge_counts, negative_weights, s1i[0], c1o, h1o, rho1, rlo1, u2e, m2e), "second_top",
    )
    u2ti = move(u2t, swap)
    u2d, g1a, g1b, rhd1, rld1 = call(
        second_end, [VMEM] * 7,
        [f32(rest, width), f32(nrows - detour, width), f32(detour, width)] + stage(rest)[1:], [vert_buf],
        (s1dx, c1e, edge_counts, negative_weights, g1t, u2e, m2e), "second_end", 10000000000,
    )
    u2di = move(u2d, swap)
    g1ax = move(g1a, unring)
    g1bx = move(g1b, change(unring, {2: 4, 5: 1}))
    c2e, h2e = call(
        second_context, [VMEM] * 8, [ctx, ctx], [],
        (s1tx, s1dx, c1e, h1e, rht1, rlt1, rhd1, rld1), "second_context",
    )
    half_rows = HALF * nrows // 256 * 16
    part = stage(half_rows)[1:]
    half_block = f32(half_rows, width)
    end_part = stage(nrows - half_rows)[1:]
    end_block = f32(nrows - half_rows, width)
    u2i, g2ot, rhot, rlot = call(
        third_odd_top, [VMEM] * 5 + [ANY], [block, half_block] + part, [],
        (u2ti, u2di, c2o, edge_counts, negative_weights, u2d), "third_odd_top",
    )
    g2t, rhet, rlet = call(
        functools.partial(third_even, 0), [VMEM] * 5, [half_block] + part, [],
        (u2x, c2e, edge_counts, negative_weights, g2ot), "third_even_top",
    )
    g2tx = move(g2t, home)
    g2od, rhod, rlod = call(
        third_odd_end, [VMEM] * 4 + [ANY], [end_block] + end_part, [],
        (u2i, c2o, edge_counts, negative_weights, g2t), "third_odd_end",
    )
    g2d, rhed, rled, g1r = call(
        functools.partial(third_even_end, half_rows), [VMEM] * 6, [end_block] + end_part + [f32(detour, width)], [],
        (u2x, c2e, edge_counts, negative_weights, g2od, g1bx), "third_even_end", 1024,
    )
    g2dx = move(g2d, home)
    g1rx = move(g1r, [(4, 1)])
    c3, h3 = call(
        third_context, [VMEM] * 14 + [ANY], [ctx, ctx], [],
        (u2i, c2o, h2o, rhot, rlot, rhod, rlod, u2x, c2e, h2e, rhet, rlet, rhed, rled, g1ax),
        "third_context", 10000000000,
    )

    def out_scratch(rows):
        return [pltpu.VMEM((rows, width), F32)] * 2 + [pltpu.SemaphoreType.DMA((2,))]

    u3, g3 = call(
        last_top, [VMEM] * 8, [block, block],
        [pltpu.VMEM((half_rows, width), F32)] + out_scratch(half_rows),
        (s1t, s1d, g1ax, g1bx, g1rx, u2ti, u2i, g2tx), "last_top", out_spec=HBM,
    )
    u3, g3 = call(
        functools.partial(last_end, half_rows), [VMEM] * 5 + [HBM] * 2, [block, block], out_scratch(nrows - half_rows),
        (s1t, s1d, g1ax, u2i, g2dx, u3, g3), "last_end", out_spec=HBM, aliases={5: 0, 6: 1},
    )
    return u3, g3, c3, h3


def solution(mesh):
    split_rows = P(("snap", "inner"), None)
    return jax.shard_map(
        per_device,
        mesh=mesh,
        in_specs=(
            split_rows,
            split_rows,
            split_rows,
            split_rows,
            P(None, None, ("snap", "inner")),
            P(None, ("snap", "inner")),
        ),
        out_specs=(split_rows,) * 4,
        check_vma=False,
    )
```

```python
import functools

import jax
import jax.numpy as jnp
from jax import lax
from jax.experimental import pallas as pl
from jax.experimental.pallas import tpu as pltpu
from jax.sharding import PartitionSpec as P

F32 = jnp.float32
BF16 = jnp.bfloat16
RATE = 0.05
DETOUR = 4
HALF = 12
EARLY = 5
VMEM = pl.BlockSpec(memory_space=pltpu.VMEM)
HBM = pl.BlockSpec(memory_space=pltpu.HBM)
ANY = pl.BlockSpec(memory_space=pl.ANY)


def split(x):
    high = x.astype(BF16)
    return high, (x - high.astype(F32)).astype(BF16)


def product(a, b, dim_a, dim_b):
    def one(x, y):
        return lax.dot_general(
            x, y, (((dim_a,), (dim_b,)), ((), ())), preferred_element_type=F32
        )

    return one(a[0], b[0]) + (one(a[1], b[0]) + one(a[0], b[1]))


def block_of(size, most):
    return most if size % most == 0 else size


def is_odd():
    return lax.rem(lax.axis_index("inner"), 2) == 1


def adagrad(value, moment, grad):
    moment = moment + grad * grad
    return value - RATE * grad * lax.rsqrt(moment), moment


def vertex_pass(u, c, e, w, r_high, r_low, ready=None):
    us = split(0.5 * u[...])
    wf = w.astype(F32)
    cols = block_of(c.shape[0], 256)
    count = c.shape[0] // cols
    parts = []

    def scores(j):
        if ready is not None:
            ready(j)
        parts.append(split(c[pl.ds(j * cols, cols), :]))
        return product(us, parts[j], 1, 1)

    grad = None
    half_scores = scores(0)
    for j in range(count):
        at = pl.ds(j * cols, cols)
        later = scores(j + 1) if j + 1 < count else None
        ef = e[:, at].astype(F32)
        wj = wf[:, j * cols : (j + 1) * cols]
        resid = split((ef + wj) * jnp.tanh(half_scores) + (wj - ef))
        r_high[:, at] = resid[0]
        r_low[:, at] = resid[1]
        term = product(resid, parts[j], 1, 0)
        grad = term if grad is None else grad + term
        half_scores = later
    return 0.5 * grad


def context_pass(parts, c, h, c_out, h_out):
    us = [split(0.5 * u[...]) for u, _, _ in parts]
    rows = block_of(c.shape[0], 256)
    for j in range(c.shape[0] // rows):
        at = pl.ds(j * rows, rows)
        grad = sum(product((high[:, at], low[:, at]), u, 0, 0) for u, (_, high, low) in zip(us, parts))
        c_out[at, :], h_out[at, :] = adagrad(c[at, :], h[at, :], grad)


def call(body, in_specs, outs, scratch, args, name, flops=1024, out_spec=VMEM, aliases=None):
    return pl.pallas_call(
        body,
        out_shape=outs,
        in_specs=in_specs,
        out_specs=[out_spec] * len(outs),
        scratch_shapes=scratch,
        input_output_aliases=aliases or {},
        compiler_params=pltpu.CompilerParams(vmem_limit_bytes=24 << 20),
        cost_estimate=pl.CostEstimate(flops=flops, bytes_accessed=1024, transcendentals=0),
        name=name,
    )(*args)


def load(pairs, sems, first=0):
    copies = [pltpu.make_async_copy(a, b, sems.at[first + i]) for i, (a, b) in enumerate(pairs)]
    for copy in copies:
        copy.start()
    return copies


def first_top(u, g, c, e, w, s1, r_high, r_low, ub, gb, cb, eb, wb, sems):
    @pl.when(is_odd())
    def _():
        rows = s1.shape[1]
        top, end = pl.ds(0, rows), pl.ds(rows, ub.shape[0] - rows)
        cols = block_of(cb.shape[0], 512)
        count = cb.shape[0] // cols
        chunks = []
        for j in range(count):
            at = pl.ds(j * cols, cols)
            chunks += [(c.at[at], cb.at[at]), (e.at[0, top, at], eb.at[top, at])]
        copies = load([(w, wb), (u, ub)] + chunks + [(g, gb), (e.at[0, end], eb.at[end])], sems)
        copies[0].wait()
        copies[1].wait()
        small = block_of(cb.shape[0], 256)

        def ready(j):
            if j * small % cols == 0:
                at = 2 + 2 * (j * small // cols)
                copies[at].wait()
                copies[at + 1].wait()

        grad = vertex_pass(ub.at[top], cb, eb.at[top], wb[0:1, :], r_high, r_low, ready)
        copies[-2].wait()
        s1[0], s1[1] = adagrad(ub[top, :], gb[top, :], grad)
        copies[-1].wait()


def first_end(
    u, g, c, h, e, w, u_odd, g_odd, c_odd, e_odd, w_odd,
    s1, r_high, r_low, hb, ub, gb, cb, eb, wb, sems,
):
    odd = is_odd()

    @pl.when(odd)
    def _():
        rows = s1.shape[1]
        end = pl.ds(u_odd.shape[0] - rows, rows)
        (copy,) = load([(h, hb)], sems)
        grad = vertex_pass(u_odd.at[end], c_odd, e_odd.at[end], w_odd[0:1, :], r_high, r_low)
        s1[0], s1[1] = adagrad(u_odd[end, :], g_odd[end, :], grad)
        copy.wait()

    @pl.when(jnp.logical_not(odd))
    def _():
        for copy in load([(w, wb), (u, ub), (c, cb), (e.at[0], eb), (g, gb)], sems):
            copy.wait()


def first_even(
    u, g, c, e, w, u_odd, c_odd, h_odd, rh_top, rl_top, rh_end, rl_end,
    u1, g1, r_high, r_low, c_out, h_out,
):
    odd = is_odd()

    @pl.when(odd)
    def _():
        middle, rest = rh_top.shape[0], rh_end.shape[0]
        parts = [
            (u_odd.at[pl.ds(0, middle)], rh_top, rl_top),
            (u_odd.at[pl.ds(middle, rest)], rh_end, rl_end),
        ]
        context_pass(parts, c_odd, h_odd, c_out, h_out)

    @pl.when(jnp.logical_not(odd))
    def _():
        grad = vertex_pass(u, c, e, w[0:1, :], r_high, r_low)
        u1[...], g1[...] = adagrad(u[...], g[...], grad)


def first_context(h, u, c, r_high, r_low, after, c_out, h_out, hb, sems):
    @pl.when(jnp.logical_not(is_odd()))
    def _():
        for copy in load([(h, hb)], sems):
            copy.wait()
        context_pass([(u, r_high, r_low)], c, hb, c_out, h_out)


def gate(*refs):
    out = refs[-1]
    out[...] = jnp.zeros_like(out)


def second_odd(u1, g1, c, e, w, after, u2, g2, r_high, r_low):
    @pl.when(is_odd())
    def _():
        grad = vertex_pass(u1, c, e.at[1], w[1:2, :], r_high, r_low)
        u2[...], g2[...] = adagrad(u1[...], g1[...], grad)


def second_top(
    s1, c, e, w, u_odd, c_odd, h_odd, rh_odd, rl_odd, u2_odd, g2_odd,
    u2, grad_out, r_high, r_low, c_out, h_out,
):
    odd = is_odd()
    rows = grad_out.shape[0]

    @pl.when(odd)
    def _():
        u2[:rows, :] = u2_odd[:rows, :]
        u2[rows:, :] = g2_odd[g2_odd.shape[0] + rows - u2.shape[0] :, :]
        context_pass([(u_odd, rh_odd, rl_odd)], c_odd, h_odd, c_out, h_out)

    @pl.when(jnp.logical_not(odd))
    def _():
        grad = vertex_pass(s1.at[0], c, e.at[1, pl.ds(0, rows)], w[1:2, :], r_high, r_low)
        grad_out[...] = grad
        u2[:rows, :] = adagrad(s1[0], s1[1], grad)[0]


def second_end(s1, c, e, w, grad_top, u2_odd, g2_odd, u2, grad_a, grad_b, r_high, r_low, buf):
    odd = is_odd()
    middle, direct = grad_top.shape[0], grad_a.shape[0]

    @pl.when(odd)
    def _():
        u2[...] = u2_odd[middle:, :]
        grad_a[...] = g2_odd[:direct, :]

    @pl.when(jnp.logical_not(odd))
    def _():
        grad = vertex_pass(s1.at[0], c, e.at[1, pl.ds(middle, s1.shape[1])], w[1:2, :], r_high, r_low)
        buf[:middle, :] = grad_top[...]
        buf[middle:, :] = grad
        grad_a[...], grad_b[...] = buf[:direct, :], buf[direct:, :]
        u2[...] = adagrad(s1[0], s1[1], grad)[0]


def second_context(s1_top, s1_end, c, h, rh_top, rl_top, rh_end, rl_end, c_out, h_out):
    @pl.when(jnp.logical_not(is_odd()))
    def _():
        parts = [(s1_top.at[0], rh_top, rl_top), (s1_end.at[0], rh_end, rl_end)]
        context_pass(parts, c, h, c_out, h_out)


def third(odd, row, u, c, e, w, g2, r_high, r_low):
    rows = pl.ds(row, g2.shape[0])

    @pl.when(is_odd() == odd)
    def _():
        g2[...] = vertex_pass(u.at[rows], c, e.at[2, rows], w[2:3, :], r_high, r_low)


def third_odd_top(u_top, u_end, c, e, w, after, u, g2, r_high, r_low):
    middle = u.shape[0] - u_end.shape[0]
    u[:middle, :] = u_top[:middle, :]
    u[middle:, :] = u_end[...]
    third(True, 0, u, c, e, w, g2, r_high, r_low)


def third_odd_end(u, c, e, w, after, g2, r_high, r_low):
    third(True, u.shape[0] - g2.shape[0], u, c, e, w, g2, r_high, r_low)


def third_even(row, u, c, e, w, g2_odd, g2, r_high, r_low):
    @pl.when(is_odd())
    def _():
        g2[...] = g2_odd[...]

    third(False, row, u, c, e, w, g2, r_high, r_low)


def third_even_end(row, u, c, e, w, g2_odd, g1, g2, r_high, r_low, g1_out):
    g1_out[...] = g1[...]
    third_even(row, u, c, e, w, g2_odd, g2, r_high, r_low)


def third_context(
    u_odd, c_odd, h_odd, rh_odd, rl_odd, rh_odd_end, rl_odd_end,
    u_even, c_even, h_even, rh_even, rl_even, rh_even_end, rl_even_end, after, c_out, h_out,
):
    odd = is_odd()
    middle = rh_odd.shape[0]
    top, end = pl.ds(0, middle), pl.ds(middle, rh_odd_end.shape[0])

    @pl.when(odd)
    def _():
        parts = [(u_odd.at[top], rh_odd, rl_odd), (u_odd.at[end], rh_odd_end, rl_odd_end)]
        context_pass(parts, c_odd, h_odd, c_out, h_out)

    @pl.when(jnp.logical_not(odd))
    def _():
        parts = [(u_even.at[top], rh_even, rl_even), (u_even.at[end], rh_even_end, rl_even_end)]
        context_pass(parts, c_even, h_even, c_out, h_out)


def last(row, s1_top, s1_end, g1, u2, g2, u_out, g_out, ub, gb, sems):
    odd = is_odd()
    rows = g2.shape[0]

    @pl.when(odd)
    def _():
        begin = 0
        for s1 in (s1_top, s1_end):
            low, high = max(row, begin), min(row + rows, begin + s1.shape[1])
            if low < high:
                at, here = pl.ds(low - begin, high - low), pl.ds(low - row, high - low)
                value, moment = adagrad(s1[0, at, :], s1[1, at, :], g1[here, :])
                ub[here, :], gb[here, :] = adagrad(value, moment, g2[here, :])
            begin += s1.shape[1]

    @pl.when(jnp.logical_not(odd))
    def _():
        ub[...], gb[...] = adagrad(u2[pl.ds(row, rows), :], g1[:rows, :], g2[...])

    at = pl.ds(row, rows)
    for copy in load([(ub, u_out.at[at]), (gb, g_out.at[at])], sems):
        copy.wait()


def last_top(s1_top, s1_end, g1, u2, g2, u_out, g_out, done, *scratch):
    last(0, s1_top, s1_end, g1, u2, g2, u_out, g_out, *scratch)


def last_end(row, s1_top, s1_end, g1_a, g1_b, g1_over, swapped, u2, g2, after, u_top, g_top, u_out, g_out, buf, *scratch):
    rows, detour = g2.shape[0], g1_b.shape[0]
    place = lax.axis_index("inner")
    odd = is_odd()

    @pl.when(jnp.logical_and(odd, place != 1))
    def _():
        buf[rows - detour :, :] = g1_b[...]

    @pl.when(place == 1)
    def _():
        buf[rows - detour :, :] = g1_over[...]

    @pl.when(jnp.logical_not(odd))
    def _():
        buf[rows - detour :, :] = swapped[swapped.shape[0] - detour :, :]

    if rows > detour:
        buf[: rows - detour, :] = g1_a[row:, :]
    last(row, s1_top, s1_end, buf, u2, g2, u_out, g_out, *scratch)


def per_device(vertices, vertex_moments, contexts, context_moments, edge_counts, negative_weights):
    nrows, width = vertices.shape
    ncols = contexts.shape[0]
    count = lax.axis_size("inner")
    assert count % 2 == 0 and count > 5 and edge_counts.shape[0] == 3

    ring = [(i, (i + 1) % count) for i in range(count)]
    unring = [(b, a) for a, b in ring]
    swap = [(i, i ^ 1) for i in range(count)]
    home = [(i, (i - 2) % count) for i in range(count)]

    def change(pairs, targets):
        return [(a, targets.get(a, b)) for a, b in pairs]

    def move(value, pairs):
        return lax.ppermute(value, "inner", pairs)

    def f32(*shape):
        return jax.ShapeDtypeStruct(shape, F32)

    block = f32(nrows, width)
    ctx = f32(ncols, width)
    half = jax.ShapeDtypeStruct((nrows, ncols), BF16)
    vert_buf = pltpu.VMEM((nrows, width), F32)
    ctx_buf = pltpu.VMEM((ncols, width), F32)
    sems = pltpu.SemaphoreType.DMA((4 + 2 * (ncols // block_of(ncols, 256)),))
    hbm = [
        pltpu.with_memory_space_constraint(x, pltpu.HBM)
        for x in (vertices, vertex_moments, contexts, context_moments, edge_counts, negative_weights)
    ]

    def stage(rows):
        return [f32(2, rows, width)] + [jax.ShapeDtypeStruct((rows, ncols), BF16)] * 2

    early = EARLY * nrows // 256 * 16
    edges = jax.ShapeDtypeStruct((nrows, ncols), jnp.int32)
    weights = jax.ShapeDtypeStruct(negative_weights.shape, jnp.int32)
    operands = [block, block, ctx, edges, weights]
    s1t, rht, rlt, *odds = call(
        first_top, [HBM] * 5, stage(early) + operands, [sems], (*hbm[:3], *hbm[4:]), "first_top",
    )
    s1tx = move(s1t, ring)
    rest = nrows - early
    s1d, rhd, rld, hb, *evens = call(
        first_end, [HBM] * 6 + [VMEM] * 5, stage(rest) + [ctx] + operands, [sems], (*hbm, *odds), "first_end",
    )
    s1dx = move(s1d, ring)
    *s1, rhe0, rle0, c1o, h1o = call(
        first_even, [VMEM] * 12, [block, block, half, half, ctx, ctx], [],
        (*evens, odds[0], odds[2], hb, rht, rlt, rhd, rld), "first_even",
    )
    s1i = [move(x, swap) for x in s1]
    (gated,) = call(gate, [ANY], [f32(8, 128)], [], (s1tx,), "gate", 7000000000)
    u2e, m2e, rho1, rlo1 = call(
        second_odd, [VMEM] * 5 + [ANY], [block, block, half, half], [],
        (*s1i, c1o, edge_counts, negative_weights, gated), "second_odd",
    )
    c1e, h1e = call(
        first_context, [HBM] + [VMEM] * 4 + [ANY], [ctx, ctx], [ctx_buf, sems],
        (hbm[3], evens[0], evens[2], rhe0, rle0, u2e), "first_context",
    )
    u2x = move(u2e, ring)
    detour = DETOUR * nrows // 256 * 16
    u2t, g1t, rht1, rlt1, c2o, h2o = call(
        second_top, [VMEM] * 11, [f32(early + detour, width), f32(early, width)] + stage(early)[1:] + [ctx, ctx], [],
        (s1tx, c1e, edge_counts, negative_weights, s1i[0], c1o, h1o, rho1, rlo1, u2e, m2e), "second_top",
    )
    u2ti = move(u2t, swap)
    u2d, g1a, g1b, rhd1, rld1 = call(
        second_end, [VMEM] * 7,
        [f32(rest, width), f32(nrows - detour, width), f32(detour, width)] + stage(rest)[1:], [vert_buf],
        (s1dx, c1e, edge_counts, negative_weights, g1t, u2e, m2e), "second_end", 10000000000,
    )
    u2di = move(u2d, swap)
    g1ax = move(g1a, unring)
    g1bx = move(g1b, change(unring, {2: 4, 5: 1}))
    c2e, h2e = call(
        second_context, [VMEM] * 8, [ctx, ctx], [],
        (s1tx, s1dx, c1e, h1e, rht1, rlt1, rhd1, rld1), "second_context",
    )
    half_rows = HALF * nrows // 256 * 16
    part = stage(half_rows)[1:]
    half_block = f32(half_rows, width)
    end_part = stage(nrows - half_rows)[1:]
    end_block = f32(nrows - half_rows, width)
    u2i, g2ot, rhot, rlot = call(
        third_odd_top, [VMEM] * 5 + [ANY], [block, half_block] + part, [],
        (u2ti, u2di, c2o, edge_counts, negative_weights, u2d), "third_odd_top",
    )
    g2t, rhet, rlet = call(
        functools.partial(third_even, 0), [VMEM] * 5, [half_block] + part, [],
        (u2x, c2e, edge_counts, negative_weights, g2ot), "third_even_top",
    )
    g2tx = move(g2t, home)
    g2od, rhod, rlod = call(
        third_odd_end, [VMEM] * 4 + [ANY], [end_block] + end_part, [],
        (u2i, c2o, edge_counts, negative_weights, g2t), "third_odd_end",
    )
    g2d, rhed, rled, g1r = call(
        functools.partial(third_even_end, half_rows), [VMEM] * 6, [end_block] + end_part + [f32(detour, width)], [],
        (u2x, c2e, edge_counts, negative_weights, g2od, g1bx), "third_even_end", 1024,
    )
    g2dx = move(g2d, home)
    g1rx = move(g1r, [(4, 1)])
    c3, h3 = call(
        third_context, [VMEM] * 14 + [ANY], [ctx, ctx], [],
        (u2i, c2o, h2o, rhot, rlot, rhod, rlod, u2x, c2e, h2e, rhet, rlet, rhed, rled, g1ax),
        "third_context", 10000000000,
    )

    def out_scratch(rows):
        return [pltpu.VMEM((rows, width), F32)] * 2 + [pltpu.SemaphoreType.DMA((2,))]

    u3, g3, done = call(
        last_top, [VMEM] * 5, [block, block, f32(8, 128)], out_scratch(half_rows), (s1t, s1d, g1ax, u2i, g2tx), "last_top",
        out_spec=HBM,
    )
    (arrived,) = call(gate, [ANY] * 2, [f32(8, 128)], [], (g1rx, done), "gate_last", 10000000000)
    u3, g3 = call(
        functools.partial(last_end, half_rows), [VMEM] * 8 + [ANY] + [HBM] * 2, [block, block],
        [pltpu.VMEM((nrows - half_rows, width), F32)] + out_scratch(nrows - half_rows),
        (s1t, s1d, g1ax, g1bx, g1rx, u2ti, u2i, g2dx, arrived, u3, g3), "last_end", out_spec=HBM, aliases={9: 0, 10: 1},
    )
    return u3, g3, c3, h3


def solution(mesh):
    split_rows = P(("snap", "inner"), None)
    return jax.shard_map(
        per_device,
        mesh=mesh,
        in_specs=(
            split_rows,
            split_rows,
            split_rows,
            split_rows,
            P(None, None, ("snap", "inner")),
            P(None, ("snap", "inner")),
        ),
        out_specs=(split_rows,) * 4,
        check_vma=False,
    )
```

```python
import functools

import jax
import jax.numpy as jnp
from jax import lax
from jax.experimental import pallas as pl
from jax.experimental.pallas import tpu as pltpu
from jax.sharding import PartitionSpec as P

F32 = jnp.float32
BF16 = jnp.bfloat16
RATE = 0.05
DETOUR = 8
HALF = 12
EARLY = 6
VMEM = pl.BlockSpec(memory_space=pltpu.VMEM)
HBM = pl.BlockSpec(memory_space=pltpu.HBM)
ANY = pl.BlockSpec(memory_space=pl.ANY)


def split(x):
    high = x.astype(BF16)
    return high, (x - high.astype(F32)).astype(BF16)


def product(a, b, dim_a, dim_b):
    def one(x, y):
        return lax.dot_general(
            x, y, (((dim_a,), (dim_b,)), ((), ())), preferred_element_type=F32
        )

    return one(a[0], b[0]) + (one(a[1], b[0]) + one(a[0], b[1]))


def block_of(size, most):
    return most if size % most == 0 else size


def is_odd():
    return lax.rem(lax.axis_index("inner"), 2) == 1


def adagrad(value, moment, grad):
    moment = moment + grad * grad
    return value - RATE * grad * lax.rsqrt(moment), moment


def vertex_pass(u, c, e, w, r_high, r_low, ready=None):
    us = split(0.5 * u[...])
    wf = w.astype(F32)
    cols = block_of(c.shape[0], 256)
    count = c.shape[0] // cols
    parts = []

    def scores(j):
        if ready is not None:
            ready(j)
        parts.append(split(c[pl.ds(j * cols, cols), :]))
        return product(us, parts[j], 1, 1)

    grad = None
    half_scores = scores(0)
    for j in range(count):
        at = pl.ds(j * cols, cols)
        later = scores(j + 1) if j + 1 < count else None
        ef = e[:, at].astype(F32)
        wj = wf[:, j * cols : (j + 1) * cols]
        resid = split((ef + wj) * jnp.tanh(half_scores) + (wj - ef))
        r_high[:, at] = resid[0]
        r_low[:, at] = resid[1]
        term = product(resid, parts[j], 1, 0)
        grad = term if grad is None else grad + term
        half_scores = later
    return 0.5 * grad


def context_pass(parts, c, h, c_out, h_out):
    us = [split(0.5 * u[...]) for u, _, _ in parts]
    rows = block_of(c.shape[0], 256)
    for j in range(c.shape[0] // rows):
        at = pl.ds(j * rows, rows)
        grad = sum(product((high[:, at], low[:, at]), u, 0, 0) for u, (_, high, low) in zip(us, parts))
        c_out[at, :], h_out[at, :] = adagrad(c[at, :], h[at, :], grad)


def call(body, in_specs, outs, scratch, args, name, flops=1024, out_spec=VMEM, aliases=None):
    return pl.pallas_call(
        body,
        out_shape=outs,
        in_specs=in_specs,
        out_specs=[out_spec] * len(outs),
        scratch_shapes=scratch,
        input_output_aliases=aliases or {},
        compiler_params=pltpu.CompilerParams(vmem_limit_bytes=24 << 20),
        cost_estimate=pl.CostEstimate(flops=flops, bytes_accessed=1024, transcendentals=0),
        name=name,
    )(*args)


def load(pairs, sems, first=0):
    copies = [pltpu.make_async_copy(a, b, sems.at[first + i]) for i, (a, b) in enumerate(pairs)]
    for copy in copies:
        copy.start()
    return copies


def first_top(u, g, c, e, w, s1, r_high, r_low, ub, gb, cb, eb, wb, sems):
    @pl.when(is_odd())
    def _():
        rows = s1.shape[1]
        top, end = pl.ds(0, rows), pl.ds(rows, ub.shape[0] - rows)
        cols = block_of(cb.shape[0], 512)
        count = cb.shape[0] // cols
        chunks = []
        for j in range(count):
            at = pl.ds(j * cols, cols)
            chunks += [(c.at[at], cb.at[at]), (e.at[0, top, at], eb.at[top, at])]
        copies = load([(w, wb), (u, ub)] + chunks + [(g, gb), (e.at[0, end], eb.at[end])], sems)
        copies[0].wait()
        copies[1].wait()
        small = block_of(cb.shape[0], 256)

        def ready(j):
            if j * small % cols == 0:
                at = 2 + 2 * (j * small // cols)
                copies[at].wait()
                copies[at + 1].wait()

        grad = vertex_pass(ub.at[top], cb, eb.at[top], wb[0:1, :], r_high, r_low, ready)
        copies[-2].wait()
        s1[0], s1[1] = adagrad(ub[top, :], gb[top, :], grad)
        copies[-1].wait()


def first_end(
    u, g, c, h, e, w, u_odd, g_odd, c_odd, e_odd, w_odd,
    s1, r_high, r_low, hb, ub, gb, cb, eb, wb, sems,
):
    odd = is_odd()

    @pl.when(odd)
    def _():
        rows = s1.shape[1]
        end = pl.ds(u_odd.shape[0] - rows, rows)
        (copy,) = load([(h, hb)], sems)
        grad = vertex_pass(u_odd.at[end], c_odd, e_odd.at[end], w_odd[0:1, :], r_high, r_low)
        s1[0], s1[1] = adagrad(u_odd[end, :], g_odd[end, :], grad)
        copy.wait()

    @pl.when(jnp.logical_not(odd))
    def _():
        for copy in load([(w, wb), (u, ub), (c, cb), (e.at[0], eb), (g, gb)], sems):
            copy.wait()


def first_even(
    u, g, c, e, w, u_odd, c_odd, h_odd, rh_top, rl_top, rh_end, rl_end,
    u1, g1, r_high, r_low, c_out, h_out,
):
    odd = is_odd()

    @pl.when(odd)
    def _():
        middle, rest = rh_top.shape[0], rh_end.shape[0]
        parts = [
            (u_odd.at[pl.ds(0, middle)], rh_top, rl_top),
            (u_odd.at[pl.ds(middle, rest)], rh_end, rl_end),
        ]
        context_pass(parts, c_odd, h_odd, c_out, h_out)

    @pl.when(jnp.logical_not(odd))
    def _():
        grad = vertex_pass(u, c, e, w[0:1, :], r_high, r_low)
        u1[...], g1[...] = adagrad(u[...], g[...], grad)


def first_context(h, u, c, r_high, r_low, after, c_out, h_out, hb, sems):
    @pl.when(jnp.logical_not(is_odd()))
    def _():
        for copy in load([(h, hb)], sems):
            copy.wait()
        context_pass([(u, r_high, r_low)], c, hb, c_out, h_out)


def gate(*refs):
    out = refs[-1]
    out[...] = jnp.zeros_like(out)


def second_odd(u1, g1, c, e, w, after, u2, g2, r_high, r_low):
    @pl.when(is_odd())
    def _():
        grad = vertex_pass(u1, c, e.at[1], w[1:2, :], r_high, r_low)
        u2[...], g2[...] = adagrad(u1[...], g1[...], grad)


def second_top(
    s1, c, e, w, u_odd, c_odd, h_odd, rh_odd, rl_odd, u2_odd, g2_odd,
    u2, grad_out, r_high, r_low, c_out, h_out,
):
    odd = is_odd()
    rows = grad_out.shape[0]

    @pl.when(odd)
    def _():
        u2[:rows, :] = u2_odd[:rows, :]
        u2[rows:, :] = g2_odd[g2_odd.shape[0] + rows - u2.shape[0] :, :]
        context_pass([(u_odd, rh_odd, rl_odd)], c_odd, h_odd, c_out, h_out)

    @pl.when(jnp.logical_not(odd))
    def _():
        grad = vertex_pass(s1.at[0], c, e.at[1, pl.ds(0, rows)], w[1:2, :], r_high, r_low)
        grad_out[...] = grad
        u2[:rows, :] = adagrad(s1[0], s1[1], grad)[0]


def second_end(s1, c, e, w, grad_top, u2_odd, g2_odd, u2, grad_a, grad_b, r_high, r_low, buf):
    odd = is_odd()
    middle, direct = grad_top.shape[0], grad_a.shape[0]

    @pl.when(odd)
    def _():
        u2[...] = u2_odd[middle:, :]
        grad_a[...] = g2_odd[:direct, :]

    @pl.when(jnp.logical_not(odd))
    def _():
        grad = vertex_pass(s1.at[0], c, e.at[1, pl.ds(middle, s1.shape[1])], w[1:2, :], r_high, r_low)
        buf[:middle, :] = grad_top[...]
        buf[middle:, :] = grad
        grad_a[...], grad_b[...] = buf[:direct, :], buf[direct:, :]
        u2[...] = adagrad(s1[0], s1[1], grad)[0]


def second_context(s1_top, s1_end, c, h, rh_top, rl_top, rh_end, rl_end, c_out, h_out):
    @pl.when(jnp.logical_not(is_odd()))
    def _():
        parts = [(s1_top.at[0], rh_top, rl_top), (s1_end.at[0], rh_end, rl_end)]
        context_pass(parts, c, h, c_out, h_out)


def third(odd, row, u, c, e, w, g2, r_high, r_low):
    rows = pl.ds(row, g2.shape[0])

    @pl.when(is_odd() == odd)
    def _():
        g2[...] = vertex_pass(u.at[rows], c, e.at[2, rows], w[2:3, :], r_high, r_low)


def third_odd_top(u_top, u_end, c, e, w, after, u, g2, r_high, r_low):
    middle = u.shape[0] - u_end.shape[0]
    u[:middle, :] = u_top[:middle, :]
    u[middle:, :] = u_end[...]
    third(True, 0, u, c, e, w, g2, r_high, r_low)


def third_odd_end(u, c, e, w, after, g2, r_high, r_low):
    third(True, u.shape[0] - g2.shape[0], u, c, e, w, g2, r_high, r_low)


def third_even(row, u, c, e, w, g2_odd, g2, r_high, r_low):
    @pl.when(is_odd())
    def _():
        g2[...] = g2_odd[...]

    third(False, row, u, c, e, w, g2, r_high, r_low)


def third_even_end(row, u, c, e, w, g2_odd, g1, g2, r_high, r_low, g1_out):
    g1_out[...] = g1[...]
    third_even(row, u, c, e, w, g2_odd, g2, r_high, r_low)


def third_context(
    u_odd, c_odd, h_odd, rh_odd, rl_odd, rh_odd_end, rl_odd_end,
    u_even, c_even, h_even, rh_even, rl_even, rh_even_end, rl_even_end, after, c_out, h_out,
):
    odd = is_odd()
    middle = rh_odd.shape[0]
    top, end = pl.ds(0, middle), pl.ds(middle, rh_odd_end.shape[0])

    @pl.when(odd)
    def _():
        parts = [(u_odd.at[top], rh_odd, rl_odd), (u_odd.at[end], rh_odd_end, rl_odd_end)]
        context_pass(parts, c_odd, h_odd, c_out, h_out)

    @pl.when(jnp.logical_not(odd))
    def _():
        parts = [(u_even.at[top], rh_even, rl_even), (u_even.at[end], rh_even_end, rl_even_end)]
        context_pass(parts, c_even, h_even, c_out, h_out)


def last(row, s1_top, s1_end, g1, u2, g2, u_out, g_out, ub, gb, sems):
    odd = is_odd()
    rows = g2.shape[0]
    at = pl.ds(row, rows)
    copies = [pltpu.make_async_copy(gb, g_out.at[at], sems.at[0]), pltpu.make_async_copy(ub, u_out.at[at], sems.at[1])]

    @pl.when(odd)
    def _():
        begin = 0
        for s1 in (s1_top, s1_end):
            low, high = max(row, begin), min(row + rows, begin + s1.shape[1])
            if low < high:
                there, here = pl.ds(low - begin, high - low), pl.ds(low - row, high - low)
                value, moment = adagrad(s1[0, there, :], s1[1, there, :], g1[here, :])
                gb[here, :] = moment + g2[here, :] * g2[here, :]
                ub[here, :] = value
            begin += s1.shape[1]

    @pl.when(jnp.logical_not(odd))
    def _():
        gb[...] = g1[:rows, :] + g2[...] * g2[...]
        ub[...] = u2[at, :]

    copies[0].start()
    ub[...] = ub[...] - RATE * g2[...] * lax.rsqrt(gb[...])
    copies[1].start()
    for copy in copies:
        copy.wait()


def last_top(s1_top, s1_end, g1, u2, g2, u_out, g_out, done, *scratch):
    last(0, s1_top, s1_end, g1, u2, g2, u_out, g_out, *scratch)


def last_end(row, s1_top, s1_end, g1_a, g1_b, g1_over, swapped, u2, g2, after, u_top, g_top, u_out, g_out, buf, *scratch):
    rows, detour = g2.shape[0], g1_b.shape[0]
    place = lax.axis_index("inner")
    odd = is_odd()

    @pl.when(jnp.logical_and(odd, place != 1))
    def _():
        buf[rows - detour :, :] = g1_b[...]

    @pl.when(place == 1)
    def _():
        buf[rows - detour :, :] = g1_over[...]

    @pl.when(jnp.logical_not(odd))
    def _():
        buf[rows - detour :, :] = swapped[swapped.shape[0] - detour :, :]

    if rows > detour:
        buf[: rows - detour, :] = g1_a[row:, :]
    last(row, s1_top, s1_end, buf, u2, g2, u_out, g_out, *scratch)


def per_device(vertices, vertex_moments, contexts, context_moments, edge_counts, negative_weights):
    nrows, width = vertices.shape
    ncols = contexts.shape[0]
    count = lax.axis_size("inner")
    assert count % 2 == 0 and count > 5 and edge_counts.shape[0] == 3

    ring = [(i, (i + 1) % count) for i in range(count)]
    unring = [(b, a) for a, b in ring]
    swap = [(i, i ^ 1) for i in range(count)]
    home = [(i, (i - 2) % count) for i in range(count)]

    def change(pairs, targets):
        return [(a, targets.get(a, b)) for a, b in pairs]

    def move(value, pairs):
        return lax.ppermute(value, "inner", pairs)

    def f32(*shape):
        return jax.ShapeDtypeStruct(shape, F32)

    block = f32(nrows, width)
    ctx = f32(ncols, width)
    half = jax.ShapeDtypeStruct((nrows, ncols), BF16)
    vert_buf = pltpu.VMEM((nrows, width), F32)
    ctx_buf = pltpu.VMEM((ncols, width), F32)
    sems = pltpu.SemaphoreType.DMA((4 + 2 * (ncols // block_of(ncols, 256)),))
    hbm = [
        pltpu.with_memory_space_constraint(x, pltpu.HBM)
        for x in (vertices, vertex_moments, contexts, context_moments, edge_counts, negative_weights)
    ]

    def stage(rows):
        return [f32(2, rows, width)] + [jax.ShapeDtypeStruct((rows, ncols), BF16)] * 2

    early = EARLY * nrows // 256 * 16
    edges = jax.ShapeDtypeStruct((nrows, ncols), jnp.int32)
    weights = jax.ShapeDtypeStruct(negative_weights.shape, jnp.int32)
    operands = [block, block, ctx, edges, weights]
    s1t, rht, rlt, *odds = call(
        first_top, [HBM] * 5, stage(early) + operands, [sems], (*hbm[:3], *hbm[4:]), "first_top",
    )
    s1tx = move(s1t, ring)
    rest = nrows - early
    s1d, rhd, rld, hb, *evens = call(
        first_end, [HBM] * 6 + [VMEM] * 5, stage(rest) + [ctx] + operands, [sems], (*hbm, *odds), "first_end",
    )
    s1dx = move(s1d, ring)
    *s1, rhe0, rle0, c1o, h1o = call(
        first_even, [VMEM] * 12, [block, block, half, half, ctx, ctx], [],
        (*evens, odds[0], odds[2], hb, rht, rlt, rhd, rld), "first_even",
    )
    s1i = [move(x, swap) for x in s1]
    (gated,) = call(gate, [ANY], [f32(8, 128)], [], (s1tx,), "gate", 6000000000)
    u2e, m2e, rho1, rlo1 = call(
        second_odd, [VMEM] * 5 + [ANY], [block, block, half, half], [],
        (*s1i, c1o, edge_counts, negative_weights, gated), "second_odd",
    )
    c1e, h1e = call(
        first_context, [HBM] + [VMEM] * 4 + [ANY], [ctx, ctx], [ctx_buf, sems],
        (hbm[3], evens[0], evens[2], rhe0, rle0, u2e), "first_context",
    )
    u2x = move(u2e, ring)
    detour = DETOUR * nrows // 512 * 16
    u2t, g1t, rht1, rlt1, c2o, h2o = call(
        second_top, [VMEM] * 11, [f32(early + detour, width), f32(early, width)] + stage(early)[1:] + [ctx, ctx], [],
        (s1tx, c1e, edge_counts, negative_weights, s1i[0], c1o, h1o, rho1, rlo1, u2e, m2e), "second_top",
    )
    u2ti = move(u2t, swap)
    u2d, g1a, g1b, rhd1, rld1 = call(
        second_end, [VMEM] * 7,
        [f32(rest, width), f32(nrows - detour, width), f32(detour, width)] + stage(rest)[1:], [vert_buf],
        (s1dx, c1e, edge_counts, negative_weights, g1t, u2e, m2e), "second_end", 10000000000,
    )
    u2di = move(u2d, swap)
    g1ax = move(g1a, unring)
    g1bx = move(g1b, change(unring, {2: 4, 5: 1}))
    c2e, h2e = call(
        second_context, [VMEM] * 8, [ctx, ctx], [],
        (s1tx, s1dx, c1e, h1e, rht1, rlt1, rhd1, rld1), "second_context",
    )
    half_rows = HALF * nrows // 256 * 16
    part = stage(half_rows)[1:]
    half_block = f32(half_rows, width)
    end_part = stage(nrows - half_rows)[1:]
    end_block = f32(nrows - half_rows, width)
    u2i, g2ot, rhot, rlot = call(
        third_odd_top, [VMEM] * 5 + [ANY], [block, half_block] + part, [],
        (u2ti, u2di, c2o, edge_counts, negative_weights, u2d), "third_odd_top",
    )
    g2t, rhet, rlet = call(
        functools.partial(third_even, 0), [VMEM] * 5, [half_block] + part, [],
        (u2x, c2e, edge_counts, negative_weights, g2ot), "third_even_top",
    )
    g2tx = move(g2t, home)
    g2od, rhod, rlod = call(
        third_odd_end, [VMEM] * 4 + [ANY], [end_block] + end_part, [],
        (u2i, c2o, edge_counts, negative_weights, g2t), "third_odd_end",
    )
    g2d, rhed, rled, g1r = call(
        functools.partial(third_even_end, half_rows), [VMEM] * 6, [end_block] + end_part + [f32(detour, width)], [],
        (u2x, c2e, edge_counts, negative_weights, g2od, g1bx), "third_even_end", 1024,
    )
    g2dx = move(g2d, home)
    g1rx = move(g1r, [(4, 1)])
    c3, h3 = call(
        third_context, [VMEM] * 14 + [ANY], [ctx, ctx], [],
        (u2i, c2o, h2o, rhot, rlot, rhod, rlod, u2x, c2e, h2e, rhet, rlet, rhed, rled, g1ax),
        "third_context", 10000000000,
    )

    def out_scratch(rows):
        return [pltpu.VMEM((rows, width), F32)] * 2 + [pltpu.SemaphoreType.DMA((2,))]

    u3, g3, done = call(
        last_top, [VMEM] * 5, [block, block, f32(8, 128)], out_scratch(half_rows), (s1t, s1d, g1ax, u2i, g2tx), "last_top",
        out_spec=HBM,
    )
    (arrived,) = call(gate, [ANY] * 2, [f32(8, 128)], [], (g1rx, done), "gate_last", 10000000000)
    u3, g3 = call(
        functools.partial(last_end, half_rows), [VMEM] * 8 + [ANY] + [HBM] * 2, [block, block],
        [pltpu.VMEM((nrows - half_rows, width), F32)] + out_scratch(nrows - half_rows),
        (s1t, s1d, g1ax, g1bx, g1rx, u2ti, u2i, g2dx, arrived, u3, g3), "last_end", out_spec=HBM, aliases={9: 0, 10: 1},
    )
    return u3, g3, c3, h3


def solution(mesh):
    split_rows = P(("snap", "inner"), None)
    return jax.shard_map(
        per_device,
        mesh=mesh,
        in_specs=(
            split_rows,
            split_rows,
            split_rows,
            split_rows,
            P(None, None, ("snap", "inner")),
            P(None, ("snap", "inner")),
        ),
        out_specs=(split_rows,) * 4,
        check_vma=False,
    )
```

```python
import functools

import jax
import jax.numpy as jnp
from jax import lax
from jax.experimental import pallas as pl
from jax.experimental.pallas import tpu as pltpu
from jax.sharding import PartitionSpec as P

F32 = jnp.float32
BF16 = jnp.bfloat16
RATE = 0.05
STACKED = 256
DETOUR = 8
HALF = 12
EARLY = 6
VMEM = pl.BlockSpec(memory_space=pltpu.VMEM)
HBM = pl.BlockSpec(memory_space=pltpu.HBM)
ANY = pl.BlockSpec(memory_space=pl.ANY)


def split(x):
    high = x.astype(BF16)
    return high, (x - high.astype(F32)).astype(BF16)


def product(a, b, dim_a, dim_b):
    def one(x, y):
        return lax.dot_general(
            x, y, (((dim_a,), (dim_b,)), ((), ())), preferred_element_type=F32
        )

    rows = a[0].shape[0]
    if dim_a == 1 and rows <= STACKED:
        both = one(jnp.concatenate(a, axis=0), b[0])
        return both[:rows] + (both[rows:] + one(a[0], b[1]))
    return one(a[0], b[0]) + (one(a[1], b[0]) + one(a[0], b[1]))


def block_of(size, most):
    return most if size % most == 0 else size


def is_odd():
    return lax.rem(lax.axis_index("inner"), 2) == 1


def adagrad(value, moment, grad):
    moment = moment + grad * grad
    return value - RATE * grad * lax.rsqrt(moment), moment


def vertex_pass(u, c, e, w, r_high, r_low, ready=None):
    us = split(0.5 * u[...])
    wf = w.astype(F32)
    cols = block_of(c.shape[0], 256)
    count = c.shape[0] // cols
    parts = []

    def scores(j):
        if ready is not None:
            ready(j)
        parts.append(split(c[pl.ds(j * cols, cols), :]))
        return product(us, parts[j], 1, 1)

    grad = None
    half_scores = scores(0)
    for j in range(count):
        at = pl.ds(j * cols, cols)
        later = scores(j + 1) if j + 1 < count else None
        ef = e[:, at].astype(F32)
        wj = wf[:, j * cols : (j + 1) * cols]
        resid = split((ef + wj) * jnp.tanh(half_scores) + (wj - ef))
        r_high[:, at] = resid[0]
        r_low[:, at] = resid[1]
        term = product(resid, parts[j], 1, 0)
        grad = term if grad is None else grad + term
        half_scores = later
    return 0.5 * grad


def context_pass(parts, c, h, c_out, h_out):
    us = [split(0.5 * u[...]) for u, _, _ in parts]
    rows = block_of(c.shape[0], 256)
    for j in range(c.shape[0] // rows):
        at = pl.ds(j * rows, rows)
        grad = sum(product((high[:, at], low[:, at]), u, 0, 0) for u, (_, high, low) in zip(us, parts))
        c_out[at, :], h_out[at, :] = adagrad(c[at, :], h[at, :], grad)


def call(body, in_specs, outs, scratch, args, name, flops=1024, out_spec=VMEM, aliases=None):
    return pl.pallas_call(
        body,
        out_shape=outs,
        in_specs=in_specs,
        out_specs=[out_spec] * len(outs),
        scratch_shapes=scratch,
        input_output_aliases=aliases or {},
        compiler_params=pltpu.CompilerParams(vmem_limit_bytes=24 << 20),
        cost_estimate=pl.CostEstimate(flops=flops, bytes_accessed=1024, transcendentals=0),
        name=name,
    )(*args)


def load(pairs, sems, first=0):
    copies = [pltpu.make_async_copy(a, b, sems.at[first + i]) for i, (a, b) in enumerate(pairs)]
    for copy in copies:
        copy.start()
    return copies


def first_top(u, g, c, e, w, s1, r_high, r_low, ub, gb, cb, eb, wb, sems):
    @pl.when(is_odd())
    def _():
        rows = s1.shape[1]
        top, end = pl.ds(0, rows), pl.ds(rows, ub.shape[0] - rows)
        cols = block_of(cb.shape[0], 512)
        count = cb.shape[0] // cols
        chunks = []
        for j in range(count):
            at = pl.ds(j * cols, cols)
            chunks += [(c.at[at], cb.at[at]), (e.at[0, top, at], eb.at[top, at])]
        copies = load([(w, wb), (u, ub)] + chunks + [(g, gb), (e.at[0, end], eb.at[end])], sems)
        copies[0].wait()
        copies[1].wait()
        small = block_of(cb.shape[0], 256)

        def ready(j):
            if j * small % cols == 0:
                at = 2 + 2 * (j * small // cols)
                copies[at].wait()
                copies[at + 1].wait()

        grad = vertex_pass(ub.at[top], cb, eb.at[top], wb[0:1, :], r_high, r_low, ready)
        copies[-2].wait()
        s1[0], s1[1] = adagrad(ub[top, :], gb[top, :], grad)
        copies[-1].wait()


def first_end(
    u, g, c, h, e, w, u_odd, g_odd, c_odd, e_odd, w_odd,
    s1, r_high, r_low, hb, ub, gb, cb, eb, wb, sems,
):
    odd = is_odd()

    @pl.when(odd)
    def _():
        rows = s1.shape[1]
        end = pl.ds(u_odd.shape[0] - rows, rows)
        (copy,) = load([(h, hb)], sems)
        grad = vertex_pass(u_odd.at[end], c_odd, e_odd.at[end], w_odd[0:1, :], r_high, r_low)
        s1[0], s1[1] = adagrad(u_odd[end, :], g_odd[end, :], grad)
        copy.wait()

    @pl.when(jnp.logical_not(odd))
    def _():
        for copy in load([(w, wb), (u, ub), (c, cb), (e.at[0], eb), (g, gb)], sems):
            copy.wait()


def first_even(
    u, g, c, e, w, u_odd, c_odd, h_odd, rh_top, rl_top, rh_end, rl_end,
    u1, g1, r_high, r_low, c_out, h_out,
):
    odd = is_odd()

    @pl.when(odd)
    def _():
        middle, rest = rh_top.shape[0], rh_end.shape[0]
        parts = [
            (u_odd.at[pl.ds(0, middle)], rh_top, rl_top),
            (u_odd.at[pl.ds(middle, rest)], rh_end, rl_end),
        ]
        context_pass(parts, c_odd, h_odd, c_out, h_out)

    @pl.when(jnp.logical_not(odd))
    def _():
        grad = vertex_pass(u, c, e, w[0:1, :], r_high, r_low)
        u1[...], g1[...] = adagrad(u[...], g[...], grad)


def first_context(h, u, c, r_high, r_low, after, c_out, h_out, hb, sems):
    @pl.when(jnp.logical_not(is_odd()))
    def _():
        for copy in load([(h, hb)], sems):
            copy.wait()
        context_pass([(u, r_high, r_low)], c, hb, c_out, h_out)


def gate(*refs):
    out = refs[-1]
    out[...] = jnp.zeros_like(out)


def second_odd(u1, g1, c, e, w, after, u2, g2, r_high, r_low):
    @pl.when(is_odd())
    def _():
        grad = vertex_pass(u1, c, e.at[1], w[1:2, :], r_high, r_low)
        u2[...], g2[...] = adagrad(u1[...], g1[...], grad)


def second_top(
    s1, c, e, w, u_odd, c_odd, h_odd, rh_odd, rl_odd, u2_odd, g2_odd,
    u2, grad_out, r_high, r_low, c_out, h_out,
):
    odd = is_odd()
    rows = grad_out.shape[0]

    @pl.when(odd)
    def _():
        u2[:rows, :] = u2_odd[:rows, :]
        u2[rows:, :] = g2_odd[g2_odd.shape[0] + rows - u2.shape[0] :, :]
        context_pass([(u_odd, rh_odd, rl_odd)], c_odd, h_odd, c_out, h_out)

    @pl.when(jnp.logical_not(odd))
    def _():
        grad = vertex_pass(s1.at[0], c, e.at[1, pl.ds(0, rows)], w[1:2, :], r_high, r_low)
        grad_out[...] = grad
        u2[:rows, :] = adagrad(s1[0], s1[1], grad)[0]


def second_end(s1, c, e, w, grad_top, u2_odd, g2_odd, u2, grad_a, grad_b, r_high, r_low, buf):
    odd = is_odd()
    middle, direct = grad_top.shape[0], grad_a.shape[0]

    @pl.when(odd)
    def _():
        u2[...] = u2_odd[middle:, :]
        grad_a[...] = g2_odd[:direct, :]

    @pl.when(jnp.logical_not(odd))
    def _():
        grad = vertex_pass(s1.at[0], c, e.at[1, pl.ds(middle, s1.shape[1])], w[1:2, :], r_high, r_low)
        buf[:middle, :] = grad_top[...]
        buf[middle:, :] = grad
        grad_a[...], grad_b[...] = buf[:direct, :], buf[direct:, :]
        u2[...] = adagrad(s1[0], s1[1], grad)[0]


def second_context(s1_top, s1_end, c, h, rh_top, rl_top, rh_end, rl_end, c_out, h_out):
    @pl.when(jnp.logical_not(is_odd()))
    def _():
        parts = [(s1_top.at[0], rh_top, rl_top), (s1_end.at[0], rh_end, rl_end)]
        context_pass(parts, c, h, c_out, h_out)


def third(odd, row, u, c, e, w, g2, r_high, r_low):
    rows = pl.ds(row, g2.shape[0])

    @pl.when(is_odd() == odd)
    def _():
        g2[...] = vertex_pass(u.at[rows], c, e.at[2, rows], w[2:3, :], r_high, r_low)


def third_odd_top(u_top, u_end, c, e, w, after, u, g2, r_high, r_low):
    middle = u.shape[0] - u_end.shape[0]
    u[:middle, :] = u_top[:middle, :]
    u[middle:, :] = u_end[...]
    third(True, 0, u, c, e, w, g2, r_high, r_low)


def third_odd_end(u, c, e, w, after, g2, r_high, r_low):
    third(True, u.shape[0] - g2.shape[0], u, c, e, w, g2, r_high, r_low)


def third_even(row, u, c, e, w, g2_odd, g2, r_high, r_low):
    @pl.when(is_odd())
    def _():
        g2[...] = g2_odd[...]

    third(False, row, u, c, e, w, g2, r_high, r_low)


def third_even_end(row, u, c, e, w, g2_odd, g1, g2, r_high, r_low, g1_out):
    g1_out[...] = g1[...]
    third_even(row, u, c, e, w, g2_odd, g2, r_high, r_low)


def third_context(
    u_odd, c_odd, h_odd, rh_odd, rl_odd, rh_odd_end, rl_odd_end,
    u_even, c_even, h_even, rh_even, rl_even, rh_even_end, rl_even_end, after, c_out, h_out,
):
    odd = is_odd()
    middle = rh_odd.shape[0]
    top, end = pl.ds(0, middle), pl.ds(middle, rh_odd_end.shape[0])

    @pl.when(odd)
    def _():
        parts = [(u_odd.at[top], rh_odd, rl_odd), (u_odd.at[end], rh_odd_end, rl_odd_end)]
        context_pass(parts, c_odd, h_odd, c_out, h_out)

    @pl.when(jnp.logical_not(odd))
    def _():
        parts = [(u_even.at[top], rh_even, rl_even), (u_even.at[end], rh_even_end, rl_even_end)]
        context_pass(parts, c_even, h_even, c_out, h_out)


def last(row, s1_top, s1_end, g1, u2, g2, u_out, g_out, ub, gb, sems):
    odd = is_odd()
    rows = g2.shape[0]
    at = pl.ds(row, rows)
    copies = [pltpu.make_async_copy(gb, g_out.at[at], sems.at[0]), pltpu.make_async_copy(ub, u_out.at[at], sems.at[1])]

    @pl.when(odd)
    def _():
        begin = 0
        for s1 in (s1_top, s1_end):
            low, high = max(row, begin), min(row + rows, begin + s1.shape[1])
            if low < high:
                there, here = pl.ds(low - begin, high - low), pl.ds(low - row, high - low)
                value, moment = adagrad(s1[0, there, :], s1[1, there, :], g1[here, :])
                gb[here, :] = moment + g2[here, :] * g2[here, :]
                ub[here, :] = value
            begin += s1.shape[1]

    @pl.when(jnp.logical_not(odd))
    def _():
        gb[...] = g1[:rows, :] + g2[...] * g2[...]
        ub[...] = u2[at, :]

    copies[0].start()
    ub[...] = ub[...] - RATE * g2[...] * lax.rsqrt(gb[...])
    copies[1].start()
    for copy in copies:
        copy.wait()


def last_top(s1_top, s1_end, g1, u2, g2, u_out, g_out, done, *scratch):
    last(0, s1_top, s1_end, g1, u2, g2, u_out, g_out, *scratch)


def last_end(row, s1_top, s1_end, g1_a, g1_b, g1_over, swapped, u2, g2, after, u_top, g_top, u_out, g_out, buf, *scratch):
    rows, detour = g2.shape[0], g1_b.shape[0]
    place = lax.axis_index("inner")
    odd = is_odd()

    @pl.when(jnp.logical_and(odd, place != 1))
    def _():
        buf[rows - detour :, :] = g1_b[...]

    @pl.when(place == 1)
    def _():
        buf[rows - detour :, :] = g1_over[...]

    @pl.when(jnp.logical_not(odd))
    def _():
        buf[rows - detour :, :] = swapped[swapped.shape[0] - detour :, :]

    if rows > detour:
        buf[: rows - detour, :] = g1_a[row:, :]
    last(row, s1_top, s1_end, buf, u2, g2, u_out, g_out, *scratch)


def per_device(vertices, vertex_moments, contexts, context_moments, edge_counts, negative_weights):
    nrows, width = vertices.shape
    ncols = contexts.shape[0]
    count = lax.axis_size("inner")
    assert count % 2 == 0 and count > 5 and edge_counts.shape[0] == 3

    ring = [(i, (i + 1) % count) for i in range(count)]
    unring = [(b, a) for a, b in ring]
    swap = [(i, i ^ 1) for i in range(count)]
    home = [(i, (i - 2) % count) for i in range(count)]

    def change(pairs, targets):
        return [(a, targets.get(a, b)) for a, b in pairs]

    def move(value, pairs):
        return lax.ppermute(value, "inner", pairs)

    def f32(*shape):
        return jax.ShapeDtypeStruct(shape, F32)

    block = f32(nrows, width)
    ctx = f32(ncols, width)
    half = jax.ShapeDtypeStruct((nrows, ncols), BF16)
    vert_buf = pltpu.VMEM((nrows, width), F32)
    ctx_buf = pltpu.VMEM((ncols, width), F32)
    sems = pltpu.SemaphoreType.DMA((4 + 2 * (ncols // block_of(ncols, 256)),))
    hbm = [
        pltpu.with_memory_space_constraint(x, pltpu.HBM)
        for x in (vertices, vertex_moments, contexts, context_moments, edge_counts, negative_weights)
    ]

    def stage(rows):
        return [f32(2, rows, width)] + [jax.ShapeDtypeStruct((rows, ncols), BF16)] * 2

    early = EARLY * nrows // 256 * 16
    edges = jax.ShapeDtypeStruct((nrows, ncols), jnp.int32)
    weights = jax.ShapeDtypeStruct(negative_weights.shape, jnp.int32)
    operands = [block, block, ctx, edges, weights]
    s1t, rht, rlt, *odds = call(
        first_top, [HBM] * 5, stage(early) + operands, [sems], (*hbm[:3], *hbm[4:]), "first_top",
    )
    s1tx = move(s1t, ring)
    rest = nrows - early
    s1d, rhd, rld, hb, *evens = call(
        first_end, [HBM] * 6 + [VMEM] * 5, stage(rest) + [ctx] + operands, [sems], (*hbm, *odds), "first_end",
    )
    s1dx = move(s1d, ring)
    *s1, rhe0, rle0, c1o, h1o = call(
        first_even, [VMEM] * 12, [block, block, half, half, ctx, ctx], [],
        (*evens, odds[0], odds[2], hb, rht, rlt, rhd, rld), "first_even",
    )
    s1i = [move(x, swap) for x in s1]
    (gated,) = call(gate, [ANY], [f32(8, 128)], [], (s1tx,), "gate", 6000000000)
    u2e, m2e, rho1, rlo1 = call(
        second_odd, [VMEM] * 5 + [ANY], [block, block, half, half], [],
        (*s1i, c1o, edge_counts, negative_weights, gated), "second_odd",
    )
    c1e, h1e = call(
        first_context, [HBM] + [VMEM] * 4 + [ANY], [ctx, ctx], [ctx_buf, sems],
        (hbm[3], evens[0], evens[2], rhe0, rle0, u2e), "first_context",
    )
    u2x = move(u2e, ring)
    detour = DETOUR * nrows // 512 * 16
    u2t, g1t, rht1, rlt1, c2o, h2o = call(
        second_top, [VMEM] * 11, [f32(early + detour, width), f32(early, width)] + stage(early)[1:] + [ctx, ctx], [],
        (s1tx, c1e, edge_counts, negative_weights, s1i[0], c1o, h1o, rho1, rlo1, u2e, m2e), "second_top",
    )
    u2ti = move(u2t, swap)
    u2d, g1a, g1b, rhd1, rld1 = call(
        second_end, [VMEM] * 7,
        [f32(rest, width), f32(nrows - detour, width), f32(detour, width)] + stage(rest)[1:], [vert_buf],
        (s1dx, c1e, edge_counts, negative_weights, g1t, u2e, m2e), "second_end", 10000000000,
    )
    u2di = move(u2d, swap)
    g1ax = move(g1a, unring)
    g1bx = move(g1b, change(unring, {2: 4, 5: 1}))
    c2e, h2e = call(
        second_context, [VMEM] * 8, [ctx, ctx], [],
        (s1tx, s1dx, c1e, h1e, rht1, rlt1, rhd1, rld1), "second_context",
    )
    half_rows = HALF * nrows // 256 * 16
    part = stage(half_rows)[1:]
    half_block = f32(half_rows, width)
    end_part = stage(nrows - half_rows)[1:]
    end_block = f32(nrows - half_rows, width)
    u2i, g2ot, rhot, rlot = call(
        third_odd_top, [VMEM] * 5 + [ANY], [block, half_block] + part, [],
        (u2ti, u2di, c2o, edge_counts, negative_weights, u2d), "third_odd_top",
    )
    g2t, rhet, rlet = call(
        functools.partial(third_even, 0), [VMEM] * 5, [half_block] + part, [],
        (u2x, c2e, edge_counts, negative_weights, g2ot), "third_even_top",
    )
    g2tx = move(g2t, home)
    g2od, rhod, rlod = call(
        third_odd_end, [VMEM] * 4 + [ANY], [end_block] + end_part, [],
        (u2i, c2o, edge_counts, negative_weights, g2t), "third_odd_end",
    )
    g2d, rhed, rled, g1r = call(
        functools.partial(third_even_end, half_rows), [VMEM] * 6, [end_block] + end_part + [f32(detour, width)], [],
        (u2x, c2e, edge_counts, negative_weights, g2od, g1bx), "third_even_end", 1024,
    )
    g2dx = move(g2d, home)
    g1rx = move(g1r, [(4, 1)])
    c3, h3 = call(
        third_context, [VMEM] * 14 + [ANY], [ctx, ctx], [],
        (u2i, c2o, h2o, rhot, rlot, rhod, rlod, u2x, c2e, h2e, rhet, rlet, rhed, rled, g1ax),
        "third_context", 10000000000,
    )

    def out_scratch(rows):
        return [pltpu.VMEM((rows, width), F32)] * 2 + [pltpu.SemaphoreType.DMA((2,))]

    u3, g3, done = call(
        last_top, [VMEM] * 5, [block, block, f32(8, 128)], out_scratch(half_rows), (s1t, s1d, g1ax, u2i, g2tx), "last_top",
        out_spec=HBM,
    )
    (arrived,) = call(gate, [ANY] * 2, [f32(8, 128)], [], (g1rx, done), "gate_last", 10000000000)
    u3, g3 = call(
        functools.partial(last_end, half_rows), [VMEM] * 8 + [ANY] + [HBM] * 2, [block, block],
        [pltpu.VMEM((nrows - half_rows, width), F32)] + out_scratch(nrows - half_rows),
        (s1t, s1d, g1ax, g1bx, g1rx, u2ti, u2i, g2dx, arrived, u3, g3), "last_end", out_spec=HBM, aliases={9: 0, 10: 1},
    )
    return u3, g3, c3, h3


def solution(mesh):
    split_rows = P(("snap", "inner"), None)
    return jax.shard_map(
        per_device,
        mesh=mesh,
        in_specs=(
            split_rows,
            split_rows,
            split_rows,
            split_rows,
            P(None, None, ("snap", "inner")),
            P(None, ("snap", "inner")),
        ),
        out_specs=(split_rows,) * 4,
        check_vma=False,
    )
```

```python
import functools

import jax
import jax.numpy as jnp
from jax import lax
from jax.experimental import pallas as pl
from jax.experimental.pallas import tpu as pltpu
from jax.sharding import PartitionSpec as P

F32 = jnp.float32
BF16 = jnp.bfloat16
RATE = 0.05
STACKED = 384
DETOUR = 8
HALF = 12
EARLY = 6
VMEM = pl.BlockSpec(memory_space=pltpu.VMEM)
HBM = pl.BlockSpec(memory_space=pltpu.HBM)
ANY = pl.BlockSpec(memory_space=pl.ANY)


def split(x):
    high = x.astype(BF16)
    return high, (x - high.astype(F32)).astype(BF16)


def product(a, b, dim_a, dim_b):
    def one(x, y):
        return lax.dot_general(
            x, y, (((dim_a,), (dim_b,)), ((), ())), preferred_element_type=F32
        )

    rows = a[0].shape[0]
    if dim_a == 1 and rows <= STACKED:
        both = one(jnp.concatenate(a, axis=0), b[0])
        return both[:rows] + (both[rows:] + one(a[0], b[1]))
    return one(a[0], b[0]) + (one(a[1], b[0]) + one(a[0], b[1]))


def block_of(size, most):
    return most if size % most == 0 else size


def is_odd():
    return lax.rem(lax.axis_index("inner"), 2) == 1


def adagrad(value, moment, grad):
    moment = moment + grad * grad
    return value - RATE * grad * lax.rsqrt(moment), moment


def vertex_pass(u, c, e, w, r_high, r_low, ready=None):
    us = split(0.5 * u[...])
    wf = w.astype(F32)
    cols = block_of(c.shape[0], 256)
    count = c.shape[0] // cols
    parts = []

    def scores(j):
        if ready is not None:
            ready(j)
        parts.append(split(c[pl.ds(j * cols, cols), :]))
        return product(us, parts[j], 1, 1)

    grad = None
    half_scores = scores(0)
    for j in range(count):
        at = pl.ds(j * cols, cols)
        later = scores(j + 1) if j + 1 < count else None
        ef = e[:, at].astype(F32)
        wj = wf[:, j * cols : (j + 1) * cols]
        resid = split((ef + wj) * jnp.tanh(half_scores) + (wj - ef))
        r_high[:, at] = resid[0]
        r_low[:, at] = resid[1]
        term = product(resid, parts[j], 1, 0)
        grad = term if grad is None else grad + term
        half_scores = later
    return 0.5 * grad


def context_pass(parts, c, h, c_out, h_out):
    us = [split(0.5 * u[...]) for u, _, _ in parts]
    rows = block_of(c.shape[0], 256)
    for j in range(c.shape[0] // rows):
        at = pl.ds(j * rows, rows)
        grad = sum(product((high[:, at], low[:, at]), u, 0, 0) for u, (_, high, low) in zip(us, parts))
        c_out[at, :], h_out[at, :] = adagrad(c[at, :], h[at, :], grad)


def call(body, in_specs, outs, scratch, args, name, flops=1024, out_spec=VMEM, aliases=None):
    return pl.pallas_call(
        body,
        out_shape=outs,
        in_specs=in_specs,
        out_specs=[out_spec] * len(outs),
        scratch_shapes=scratch,
        input_output_aliases=aliases or {},
        compiler_params=pltpu.CompilerParams(vmem_limit_bytes=24 << 20),
        cost_estimate=pl.CostEstimate(flops=flops, bytes_accessed=1024, transcendentals=0),
        name=name,
    )(*args)


def load(pairs, sems, first=0):
    copies = [pltpu.make_async_copy(a, b, sems.at[first + i]) for i, (a, b) in enumerate(pairs)]
    for copy in copies:
        copy.start()
    return copies


def first_top(u, g, c, e, w, s1, r_high, r_low, ub, gb, cb, eb, wb, sems):
    @pl.when(is_odd())
    def _():
        rows = s1.shape[1]
        top, end = pl.ds(0, rows), pl.ds(rows, ub.shape[0] - rows)
        cols = block_of(cb.shape[0], 512)
        count = cb.shape[0] // cols
        chunks = []
        for j in range(count):
            at = pl.ds(j * cols, cols)
            chunks += [(c.at[at], cb.at[at]), (e.at[0, top, at], eb.at[top, at])]
        copies = load([(w, wb), (u, ub)] + chunks + [(g, gb), (e.at[0, end], eb.at[end])], sems)
        copies[0].wait()
        copies[1].wait()
        small = block_of(cb.shape[0], 256)

        def ready(j):
            if j * small % cols == 0:
                at = 2 + 2 * (j * small // cols)
                copies[at].wait()
                copies[at + 1].wait()

        grad = vertex_pass(ub.at[top], cb, eb.at[top], wb[0:1, :], r_high, r_low, ready)
        copies[-2].wait()
        s1[0], s1[1] = adagrad(ub[top, :], gb[top, :], grad)
        copies[-1].wait()


def first_end(
    u, g, c, h, e, w, u_odd, g_odd, c_odd, e_odd, w_odd,
    s1, r_high, r_low, hb, ub, gb, cb, eb, wb, sems,
):
    odd = is_odd()

    @pl.when(odd)
    def _():
        rows = s1.shape[1]
        end = pl.ds(u_odd.shape[0] - rows, rows)
        (copy,) = load([(h, hb)], sems)
        grad = vertex_pass(u_odd.at[end], c_odd, e_odd.at[end], w_odd[0:1, :], r_high, r_low)
        s1[0], s1[1] = adagrad(u_odd[end, :], g_odd[end, :], grad)
        copy.wait()

    @pl.when(jnp.logical_not(odd))
    def _():
        for copy in load([(w, wb), (u, ub), (c, cb), (e.at[0], eb), (g, gb)], sems):
            copy.wait()


def first_even(
    u, g, c, e, w, u_odd, c_odd, h_odd, rh_top, rl_top, rh_end, rl_end,
    u1, g1, r_high, r_low, c_out, h_out,
):
    odd = is_odd()

    @pl.when(odd)
    def _():
        middle, rest = rh_top.shape[0], rh_end.shape[0]
        parts = [
            (u_odd.at[pl.ds(0, middle)], rh_top, rl_top),
            (u_odd.at[pl.ds(middle, rest)], rh_end, rl_end),
        ]
        context_pass(parts, c_odd, h_odd, c_out, h_out)

    @pl.when(jnp.logical_not(odd))
    def _():
        grad = vertex_pass(u, c, e, w[0:1, :], r_high, r_low)
        u1[...], g1[...] = adagrad(u[...], g[...], grad)


def first_context(h, u, c, r_high, r_low, after, c_out, h_out, hb, sems):
    @pl.when(jnp.logical_not(is_odd()))
    def _():
        for copy in load([(h, hb)], sems):
            copy.wait()
        context_pass([(u, r_high, r_low)], c, hb, c_out, h_out)


def gate(*refs):
    out = refs[-1]
    out[...] = jnp.zeros_like(out)


def second_odd(u1, g1, c, e, w, after, u2, g2, r_high, r_low):
    @pl.when(is_odd())
    def _():
        grad = vertex_pass(u1, c, e.at[1], w[1:2, :], r_high, r_low)
        u2[...], g2[...] = adagrad(u1[...], g1[...], grad)


def second_top(
    s1, c, e, w, u_odd, c_odd, h_odd, rh_odd, rl_odd, u2_odd, g2_odd,
    u2, grad_out, r_high, r_low, c_out, h_out,
):
    odd = is_odd()
    rows = grad_out.shape[0]

    @pl.when(odd)
    def _():
        u2[:rows, :] = u2_odd[:rows, :]
        u2[rows:, :] = g2_odd[g2_odd.shape[0] + rows - u2.shape[0] :, :]
        context_pass([(u_odd, rh_odd, rl_odd)], c_odd, h_odd, c_out, h_out)

    @pl.when(jnp.logical_not(odd))
    def _():
        grad = vertex_pass(s1.at[0], c, e.at[1, pl.ds(0, rows)], w[1:2, :], r_high, r_low)
        grad_out[...] = grad
        u2[:rows, :] = adagrad(s1[0], s1[1], grad)[0]


def second_end(s1, c, e, w, grad_top, u2_odd, g2_odd, u2, grad_a, grad_b, r_high, r_low, buf):
    odd = is_odd()
    middle, direct = grad_top.shape[0], grad_a.shape[0]

    @pl.when(odd)
    def _():
        u2[...] = u2_odd[middle:, :]
        grad_a[...] = g2_odd[:direct, :]

    @pl.when(jnp.logical_not(odd))
    def _():
        grad = vertex_pass(s1.at[0], c, e.at[1, pl.ds(middle, s1.shape[1])], w[1:2, :], r_high, r_low)
        buf[:middle, :] = grad_top[...]
        buf[middle:, :] = grad
        grad_a[...], grad_b[...] = buf[:direct, :], buf[direct:, :]
        u2[...] = adagrad(s1[0], s1[1], grad)[0]


def second_context(s1_top, s1_end, c, h, rh_top, rl_top, rh_end, rl_end, c_out, h_out):
    @pl.when(jnp.logical_not(is_odd()))
    def _():
        parts = [(s1_top.at[0], rh_top, rl_top), (s1_end.at[0], rh_end, rl_end)]
        context_pass(parts, c, h, c_out, h_out)


def third(odd, row, u, c, e, w, g2, r_high, r_low):
    rows = pl.ds(row, g2.shape[0])

    @pl.when(is_odd() == odd)
    def _():
        g2[...] = vertex_pass(u.at[rows], c, e.at[2, rows], w[2:3, :], r_high, r_low)


def third_odd_top(u_top, u_end, c, e, w, after, u, g2, r_high, r_low):
    middle = u.shape[0] - u_end.shape[0]
    u[:middle, :] = u_top[:middle, :]
    u[middle:, :] = u_end[...]
    third(True, 0, u, c, e, w, g2, r_high, r_low)


def third_odd_end(u, c, e, w, after, g2, r_high, r_low):
    third(True, u.shape[0] - g2.shape[0], u, c, e, w, g2, r_high, r_low)


def third_even(row, u, c, e, w, g2_odd, g2, r_high, r_low):
    @pl.when(is_odd())
    def _():
        g2[...] = g2_odd[...]

    third(False, row, u, c, e, w, g2, r_high, r_low)


def third_even_end(row, u, c, e, w, g2_odd, g1, g2, r_high, r_low, g1_out):
    g1_out[...] = g1[...]
    third_even(row, u, c, e, w, g2_odd, g2, r_high, r_low)


def third_context(
    u_odd, c_odd, h_odd, rh_odd, rl_odd, rh_odd_end, rl_odd_end,
    u_even, c_even, h_even, rh_even, rl_even, rh_even_end, rl_even_end, after, c_out, h_out,
):
    odd = is_odd()
    middle = rh_odd.shape[0]
    top, end = pl.ds(0, middle), pl.ds(middle, rh_odd_end.shape[0])

    @pl.when(odd)
    def _():
        parts = [(u_odd.at[top], rh_odd, rl_odd), (u_odd.at[end], rh_odd_end, rl_odd_end)]
        context_pass(parts, c_odd, h_odd, c_out, h_out)

    @pl.when(jnp.logical_not(odd))
    def _():
        parts = [(u_even.at[top], rh_even, rl_even), (u_even.at[end], rh_even_end, rl_even_end)]
        context_pass(parts, c_even, h_even, c_out, h_out)


def last(row, s1_top, s1_end, g1, u2, g2, u_out, g_out, ub, gb, sems):
    odd = is_odd()
    rows = g2.shape[0]
    at = pl.ds(row, rows)
    copies = [pltpu.make_async_copy(gb, g_out.at[at], sems.at[0]), pltpu.make_async_copy(ub, u_out.at[at], sems.at[1])]

    @pl.when(odd)
    def _():
        begin = 0
        for s1 in (s1_top, s1_end):
            low, high = max(row, begin), min(row + rows, begin + s1.shape[1])
            if low < high:
                there, here = pl.ds(low - begin, high - low), pl.ds(low - row, high - low)
                value, moment = adagrad(s1[0, there, :], s1[1, there, :], g1[here, :])
                gb[here, :] = moment + g2[here, :] * g2[here, :]
                ub[here, :] = value
            begin += s1.shape[1]

    @pl.when(jnp.logical_not(odd))
    def _():
        gb[...] = g1[:rows, :] + g2[...] * g2[...]
        ub[...] = u2[at, :]

    copies[0].start()
    ub[...] = ub[...] - RATE * g2[...] * lax.rsqrt(gb[...])
    copies[1].start()
    for copy in copies:
        copy.wait()


def last_top(s1_top, s1_end, g1, u2, g2, u_out, g_out, done, *scratch):
    last(0, s1_top, s1_end, g1, u2, g2, u_out, g_out, *scratch)


def last_end(row, s1_top, s1_end, g1_a, g1_b, g1_over, swapped, u2, g2, after, u_top, g_top, u_out, g_out, buf, *scratch):
    rows, detour = g2.shape[0], g1_b.shape[0]
    place = lax.axis_index("inner")
    odd = is_odd()

    @pl.when(jnp.logical_and(odd, place != 1))
    def _():
        buf[rows - detour :, :] = g1_b[...]

    @pl.when(place == 1)
    def _():
        buf[rows - detour :, :] = g1_over[...]

    @pl.when(jnp.logical_not(odd))
    def _():
        buf[rows - detour :, :] = swapped[swapped.shape[0] - detour :, :]

    if rows > detour:
        buf[: rows - detour, :] = g1_a[row:, :]
    last(row, s1_top, s1_end, buf, u2, g2, u_out, g_out, *scratch)


def per_device(vertices, vertex_moments, contexts, context_moments, edge_counts, negative_weights):
    nrows, width = vertices.shape
    ncols = contexts.shape[0]
    count = lax.axis_size("inner")
    assert count % 2 == 0 and count > 5 and edge_counts.shape[0] == 3

    ring = [(i, (i + 1) % count) for i in range(count)]
    unring = [(b, a) for a, b in ring]
    swap = [(i, i ^ 1) for i in range(count)]
    home = [(i, (i - 2) % count) for i in range(count)]

    def change(pairs, targets):
        return [(a, targets.get(a, b)) for a, b in pairs]

    def move(value, pairs):
        return lax.ppermute(value, "inner", pairs)

    def f32(*shape):
        return jax.ShapeDtypeStruct(shape, F32)

    block = f32(nrows, width)
    ctx = f32(ncols, width)
    half = jax.ShapeDtypeStruct((nrows, ncols), BF16)
    vert_buf = pltpu.VMEM((nrows, width), F32)
    ctx_buf = pltpu.VMEM((ncols, width), F32)
    sems = pltpu.SemaphoreType.DMA((4 + 2 * (ncols // block_of(ncols, 256)),))
    hbm = [
        pltpu.with_memory_space_constraint(x, pltpu.HBM)
        for x in (vertices, vertex_moments, contexts, context_moments, edge_counts, negative_weights)
    ]

    def stage(rows):
        return [f32(2, rows, width)] + [jax.ShapeDtypeStruct((rows, ncols), BF16)] * 2

    early = EARLY * nrows // 256 * 16
    edges = jax.ShapeDtypeStruct((nrows, ncols), jnp.int32)
    weights = jax.ShapeDtypeStruct(negative_weights.shape, jnp.int32)
    operands = [block, block, ctx, edges, weights]
    s1t, rht, rlt, *odds = call(
        first_top, [HBM] * 5, stage(early) + operands, [sems], (*hbm[:3], *hbm[4:]), "first_top",
    )
    s1tx = move(s1t, ring)
    rest = nrows - early
    s1d, rhd, rld, hb, *evens = call(
        first_end, [HBM] * 6 + [VMEM] * 5, stage(rest) + [ctx] + operands, [sems], (*hbm, *odds), "first_end",
    )
    s1dx = move(s1d, ring)
    *s1, rhe0, rle0, c1o, h1o = call(
        first_even, [VMEM] * 12, [block, block, half, half, ctx, ctx], [],
        (*evens, odds[0], odds[2], hb, rht, rlt, rhd, rld), "first_even",
    )
    s1i = [move(x, swap) for x in s1]
    (gated,) = call(gate, [ANY], [f32(8, 128)], [], (s1tx,), "gate", 6000000000)
    u2e, m2e, rho1, rlo1 = call(
        second_odd, [VMEM] * 5 + [ANY], [block, block, half, half], [],
        (*s1i, c1o, edge_counts, negative_weights, gated), "second_odd",
    )
    c1e, h1e = call(
        first_context, [HBM] + [VMEM] * 4 + [ANY], [ctx, ctx], [ctx_buf, sems],
        (hbm[3], evens[0], evens[2], rhe0, rle0, u2e), "first_context",
    )
    u2x = move(u2e, ring)
    detour = DETOUR * nrows // 512 * 16
    u2t, g1t, rht1, rlt1, c2o, h2o = call(
        second_top, [VMEM] * 11, [f32(early + detour, width), f32(early, width)] + stage(early)[1:] + [ctx, ctx], [],
        (s1tx, c1e, edge_counts, negative_weights, s1i[0], c1o, h1o, rho1, rlo1, u2e, m2e), "second_top",
    )
    u2ti = move(u2t, swap)
    u2d, g1a, g1b, rhd1, rld1 = call(
        second_end, [VMEM] * 7,
        [f32(rest, width), f32(nrows - detour, width), f32(detour, width)] + stage(rest)[1:], [vert_buf],
        (s1dx, c1e, edge_counts, negative_weights, g1t, u2e, m2e), "second_end", 10000000000,
    )
    u2di = move(u2d, swap)
    g1ax = move(g1a, unring)
    g1bx = move(g1b, change(unring, {2: 4, 5: 1}))
    c2e, h2e = call(
        second_context, [VMEM] * 8, [ctx, ctx], [],
        (s1tx, s1dx, c1e, h1e, rht1, rlt1, rhd1, rld1), "second_context",
    )
    half_rows = HALF * nrows // 256 * 16
    part = stage(half_rows)[1:]
    half_block = f32(half_rows, width)
    end_part = stage(nrows - half_rows)[1:]
    end_block = f32(nrows - half_rows, width)
    u2i, g2ot, rhot, rlot = call(
        third_odd_top, [VMEM] * 5 + [ANY], [block, half_block] + part, [],
        (u2ti, u2di, c2o, edge_counts, negative_weights, u2d), "third_odd_top",
    )
    g2t, rhet, rlet = call(
        functools.partial(third_even, 0), [VMEM] * 5, [half_block] + part, [],
        (u2x, c2e, edge_counts, negative_weights, g2ot), "third_even_top",
    )
    g2tx = move(g2t, home)
    g2od, rhod, rlod = call(
        third_odd_end, [VMEM] * 4 + [ANY], [end_block] + end_part, [],
        (u2i, c2o, edge_counts, negative_weights, g2t), "third_odd_end",
    )
    g2d, rhed, rled, g1r = call(
        functools.partial(third_even_end, half_rows), [VMEM] * 6, [end_block] + end_part + [f32(detour, width)], [],
        (u2x, c2e, edge_counts, negative_weights, g2od, g1bx), "third_even_end", 1024,
    )
    g2dx = move(g2d, home)
    g1rx = move(g1r, [(4, 1)])
    c3, h3 = call(
        third_context, [VMEM] * 14 + [ANY], [ctx, ctx], [],
        (u2i, c2o, h2o, rhot, rlot, rhod, rlod, u2x, c2e, h2e, rhet, rlet, rhed, rled, g1ax),
        "third_context", 10000000000,
    )

    def out_scratch(rows):
        return [pltpu.VMEM((rows, width), F32)] * 2 + [pltpu.SemaphoreType.DMA((2,))]

    u3, g3, done = call(
        last_top, [VMEM] * 5, [block, block, f32(8, 128)], out_scratch(half_rows), (s1t, s1d, g1ax, u2i, g2tx), "last_top",
        out_spec=HBM,
    )
    (arrived,) = call(gate, [ANY] * 2, [f32(8, 128)], [], (g1rx, done), "gate_last", 10000000000)
    u3, g3 = call(
        functools.partial(last_end, half_rows), [VMEM] * 8 + [ANY] + [HBM] * 2, [block, block],
        [pltpu.VMEM((nrows - half_rows, width), F32)] + out_scratch(nrows - half_rows),
        (s1t, s1d, g1ax, g1bx, g1rx, u2ti, u2i, g2dx, arrived, u3, g3), "last_end", out_spec=HBM, aliases={9: 0, 10: 1},
    )
    return u3, g3, c3, h3


def solution(mesh):
    split_rows = P(("snap", "inner"), None)
    return jax.shard_map(
        per_device,
        mesh=mesh,
        in_specs=(
            split_rows,
            split_rows,
            split_rows,
            split_rows,
            P(None, None, ("snap", "inner")),
            P(None, ("snap", "inner")),
        ),
        out_specs=(split_rows,) * 4,
        check_vma=False,
    )
```
